32 devices in a mesh: dp: 8 (over y, x, core), group: 4 (over z).
Axes of the slice: x: 2, y: 2, z: 4, core: 2. Of those that a mesh axis runs over, the one named last changes fastest.
Arguments:
- tokens: bfloat16 [16384, 896], P(('dp', 'group')), may hold values from -6 to 6
- positions: int32 [8, 2048], P('dp'), may hold values from 0 to 2047, as said below
- cotangent: bfloat16 [16384, 896], P(('dp', 'group')), may hold values from -6 to 6
- query_weight: float32 [896, 896], P(('dp', 'group')), may hold values from -0.1875 to 0.1875
- query_first: float32 [896, 896], P(('dp', 'group')), may hold values from -16384 to 16384
- query_second: float32 [896, 896], P(('dp', 'group')), may hold values from 0 to 14680064, as said below
- keyval_weight: float32 [896, 256], P(('dp', 'group')), may hold values from -0.1875 to 0.1875
- keyval_first: float32 [896, 256], P(('dp', 'group')), may hold values from -16384 to 16384
- keyval_second: float32 [896, 256], P(('dp', 'group')), may hold values from 0 to 16384, as said below
- output_weight: float32 [896, 896], P(('dp', 'group')), may hold values from -6 to 6
- output_first: float32 [896, 896], P(('dp', 'group')), may hold values from -16384 to 16384
- output_second: float32 [896, 896], P(('dp', 'group')), may hold values from 0 to 16384, as said below
- gateup_weight: float32 [896, 9728], P(('dp', 'group')), may hold values from -0.1875 to 0.1875
- gateup_first: float32 [896, 9728], P(('dp', 'group')), may hold values from -16384 to 16384
- gateup_second: float32 [896, 9728], P(('dp', 'group')), may hold values from 0 to 16384, as said below
- down_weight: float32 [4864, 896], P(('dp', 'group')), may hold values from -0.078125 to 0.078125
- down_first: float32 [4864, 896], P(('dp', 'group')), may hold values from -16384 to 16384
- down_second: float32 [4864, 896], P(('dp', 'group')), may hold values from 0 to 16384, as said below
- small_weight: float32 [2944], P(('dp', 'group')), may hold values from -2 to 2, as said below
- small_first: float32 [2944], P(('dp', 'group')), may hold values from -16384 to 16384
- small_second: float32 [2944], P(('dp', 'group')), may hold values from 0 to 205520896, as said below
Outputs:
- layer_out: bfloat16 [16384, 896], P(('dp', 'group'))
- tokens_grad: bfloat16 [16384, 896], P(('dp', 'group'))
- query_grad: float32 [896, 896], P(('dp', 'group'))
- query_second_out: float32 [896, 896], P(('dp', 'group'))
- query_weight_out: float32 [896, 896], P(('dp', 'group'))
- keyval_grad: float32 [896, 256], P(('dp', 'group'))
- keyval_second_out: float32 [896, 256], P(('dp', 'group'))
- keyval_weight_out: float32 [896, 256], P(('dp', 'group'))
- output_grad: float32 [896, 896], P(('dp', 'group'))
- output_second_out: float32 [896, 896], P(('dp', 'group'))
- output_weight_out: float32 [896, 896], P(('dp', 'group'))
- gateup_grad: float32 [896, 9728], P(('dp', 'group'))
- gateup_second_out: float32 [896, 9728], P(('dp', 'group'))
- gateup_weight_out: float32 [896, 9728], P(('dp', 'group'))
- down_grad: float32 [4864, 896], P(('dp', 'group'))
- down_second_out: float32 [4864, 896], P(('dp', 'group'))
- down_weight_out: float32 [4864, 896], P(('dp', 'group'))
- small_grad: float32 [2944], P(('dp', 'group'))
- small_second_out: float32 [2816], P(('dp', 'group'))
- value_bias_second_out: float32 [128], P(('dp', 'group'))
- small_weight_out: float32 [2944], P(('dp', 'group'))
The draws below stay inside these ranges and needn't reach their ends.
Inputs may be any that keep to these rules, and one draw needn't show every extreme that they name: `positions`: each row counts the place of a token within its packed document: 0 at the row's first token and at every document start, otherwise one more than the token before. Documents start only at the first token of a row, within its first 256 tokens, or within its last 256 tokens. At least one row is a single document. `query_second`: Positive. `keyval_second`: Positive. `output_second`: Positive. `gateup_second`: Positive. `down_second`: Positive. `small_second`: Positive. `small_weight`: gains lie in 0.6 to 1.4.
All inputs are finite; a program needn't handle non-finite values.
Results may differ from the reference program's by a relative error of at most 0.015.
The reference program's roundings to bfloat16 on the way count: a program that leaves them out, or rounds other values in their place, can miss the bound.
Values may be sent and summed in bfloat16 or wider, within the bound.
No kernel may reach another device: no remote copies, remote signals or barrier semaphores. Data moves between devices by JAX's collectives and lax.ppermute only.
A program may use at most 320 MiB of HBM per device.

```python
import math
import jax
import jax.numpy as jnp
from jax import lax

D = 896
HQ = 14
HK = 2
HD = 64
FF = 4864
SPAN = 512
STEP = 10
QW = 896
KVW = 128
SMALL = 2944
SEQ_LEN = 2048
SEQS = 8
TOKENS = 16384


def first_moment(key, shape_now, grad_scale):
    return 0.1 / 0.9 * grad_scale * jax.random.truncated_normal(key, -3.0, 3.0, shape_now, jnp.float32)


def second_moment(key, shape_now, grad_scale, power):
    spread = jax.random.uniform(key, shape_now, jnp.float32, 0.0, 1.0)
    factor = 0.5 * jnp.exp(math.log(4.0) * spread ** power)
    return 0.05 / 0.95 * 2.0 * grad_scale * grad_scale * factor


def query_scale():
    return 0.2 * math.sqrt(D / max(1, QW * 4 // SEQ_LEN)) * math.sqrt(TOKENS)


def small_scale():
    value_scale = math.sqrt(TOKENS * (HQ // HK) * D / max(1, QW * 4 // SEQ_LEN))
    rest_part = jnp.full((2 * D + QW + KVW,), math.sqrt(TOKENS), jnp.float32)
    value_part = jnp.full((KVW,), value_scale, jnp.float32)
    return jnp.concatenate([rest_part, value_part])


def draw_positions(key, part):
    key = jax.random.fold_in(key, 7)
    row_key = jax.random.fold_in(key, 1)
    token_index = jnp.arange(SEQ_LEN, dtype=jnp.int32)
    edge_width = SPAN // 2
    region = (token_index >= 1) & (token_index < edge_width) | (token_index >= SEQ_LEN - edge_width)
    whole_row = jax.random.randint(row_key, (), 0, SEQS).astype(jnp.int32)
    row_ids = jnp.arange(SEQS, dtype=jnp.int32)
    cut_marks = jax.random.randint(key, (SEQS, SEQ_LEN), 0, 16) == 0
    cut_marks = cut_marks & region[None, :] & (row_ids[:, None] != whole_row)
    starts = jnp.where(cut_marks, token_index[None, :], 0).astype(jnp.int32)
    return (token_index[None, :] - lax.cummax(starts, axis=1)).astype(jnp.int32)


def draw_small_weight(key, part):
    key = jax.random.fold_in(key, 11)
    gain_key, bias_key = jax.random.split(key)
    gains = jax.random.uniform(gain_key, (2 * D,), jnp.float32, 0.6, 1.4)
    biases = 0.5 * jax.random.truncated_normal(bias_key, -4.0, 4.0, (QW + 2 * KVW,), jnp.float32)
    return jnp.concatenate([gains, biases])


def draw_query_first(key, part):
    key = jax.random.fold_in(key, 21)
    return first_moment(key, (D, QW), query_scale())


def draw_query_second(key, part):
    key = jax.random.fold_in(key, 22)
    return second_moment(key, (D, QW), query_scale(), 1.0)


def draw_keyval_first(key, part):
    key = jax.random.fold_in(key, 23)
    return first_moment(key, (D, 2 * KVW), 1.9 * math.sqrt(TOKENS))


def draw_keyval_second(key, part):
    key = jax.random.fold_in(key, 24)
    return second_moment(key, (D, 2 * KVW), 1.9 * math.sqrt(TOKENS), 1.0)


def draw_output_first(key, part):
    key = jax.random.fold_in(key, 25)
    return first_moment(key, (QW, D), 2.6 * math.sqrt(TOKENS / SEQ_LEN))


def draw_output_second(key, part):
    key = jax.random.fold_in(key, 26)
    return second_moment(key, (QW, D), 2.6 * math.sqrt(TOKENS / SEQ_LEN), 1.0)


def draw_gateup_first(key, part):
    key = jax.random.fold_in(key, 27)
    return first_moment(key, (D, 2 * FF), 0.25 * math.sqrt(TOKENS))


def draw_gateup_second(key, part):
    key = jax.random.fold_in(key, 28)
    return second_moment(key, (D, 2 * FF), 0.25 * math.sqrt(TOKENS), 1.0)


def draw_down_first(key, part):
    key = jax.random.fold_in(key, 29)
    return first_moment(key, (FF, D), 0.6 * math.sqrt(TOKENS))


def draw_down_second(key, part):
    key = jax.random.fold_in(key, 30)
    return second_moment(key, (FF, D), 0.6 * math.sqrt(TOKENS), 1.0)


def draw_small_first(key, part):
    key = jax.random.fold_in(key, 31)
    return first_moment(key, (SMALL,), small_scale())


def draw_small_second(key, part):
    key = jax.random.fold_in(key, 32)
    return second_moment(key, (SMALL,), small_scale(), 1.0)


def with_spikes(entries, stream_key, source, target, shards_of, factor):
    def block_of(axis_at):
        return (jnp.arange(entries.shape[axis_at]) // (entries.shape[axis_at] // shards_of)).reshape((-1,) + (1,) * (entries.ndim - 1 - axis_at))

    one_side = jax.random.permutation(stream_key, shards_of)[block_of(target)]
    other_side = (block_of(target) + shards_of // 2) % shards_of
    return jnp.where((block_of(source) == one_side) | (block_of(source) == other_side), factor * entries, entries)


def steps_of(own_key, shape, cuts, smallest, top_value):
    loudness, own = 1.0, jax.random.fold_in(own_key, 6)
    for position, shards_of in cuts:
        steps = jnp.exp(jax.random.uniform(jax.random.fold_in(own, position), (shards_of,), jnp.float32, smallest / len(cuts), top_value / len(cuts)))
        loudness = loudness * jnp.repeat(steps, shape[position] // shards_of).reshape([-1 if axis == position else 1 for axis in range(len(shape))])
    return loudness


def bell_draw(rng, dims, width, limit, pieces=(), kind=jnp.bfloat16):
    array = jax.random.normal(rng, dims, jnp.float32) * width
    if len(pieces) > 0:
        array = steps_of(rng, dims, pieces, -0.22, 0.18) * array
    return jnp.clip(array, min=-limit, max=limit).astype(kind)


def bell_draw_with(key, dims, width, limit, cuts, heavy, held_as=jnp.bfloat16):
    values = width * jax.random.normal(key, dims, jnp.float32)
    if cuts:
        values = values * steps_of(key, dims, cuts, -0.22, 0.18)
    return jnp.clip(with_spikes(values, jax.random.fold_in(key, 3), *heavy), -limit, limit).astype(held_as)


def setup_inputs(seed: int = 0) -> dict:
    arg_keys = jax.random.split(jax.random.key(seed), 22)
    tokens = bell_draw_with(arg_keys[0], (TOKENS, D), 1.0, 6.0, ((0, 32),), (0, 1, 32, 2.75))
    positions = draw_positions(jax.random.fold_in(arg_keys[21], 71), 0)
    cotangent = bell_draw(arg_keys[2], (TOKENS, D), 1.0, 6.0, ((0, 32),))
    query_weight = bell_draw(arg_keys[3], (D, QW), D ** -0.5, 0.1875, ((0, 32),), jnp.float32)
    query_first = draw_query_first(jax.random.fold_in(arg_keys[21], 71), 0)
    query_second = draw_query_second(jax.random.fold_in(arg_keys[21], 71), 0)
    keyval_weight = bell_draw(arg_keys[6], (D, 2 * KVW), D ** -0.5, 0.1875, ((0, 32),), jnp.float32)
    keyval_first = draw_keyval_first(jax.random.fold_in(arg_keys[21], 71), 0)
    keyval_second = draw_keyval_second(jax.random.fold_in(arg_keys[21], 71), 0)
    output_weight = bell_draw(arg_keys[9], (QW, D), (max(1, QW * 4 // SEQ_LEN)) ** -0.5, 6.0, ((0, 32),), jnp.float32)
    output_first = draw_output_first(jax.random.fold_in(arg_keys[21], 71), 0)
    output_second = draw_output_second(jax.random.fold_in(arg_keys[21], 71), 0)
    gateup_weight = bell_draw(arg_keys[12], (D, 2 * FF), D ** -0.5, 0.1875, ((0, 32),), jnp.float32)
    gateup_first = draw_gateup_first(jax.random.fold_in(arg_keys[21], 71), 0)
    gateup_second = draw_gateup_second(jax.random.fold_in(arg_keys[21], 71), 0)
    down_weight = bell_draw(arg_keys[15], (FF, D), FF ** -0.5, 0.078125, ((0, 32),), jnp.float32)
    down_first = draw_down_first(jax.random.fold_in(arg_keys[21], 71), 0)
    down_second = draw_down_second(jax.random.fold_in(arg_keys[21], 71), 0)
    small_weight = draw_small_weight(jax.random.fold_in(arg_keys[21], 71), 0)
    small_first = draw_small_first(jax.random.fold_in(arg_keys[21], 71), 0)
    small_second = draw_small_second(jax.random.fold_in(arg_keys[21], 71), 0)
    return dict(tokens=tokens, positions=positions, cotangent=cotangent, query_weight=query_weight, query_first=query_first, query_second=query_second, keyval_weight=keyval_weight, keyval_first=keyval_first, keyval_second=keyval_second, output_weight=output_weight, output_first=output_first, output_second=output_second, gateup_weight=gateup_weight, gateup_first=gateup_first, gateup_second=gateup_second, down_weight=down_weight, down_first=down_first, down_second=down_second, small_weight=small_weight, small_first=small_first, small_second=small_second)


theta_base = 1000000.0
norm_eps = 1e-06
beta_one = 0.9
beta_two = 0.95
adam_eps = 1e-08
decay_rate = 0.1
rate_proj = 0.02
rate_out = 0.5
rate_small = 0.2
masked_score = -1e+30

@jax.custom_vjp
def low(v):
    return lax.optimization_barrier(v.astype(jnp.bfloat16)).astype(jnp.float32)

@jax.custom_vjp
def low_back(v):
    return v

def low_keep(v):
    return (low(v), None)

def low_pass(kept, grad):
    return (grad,)

def back_keep(v):
    return (v, None)

def back_low(kept, grad):
    return (low(grad),)
low.defvjp(low_keep, low_pass)
low_back.defvjp(back_keep, back_low)

def rotary_tables(places):
    half_size = HD // 2
    inv_freq = theta_base ** (-(jnp.arange(half_size, dtype=jnp.float32) * 2.0) / HD)
    angles = places.astype(jnp.float32)[:, None] * inv_freq[None, :]
    return (jnp.cos(angles), jnp.sin(angles))

def rotate(values, cosine, sine_table, head_count, direction):
    row_count = values.shape[0]
    halves = values.reshape(row_count, head_count, 2, HD // 2)
    lower_half = halves[:, :, 0]
    upper_half = halves[:, :, 1]
    cos_b = cosine[:, None, :]
    sin_b = direction * sine_table[:, None, :]
    joined = jnp.stack([lower_half * cos_b - upper_half * sin_b, upper_half * cos_b + lower_half * sin_b], axis=2)
    return joined.reshape(row_count, head_count * HD)

def attend(query_rot, key_rot, value_all, places):
    seq_len = query_rot.shape[0]
    block_size = min(512, seq_len)
    head_ratio = HQ // HK
    query_heads = query_rot.reshape(seq_len, HK, head_ratio, HD)
    key_heads = key_rot.reshape(seq_len, HK, HD)
    value_heads = value_all.reshape(seq_len, HK, HD)
    token_index = jnp.arange(seq_len, dtype=jnp.int32)
    doc_start = (token_index - places).astype(jnp.int32)
    scale_factor = 1.0 / math.sqrt(HD)

    def one_block(number):
        low_edge = (number * block_size).astype(jnp.int32)
        query_part = lax.dynamic_slice_in_dim(query_heads, low_edge, block_size, 0)
        query_index = lax.dynamic_slice_in_dim(token_index, low_edge, block_size, 0)
        query_start = lax.dynamic_slice_in_dim(doc_start, low_edge, block_size, 0)
        scores = jnp.einsum('qhgd,khd->hgqk', query_part, key_heads, precision=lax.Precision.HIGHEST) * scale_factor
        allowed = (token_index[None, :] <= query_index[:, None]) & (doc_start[None, :] == query_start[:, None])
        scores = low_back(jnp.where(allowed[None, None], scores, masked_score))
        top_score = lax.optimization_barrier(jnp.max(scores, axis=3, keepdims=True))
        log_total = top_score + jnp.log(lax.optimization_barrier(jnp.sum(jnp.exp(scores - top_score), axis=3, keepdims=True)))
        weights_low = low(jnp.exp(scores - log_total))
        return jnp.einsum('hgqk,khd->qhgd', weights_low, value_heads, precision=lax.Precision.HIGHEST)
    outcome = lax.map(jax.checkpoint(one_block), jnp.arange(seq_len // block_size, dtype=jnp.int32))
    return outcome.reshape(seq_len, HQ * HD)

def layer_forward(act_in, query_full, keyval_full, output_full, gateup_full, down_full, small_full, places):
    highest = lax.Precision.HIGHEST
    query_width = HQ * HD
    kv_width = HK * HD
    gain_one = small_full[:D]
    gain_two = small_full[D:2 * D]
    bias_query = small_full[2 * D:2 * D + query_width]
    bias_keyval = small_full[2 * D + query_width:]
    inv_one = lax.rsqrt(lax.optimization_barrier(jnp.mean(act_in * act_in, axis=1, keepdims=True)) + norm_eps)
    normed_one = low(act_in * inv_one * gain_one)
    query_pre = low_back(jnp.dot(normed_one, query_full, preferred_element_type=jnp.float32, precision=highest) + bias_query)
    keyval_pre = low_back(jnp.dot(normed_one, keyval_full, preferred_element_type=jnp.float32, precision=highest) + bias_keyval)
    cosine, sine_table = rotary_tables(places)
    query_rot = low(rotate(query_pre, cosine, sine_table, HQ, 1.0))
    key_rot = low(rotate(keyval_pre[:, :kv_width], cosine, sine_table, HK, 1.0))
    value_all = low(keyval_pre[:, kv_width:])
    attn_out = low(low_back(attend(query_rot, key_rot, value_all, places)))
    middle = act_in + low_back(jnp.dot(attn_out, output_full, preferred_element_type=jnp.float32, precision=highest))
    inv_two = lax.rsqrt(lax.optimization_barrier(jnp.mean(middle * middle, axis=1, keepdims=True)) + norm_eps)
    normed_two = low(middle * inv_two * gain_two)
    gate_up = low_back(jnp.dot(normed_two, gateup_full, preferred_element_type=jnp.float32, precision=highest))
    hidden = low(jax.nn.silu(gate_up[:, :FF]) * gate_up[:, FF:])
    return middle + low_back(jnp.dot(hidden, down_full, preferred_element_type=jnp.float32, precision=highest))

def adamw_step(gradient, first_old, second_old, weight, step_rate, decay_factor):
    first_new = beta_one * first_old + (1.0 - beta_one) * gradient
    second_new = beta_two * second_old + (1.0 - beta_two) * gradient * gradient
    first_hat = first_new / (1.0 - beta_one ** STEP)
    second_hat = second_new / (1.0 - beta_two ** STEP)
    updated = weight - step_rate * (first_hat / (jnp.sqrt(second_hat) + adam_eps) + decay_factor * weight)
    return (second_new, updated)

def reference(tokens, positions, cotangent, query_weight, query_first, query_second, keyval_weight, keyval_first, keyval_second, output_weight, output_first, output_second, gateup_weight, gateup_first, gateup_second, down_weight, down_first, down_second, small_weight, small_first, small_second):
    masters = (query_weight, keyval_weight, output_weight, gateup_weight, down_weight, small_weight)
    rounded = tuple((low(master) for master in masters))
    act_all = tokens.astype(jnp.float32).reshape(SEQS, SEQ_LEN, D)
    cot_all = cotangent.astype(jnp.float32).reshape(SEQS, SEQ_LEN, D)

    def per_sequence(running_sums, inputs_now):
        act_seq, places, cot_seq = inputs_now

        def forward_only(act_arg, query_arg, keyval_arg, output_arg, gateup_arg, down_arg, small_arg):
            return layer_forward(act_arg, query_arg, keyval_arg, output_arg, gateup_arg, down_arg, small_arg, places)
        out_seq, pull_back = jax.vjp(forward_only, act_seq, rounded[0], rounded[1], rounded[2], rounded[3], rounded[4], rounded[5])
        grads_seq = pull_back(cot_seq)
        new_sums = tuple((summed + addend for summed, addend in zip(running_sums, grads_seq[1:])))
        return (new_sums, (out_seq.astype(jnp.bfloat16), grads_seq[0].astype(jnp.bfloat16)))
    zero_sums = tuple((jnp.zeros(master.shape, jnp.float32) for master in masters))
    grad_sums, (outs_seq, grads_in) = lax.scan(per_sequence, zero_sums, (act_all, positions, cot_all))
    layer_out = outs_seq.reshape(TOKENS, D)
    tokens_grad = grads_in.reshape(TOKENS, D)
    query_grad, keyval_grad, output_grad, gateup_grad, down_grad, small_grad = grad_sums
    query_second_out, query_weight_out = adamw_step(query_grad, query_first, query_second, query_weight, rate_proj, decay_rate)
    keyval_second_out, keyval_weight_out = adamw_step(keyval_grad, keyval_first, keyval_second, keyval_weight, rate_proj, decay_rate)
    output_second_out, output_weight_out = adamw_step(output_grad, output_first, output_second, output_weight, rate_out, decay_rate)
    gateup_second_out, gateup_weight_out = adamw_step(gateup_grad, gateup_first, gateup_second, gateup_weight, rate_proj, decay_rate)
    down_second_out, down_weight_out = adamw_step(down_grad, down_first, down_second, down_weight, rate_proj, decay_rate)
    small_second_all, small_weight_out = adamw_step(small_grad, small_first, small_second, small_weight, rate_small, 0.0)
    rest_length = 2 * D + HQ * HD + HK * HD
    small_second_out = small_second_all[:rest_length]
    value_bias_second_out = small_second_all[rest_length:]
    return (layer_out, tokens_grad, query_grad, query_second_out, query_weight_out, keyval_grad, keyval_second_out, keyval_weight_out, output_grad, output_second_out, output_weight_out, gateup_grad, gateup_second_out, gateup_weight_out, down_grad, down_second_out, down_weight_out, small_grad, small_second_out, value_bias_second_out, small_weight_out)
```

```python
import functools

import jax
import jax.numpy as jnp
from jax import lax
from jax.experimental import pallas as pl
from jax.experimental.pallas import tpu as pltpu
from jax.sharding import PartitionSpec as P

D = 896
HQ = 14
HK = 2
HD = 64
FF = 4864
STEP = 10


theta_base = 1000000.0
norm_eps = 1e-06
beta_one = 0.9
beta_two = 0.95
adam_eps = 1e-08
decay_rate = 0.1
rate_proj = 0.02
rate_out = 0.5
rate_small = 0.2
masked_score = -1e30

low = jnp.bfloat16
wide = jnp.float32


MIB = 1024 * 1024
LANES = 128
ROWS = 16
NT = (((1,), (1,)), ((), ()))
TN = (((0,), (0,)), ((), ()))


def padded(size, unit):
    return -(-size // unit) * unit


def rotary_angles(places):
    half_size = HD // 2
    inv_freq = theta_base ** (-(jnp.arange(half_size, dtype=wide) * 2.0) / HD)
    return places.astype(wide)[:, None] * inv_freq[None, :]


def adamw_step(gradient, first_old, second_old, weight, step_rate, decay_factor):
    first_new = beta_one * first_old + (1.0 - beta_one) * gradient
    second_new = beta_two * second_old + (1.0 - beta_two) * gradient * gradient
    first_hat = first_new / (1.0 - beta_one**STEP)
    second_hat = second_new / (1.0 - beta_two**STEP)
    updated = weight - step_rate * (
        first_hat / (jnp.sqrt(second_hat) + adam_eps) + decay_factor * weight
    )
    return (second_new, updated)


def params(limit=56):
    return pltpu.CompilerParams(
        vmem_limit_bytes=limit * MIB, dimension_semantics=("arbitrary",)
    )


def cost(micros):
    return pl.CostEstimate(flops=int(micros * 10**9), bytes_accessed=10**6, transcendentals=0)


def split_heads(pair, number):
    lane = lax.broadcasted_iota(jnp.int32, pair.shape, 1)
    zero = jnp.zeros_like(pair)
    turned = pltpu.roll(pair, HD, 1)
    low_a = 2 * number < HQ // HK
    low_b = 2 * number + 1 < HQ // HK
    first = jnp.where((lane < HD) == low_a, jnp.where(low_a, pair, turned), zero)
    second = jnp.where((lane < HD) == low_b, jnp.where(low_b, turned, pair), zero)
    return jnp.concatenate([first, second], axis=0)


def join_heads(both, number, half):
    low_a = 2 * number < HQ // HK
    low_b = 2 * number + 1 < HQ // HK
    first = jnp.where(low_a, both[:HD, :half], both[HD:, :half])
    second = jnp.where(low_b, both[:HD, half:], both[HD:, half:])
    return first, second


def key_mask(start, first_key, first_query, half, causal):
    key_row = lax.broadcasted_iota(jnp.int32, (half, half), 0)
    ok = key_row >= start - first_key
    if causal:
        ok &= key_row <= lax.broadcasted_iota(jnp.int32, (1, half), 1) + (first_query - first_key)
    return jnp.concatenate([ok, ok], axis=1)


def query_mask(start, first_key, first_query, half, causal):
    key = lax.broadcasted_iota(jnp.int32, (half, half), 1)
    ok = key >= jnp.concatenate([start - first_key] * (half // LANES), axis=1)
    if causal:
        ok &= key <= lax.broadcasted_iota(jnp.int32, (half, half), 0) + (first_query - first_key)
    return jnp.concatenate([ok, ok], axis=0)


def visit_blocks(meta, start_ref, half, pieces, visit):
    mine = meta[0]
    first_query = mine * 2 * half
    turned = start_ref.shape[2] == LANES
    mask_of = query_mask if turned else key_mask
    start_of = lambda sel: start_ref[sel] if turned else start_ref[sel, 0:1, :]
    for sel, block in ((0, 0), (1, 0), (1, 1)):
        mask = mask_of(
            start_of(sel), first_query + block * half, first_query + sel * half, half, sel == block
        )
        visit(sel, 0, block, mask)
    for piece in range(1, pieces):
        first_key = (mine - piece) * 2 * half

        def region(cut):
            for block in range(2):
                for sel in range(2):
                    if cut and block == 0:
                        mask = mask_of(start_of(sel), first_key, first_query, half, False)
                    else:
                        mask = start_of(sel) <= first_key + block * half
                        mask = jnp.concatenate([mask, mask], axis=0 if turned else 1)
                    visit(sel, piece, block, mask)

        pl.when(mine == piece)(functools.partial(region, True))
        pl.when(mine > piece)(functools.partial(region, False))


def forward_kernel(pieces, meta, pre_ref, cos_ref, sin_ref, start_ref, starts_ref, *refs):
    kv_refs = refs[:pieces]
    o_ref, lse_ref, q_ref, two_ref, top_ref, sum_ref, acc_ref = refs[pieces:]
    number = pl.program_id(0)
    rows = pre_ref.shape[0]
    half = rows // 2
    pre = pre_ref[...]
    lane = lax.broadcasted_iota(jnp.int32, pre.shape, 1)
    swapped = jnp.where(
        lane % HD < HD // 2, pltpu.roll(pre, LANES - HD // 2, 1), pltpu.roll(pre, HD // 2, 1)
    )
    turned = (pre * cos_ref[...] + swapped * sin_ref[...]).astype(low)
    turned = (turned.astype(wide) * (1.0 / HD**0.5)).astype(low)
    q_ref[...] = turned
    for which in range(2):
        two_ref[which] = split_heads(turned[which * half : (which + 1) * half, :], number)
    top_ref[...] = jnp.full_like(top_ref, masked_score)
    sum_ref[...] = jnp.zeros_like(sum_ref)
    acc_ref[...] = jnp.zeros_like(acc_ref)

    def scores_of(sel, piece, block):
        part = slice(block * half, (block + 1) * half)
        return lax.dot_general(
            two_ref[sel], kv_refs[piece][part, :LANES], NT, preferred_element_type=wide
        )

    def find_top(sel, piece, block, mask):
        scores = scores_of(sel, piece, block)
        if mask.shape[1] > LANES:
            scores = jnp.where(mask, scores, masked_score)
        peak = functools.reduce(jnp.maximum, [scores[:, i : i + LANES] for i in range(0, half, LANES)])
        if mask.shape[1] <= LANES:
            peak = jnp.where(mask, peak, masked_score)
        top_ref[sel] = jnp.maximum(top_ref[sel], peak)

    def sum_up(sel, piece, block, mask):
        part = slice(block * half, (block + 1) * half)
        scores = scores_of(sel, piece, block)
        level = top_ref[sel]
        if mask.shape[1] > LANES:
            scores = jnp.where(mask, scores, masked_score)
        else:
            level = jnp.where(mask, level, -masked_score)
        weights = [jnp.exp(scores[:, i : i + LANES] - level) for i in range(0, half, LANES)]
        sum_ref[sel] += functools.reduce(jnp.add, weights)
        acc_ref[sel] += jnp.dot(
            jnp.concatenate(weights, axis=1).astype(low),
            kv_refs[piece][part, LANES:],
            preferred_element_type=wide,
        )

    visit_blocks(meta, starts_ref, half, pieces, find_top)
    for which in range(2):
        top_ref[which] = jnp.broadcast_to(
            jnp.max(top_ref[which], axis=1, keepdims=True), top_ref.shape[1:]
        )
    visit_blocks(meta, starts_ref, half, pieces, sum_up)
    lane = lax.broadcasted_iota(jnp.int32, (half, LANES), 1)
    low_a = 2 * number < HQ // HK
    low_b = 2 * number + 1 < HQ // HK
    pick = jnp.where(lax.broadcasted_iota(jnp.int32, (8, LANES), 1) == 0, 1.0, 0.0).astype(wide)
    for which in range(2):
        total = jnp.sum(sum_ref[which], axis=1, keepdims=True)
        out = acc_ref[which] / total
        first, second = out[:half], out[half:]
        first = jnp.where(low_a, first, pltpu.roll(first, HD, 1))
        second = jnp.where(low_b, pltpu.roll(second, HD, 1), second)
        o_ref[which * half : (which + 1) * half, :] = jnp.where(lane < HD, first, second)
        lse = top_ref[which] + jnp.log(total)
        lse_ref[0, :, which * rows : (which + 1) * rows] = lax.dot_general(
            pick, lse, NT, precision=lax.Precision.HIGHEST, preferred_element_type=wide
        )


def attention_forward(pre, cos_wide, sin_wide, starts, kv_pieces, meta):
    rows, width = pre.shape
    pairs, pieces = width // LANES, len(kv_pieces)
    pair = pl.BlockSpec((rows, LANES), lambda p, m: (0, p))
    whole = lambda a: pl.BlockSpec(a.shape, lambda p, m: (0,) * a.ndim)
    starts_wide = jnp.broadcast_to(starts[:, 0, :, None], (2, rows // 2, LANES))
    operands = (cos_wide, sin_wide, starts, starts_wide, *kv_pieces)
    spec = pltpu.PrefetchScalarGridSpec(
        num_scalar_prefetch=1,
        grid=(pairs,),
        in_specs=[pair] + [whole(a) for a in operands],
        out_specs=[pair, pl.BlockSpec((1, 8, 2 * rows), lambda p, m: (p, 0, 0)), pair],
        scratch_shapes=[
            pltpu.VMEM((2, rows, LANES), low),
            pltpu.VMEM((2, rows, LANES), wide),
            pltpu.VMEM((2, rows, LANES), wide),
            pltpu.VMEM((2, rows, LANES), wide),
        ],
    )
    return pl.pallas_call(
        functools.partial(forward_kernel, pieces),
        grid_spec=spec,
        out_shape=[
            jax.ShapeDtypeStruct((rows, width), wide),
            jax.ShapeDtypeStruct((pairs, 8, 2 * rows), wide),
            jax.ShapeDtypeStruct((rows, width), low),
        ],
        compiler_params=params(48),
        cost_estimate=cost(40),
        name="attention_forward",
    )(meta, pre, *operands)


def backward_kernel(pieces, meta, q_ref, do_ref, o_ref, lse_ref, start_ref, cos_ref, sin_ref, *refs):
    kv_refs = refs[:pieces]
    dq_ref = refs[pieces]
    out_refs = refs[pieces + 1 : 2 * pieces + 1]
    kt_ref, two_ref, dot_ref, delta_ref, acc_ref, dkv_ref = refs[2 * pieces + 1 :]
    number = pl.program_id(0)
    rows = q_ref.shape[0]
    half = rows // 2

    @pl.when(number == 0)
    def _():
        dkv_ref[...] = jnp.zeros_like(dkv_ref)
        for piece in range(pieces):
            kt_ref[piece] = kv_refs[piece][:, :LANES].astype(wide).T.astype(low)

    acc_ref[...] = jnp.zeros_like(acc_ref)
    lane = lax.broadcasted_iota(jnp.int32, (8, LANES), 1)
    pick_a = jnp.where(lane < HD, 1.0, 0.0).astype(wide)
    pick_b = 1.0 - pick_a
    for which in range(2):
        part = slice(which * half, (which + 1) * half)
        two_ref[which] = split_heads(q_ref[part, :], number)
        dot_ref[which] = split_heads(do_ref[part, :], number)
        product = do_ref[part, :].astype(wide) * o_ref[part, :]
        delta_ref[which] = jnp.concatenate(
            [
                lax.dot_general(
                    pick, product, NT, precision=lax.Precision.HIGHEST, preferred_element_type=wide
                )
                for pick in (pick_a, pick_b)
            ],
            axis=1,
        )

    def visit(sel, piece, block, mask):
        part = slice(block * half, (block + 1) * half)
        two, dot = two_ref[sel], dot_ref[sel]
        keys, values = kv_refs[piece][part, :LANES], kv_refs[piece][part, LANES:]
        scores = lax.dot_general(keys, two, NT, preferred_element_type=wide)
        grad_weights = lax.dot_general(values, dot, NT, preferred_element_type=wide)
        lse = lse_ref[0, 0:1, sel * rows : (sel + 1) * rows]
        if mask.shape[0] > 1:
            weights = jnp.where(mask, jnp.exp(scores - lse), 0.0)
        else:
            weights = jnp.exp(scores - jnp.where(mask, lse, -masked_score))
        grad_scores = (weights * (grad_weights - delta_ref[sel, 0:1, :])).astype(low)
        dkv_ref[piece, part, LANES:] += jnp.dot(
            weights.astype(low), dot, preferred_element_type=wide
        )
        dkv_ref[piece, part, :LANES] += jnp.dot(grad_scores, two, preferred_element_type=wide)
        acc_ref[sel] += jnp.dot(kt_ref[piece, :, part], grad_scores, preferred_element_type=wide)

    visit_blocks(meta, start_ref, half, pieces, visit)
    for which in range(2):
        part = slice(which * half, (which + 1) * half)
        cos, sin = cos_ref[:, part], sin_ref[:, part]
        turned = []
        for head in join_heads(acc_ref[which] * (1.0 / HD**0.5), number, half):
            upper, lower = head[: HD // 2], head[HD // 2 :]
            turned += [upper * cos + lower * sin, lower * cos - upper * sin]
        dq_ref[part, :] = jnp.concatenate(turned, axis=0).T.astype(low)

    @pl.when(number == pl.num_programs(0) - 1)
    def _():
        for piece in range(pieces):
            out_refs[piece][...] = dkv_ref[piece].astype(out_refs[piece].dtype)


def attention_backward(q, do, o, lse, starts, cos_turned, sin_turned, kv_pieces, meta):
    rows, width = q.shape
    pairs, pieces = width // LANES, len(kv_pieces)
    pair = pl.BlockSpec((rows, LANES), lambda p, m: (0, p))
    whole = lambda a: pl.BlockSpec(a.shape, lambda p, m: (0,) * a.ndim)
    fixed = (starts, cos_turned, sin_turned, *kv_pieces)
    spec = pltpu.PrefetchScalarGridSpec(
        num_scalar_prefetch=1,
        grid=(pairs,),
        in_specs=[pair, pair, pair, pl.BlockSpec((1, 8, 2 * rows), lambda p, m: (p, 0, 0))]
        + [whole(a) for a in fixed],
        out_specs=[pair] + [whole(a) for a in kv_pieces],
        scratch_shapes=[
            pltpu.VMEM((pieces, LANES, rows), low),
            pltpu.VMEM((2, rows, LANES), low),
            pltpu.VMEM((2, rows, LANES), low),
            pltpu.VMEM((2, 8, rows), wide),
            pltpu.VMEM((2, LANES, rows), wide),
            pltpu.VMEM((pieces, rows, 2 * LANES), wide),
        ],
    )
    return pl.pallas_call(
        functools.partial(backward_kernel, pieces),
        grid_spec=spec,
        out_shape=[jax.ShapeDtypeStruct((rows, width), low)]
        + [
            jax.ShapeDtypeStruct((rows, 2 * LANES), wide if piece == 0 else low)
            for piece in range(pieces)
        ],
        compiler_params=params(48),
        cost_estimate=cost(40),
        name="attention_backward",
    )(meta, q, do, o, lse, *fixed)


def feed_kernel(
    steps, fresh, place, n_a, n_b, cot_ref, gateup_ref, down_ref, *refs
):
    refs = refs[0 if fresh else 5 :]
    back_a, back_b, left_ref, right_ref, hidden_ref, grad_ref, kept_ref = refs
    width = down_ref.shape[0]
    first = pl.program_id(0) < steps // 2
    normed = jnp.where(first, n_a[...], n_b[...])
    cot = cot_ref[...]
    gate = jnp.dot(normed, gateup_ref[:, :width], preferred_element_type=wide)
    up = jnp.dot(normed, gateup_ref[:, width:], preferred_element_type=wide)
    grad_hidden = lax.dot_general(cot, down_ref[...], NT, preferred_element_type=wide)
    sigmoid = jax.nn.sigmoid(gate)
    act = gate * sigmoid
    hidden = (act * up).astype(low)
    grad_gate = (grad_hidden * up * sigmoid * (1.0 + gate * (1.0 - sigmoid))).astype(low)
    grad_up = (grad_hidden * act).astype(low)
    kept_ref[...] = normed
    hidden_ref[...] = hidden
    grad_ref[:, :width] = grad_gate
    grad_ref[:, width:] = grad_up
    out = jnp.dot(hidden, down_ref[...], preferred_element_type=wide).astype(low)
    left_ref[...] = out[:, : left_ref.shape[1]]
    right_ref[...] = out[:, left_ref.shape[1] :]
    back = lax.dot_general(grad_gate, gateup_ref[:, :width], NT, preferred_element_type=wide)
    back = back + lax.dot_general(grad_up, gateup_ref[:, width:], NT, preferred_element_type=wide)

    @pl.when(first)
    def _():
        back_a[...] = back.astype(low)

    @pl.when(jnp.logical_not(first))
    def _():
        back_b[...] = back.astype(low)


def feed_forward(n_a, n_b, cot_all, gateup, down, place, kept, block=256):
    rows, d = n_a.shape
    total, width = cot_all.shape[0], down.shape[0]
    block = min(block, rows)
    left = padded(d // 2, LANES)
    each = rows // block
    steps = 2 * each
    spot = lambda i, place: (place[i // each] * each + i % each, 0)
    whole = lambda a: pl.BlockSpec(a.shape, lambda i, place: (0, 0))
    halves = [
        pl.BlockSpec((block, d), lambda i, place: (jnp.minimum(i, each - 1), 0)),
        pl.BlockSpec((block, d), lambda i, place: (jnp.maximum(i - each, 0), 0)),
    ]
    in_specs = halves + [
        pl.BlockSpec((block, d), spot),
        whole(gateup),
        whole(down),
    ]
    fresh = kept is None
    if not fresh:
        in_specs += [pl.BlockSpec(memory_space=pl.ANY)] * 5
    spec = pltpu.PrefetchScalarGridSpec(
        num_scalar_prefetch=1,
        grid=(steps,),
        in_specs=in_specs,
        out_specs=halves
        + [pl.BlockSpec((block, n), spot) for n in (left, d - left, width, 2 * width, d)],
    )
    shapes = [(rows, d)] * 2 + [(total, n) for n in (left, d - left, width, 2 * width, d)]
    return pl.pallas_call(
        functools.partial(feed_kernel, steps, fresh),
        grid_spec=spec,
        out_shape=[jax.ShapeDtypeStruct(s, low) for s in shapes],
        input_output_aliases={} if fresh else {6 + i: 2 + i for i in range(5)},
        compiler_params=params(),
        cost_estimate=cost(4),
        name="feed_forward",
    )(place, n_a, n_b, cot_all, gateup, down, *(() if fresh else kept))


def weight_kernel(steps, shape, take, give, split, fill, where, x_ref, y_ref, *refs):
    outputs = 2 if split else 1
    acc_ref = refs[-1]
    out_refs = refs[-1 - outputs : -1]
    chips, cores, groups = shape
    step = pl.program_id(0)
    size = x_ref.shape[1]
    product = lax.dot_general(x_ref[...], y_ref[...], TN, preferred_element_type=wide)

    @pl.when(step == 0)
    def _():
        acc_ref[:size] = product
        acc_ref[size:] = jnp.zeros_like(acc_ref[size:])

    @pl.when(step > 0)
    def _():
        acc_ref[:size] += product

    keep = lax.broadcasted_iota(jnp.int32, (give, 1), 0) < take

    def write(mine):
        for chip in range(chips):
            for core in range(cores):
                for group in range(groups):
                    low_edge = ((chip * cores + core) * groups + group) * take
                    value = jnp.where(keep, acc_ref[low_edge : low_edge + give], 0.0)
                    if fill:
                        value += refs[0][low_edge // take].astype(wide)
                    value = value.astype(low)
                    at = lax.rem(group + groups - where[2], groups)
                    if split:
                        out_refs[core ^ mine][chip ^ where[1], at] = value
                    else:
                        row = (chip * cores + core) * give
                        out_refs[0][at, row : row + give] = value

    if split:
        for mine in range(cores):
            pl.when((step == steps - 1) & (where[0] == mine))(functools.partial(write, mine))
    else:
        pl.when(step == steps - 1)(functools.partial(write, 0))


def weight_gradient(
    x, y, shape, take, where, split=False, block=1024, column=0, columns=1, into=None, extra=None
):
    total, size = x.shape
    width = y.shape[1]
    give = padded(take, ROWS) if extra is None else extra.shape[1]
    block = min(block, total)
    steps = total // block
    chips, cores, groups = shape
    if split:
        out = pl.BlockSpec((chips, groups, give, width), lambda i, w: (0, 0, 0, column))
        shapes = [(chips, groups, give, columns * width)] * 2
    else:
        out = pl.BlockSpec((groups, chips * cores * give, width), lambda i, w: (0, 0, 0))
        shapes = [(groups, chips * cores * give, width)]
    fill = extra is not None
    into = [] if into is None else into
    return pl.pallas_call(
        functools.partial(weight_kernel, steps, shape, take, give, split, fill),
        grid_spec=pltpu.PrefetchScalarGridSpec(
            num_scalar_prefetch=1,
            grid=(steps,),
            in_specs=[
                pl.BlockSpec((block, size), lambda i, w: (i, 0)),
                pl.BlockSpec((block, width), lambda i, w: (i, 0)),
            ]
            + [pl.BlockSpec(extra.shape, lambda i, w: (0, 0, 0)) for _ in range(fill)]
            + [pl.BlockSpec(memory_space=pl.ANY)] * len(into),
            out_specs=[out] * len(shapes),
            scratch_shapes=[pltpu.VMEM((padded(size, 8) + give, width), wide)],
        ),
        out_shape=[jax.ShapeDtypeStruct(shape, low) for shape in shapes],
        input_output_aliases={3 + fill + i: i for i in range(len(into))},
        compiler_params=params(),
        cost_estimate=cost(1 if steps > 1 else 0.2),
        name="weight_gradient",
    )(where, x, y, *([extra] if fill else []), *into)


def assemble_kernel(
    n_dp, n_group, take, give, meta, own_ref, other_ref, o_ref, small_ref, at_ref, acc_ref
):
    me, mine = meta[0], meta[1]
    for r in range(n_dp):
        source = own_ref if r % 2 == 0 else other_ref
        for s in range(n_group):
            row = (r // 2 * n_group + s) * give
            z = lax.rem(mine + s, n_group)
            at_ref[(me ^ r) * n_group + z] = source[row : row + give].astype(wide)
    for i in range(n_dp * n_group):
        acc_ref[i * take : i * take + give] = at_ref[i]
        for j in range(2):
            small_ref[j, i : i + 1] = at_ref[i, take + j : take + j + 1]
    size = o_ref.shape[0]
    o_ref[...] = acc_ref[:size].astype(low)


def assemble(own, other, n_dp, n_group, take, give, me, mine):
    width = own.shape[1]
    size = n_dp * n_group * take
    return pl.pallas_call(
        functools.partial(assemble_kernel, n_dp, n_group, take, give),
        grid_spec=pltpu.PrefetchScalarGridSpec(
            num_scalar_prefetch=1,
            grid=(1,),
            in_specs=[pl.BlockSpec(own.shape, lambda i, m: (0, 0))] * 2,
            out_specs=[
                pl.BlockSpec((size, width), lambda i, m: (0, 0)),
                pl.BlockSpec((2, n_dp * n_group, width), lambda i, m: (0, 0, 0)),
            ],
            scratch_shapes=[
                pltpu.VMEM((n_dp * n_group, give, width), wide),
                pltpu.VMEM((size + give, width), wide),
            ],
        ),
        out_shape=[
            jax.ShapeDtypeStruct((size, width), low),
            jax.ShapeDtypeStruct((2, n_dp * n_group, width), wide),
        ],
        compiler_params=params(),
        cost_estimate=cost(1),
        name="assemble_rows",
    )(jnp.stack([me, mine]).astype(jnp.int32), own, other)


def stack_kernel(outer, count, take, give, meta, *refs):
    o_ref, at_ref, acc_ref = refs[count:]
    for s in range(count):
        z = lax.rem(meta[0] + s, count)
        for i in range(outer):
            at_ref[i * count + z] = refs[s][i * give : (i + 1) * give].astype(wide)
    for i in range(outer * count):
        acc_ref[i * take : i * take + give] = at_ref[i]
    size = outer * count * take
    o_ref[:size] = acc_ref[:size].astype(low)
    if o_ref.shape[0] > size:
        o_ref[size:] = jnp.zeros_like(o_ref[size:])


def stack_rows(pieces, outer, take, me, rows):
    count, width = len(pieces), pieces[0].shape[1]
    give = pieces[0].shape[0] // outer
    whole = lambda r: pl.BlockSpec((r, width), lambda i, m: (0, 0))
    return pl.pallas_call(
        functools.partial(stack_kernel, outer, count, take, give),
        grid_spec=pltpu.PrefetchScalarGridSpec(
            num_scalar_prefetch=1,
            grid=(1,),
            in_specs=[whole(outer * give)] * count,
            out_specs=whole(rows),
            scratch_shapes=[
                pltpu.VMEM((outer * count, give, width), wide),
                pltpu.VMEM((padded(outer * count * take, 8) + give, width), wide),
            ],
        ),
        out_shape=jax.ShapeDtypeStruct((rows, width), low),
        compiler_params=params(),
        cost_estimate=cost(1),
        name="stack_rows",
    )(me, *pieces)


def cut_kernel(count, part, part_wide, w_ref, o_ref, buffer_ref):
    rows = w_ref.shape[0]
    buffer_ref[...] = jnp.zeros_like(buffer_ref)
    for p in range(count):
        for j in range(2):
            column = (j * count + p) * part
            buffer_ref[:rows, j * part_wide : j * part_wide + part] = w_ref[
                :, column : column + part
            ]
        o_ref[p] = buffer_ref[...].astype(low)


def cut_columns(weight, count, part_wide, give):
    rows, width = weight.shape
    part = width // (2 * count)
    shape = (count, give, 2 * part_wide)
    return pl.pallas_call(
        functools.partial(cut_kernel, count, part, part_wide),
        grid=(1,),
        in_specs=[pl.BlockSpec(weight.shape, lambda i: (0, 0))],
        out_specs=pl.BlockSpec(shape, lambda i: (0, 0, 0)),
        out_shape=jax.ShapeDtypeStruct(shape, low),
        scratch_shapes=[pltpu.VMEM((give, 2 * part_wide), wide)],
        compiler_params=params(),
        cost_estimate=cost(1),
        name="cut_columns",
    )(weight)


def update_kernel(count, part, part_wide, g_ref, m_ref, v_ref, w_ref, go_ref, vo_ref, wo_ref):
    rows = w_ref.shape[0]
    for p in range(count):
        piece = g_ref[p].astype(wide)
        for j in range(2):
            column = (j * count + p) * part
            go_ref[:, column : column + part] = piece[
                :rows, j * part_wide : j * part_wide + part
            ]
    vo_ref[...], wo_ref[...] = adamw_step(
        go_ref[...], m_ref[...], v_ref[...], w_ref[...], rate_proj, decay_rate
    )


def update_columns(pieces, first, second, weight):
    count, _, width = pieces.shape
    spec = pl.BlockSpec(weight.shape, lambda i: (0, 0))
    return pl.pallas_call(
        functools.partial(
            update_kernel, count, weight.shape[1] // (2 * count), width // 2
        ),
        grid=(1,),
        in_specs=[pl.BlockSpec(pieces.shape, lambda i: (0, 0, 0))] + [spec] * 3,
        out_specs=[spec] * 3,
        out_shape=[jax.ShapeDtypeStruct(weight.shape, wide)] * 3,
        compiler_params=params(),
        cost_estimate=cost(1),
        name="update_columns",
    )(pieces, first, second, weight)


def flip(value, mask):
    count = lax.axis_size("dp")
    return lax.ppermute(value, "dp", [(i, i ^ mask) for i in range(count)])


def shift(value, step):
    count = lax.axis_size("group")
    return lax.ppermute(value, "group", [((i + step) % count, i) for i in range(count)])


def after(value, *others):
    return lax.optimization_barrier((value, *others))[0]


def group_pieces(block, steps=None):
    return [block] + [shift(block, s) for s in range(1, lax.axis_size("group"))]


def group_send(blocks):
    count = lax.axis_size("group")
    return [blocks[0]] + [shift(blocks[count - s].astype(low), s) for s in range(1, count)]


def add_up(terms):
    return functools.reduce(jnp.add, [term.astype(wide) for term in terms])


def gather_column(block):
    return jnp.concatenate(group_pieces(block), axis=0)


def gather_chips(column):
    evens = [column] + [flip(column, r) for r in range(2, lax.axis_size("dp"), 2)]
    return jnp.concatenate(evens, axis=0)


def gather_rows(own, other, take):
    n_dp, n_group = lax.axis_size("dp"), lax.axis_size("group")
    give = own.shape[0] // (n_dp // 2 * n_group)
    return assemble(
        own, other, n_dp, n_group, take, give, lax.axis_index("dp"), lax.axis_index("group")
    )


def scatter_chips(keep, send):
    pair = keep.astype(wide) + flip(send, 1).astype(wide)
    got = [flip(pair[r].astype(low), 2 * r) for r in range(1, pair.shape[0])]
    return add_up([pair[0]] + got)


def split_low(value):
    first = lax.reduce_precision(value, 8, 7)
    rest = value - first
    second = lax.reduce_precision(rest, 8, 7)
    return [first.astype(low), second.astype(low), (rest - second).astype(low)]


def body(
    tokens,
    positions,
    cotangent,
    query_weight,
    query_first,
    query_second,
    keyval_weight,
    keyval_first,
    keyval_second,
    output_weight,
    output_first,
    output_second,
    gateup_weight,
    gateup_first,
    gateup_second,
    down_weight,
    down_first,
    down_second,
    small_weight,
    small_first,
    small_second,
):
    row_count = tokens.shape[0]
    half = row_count // 2
    n_dp = lax.axis_size("dp")
    group_size = lax.axis_size("group")
    device_count = n_dp * group_size
    my_dp = lax.axis_index("dp")
    my_index = lax.axis_index("group")
    flat_index = my_dp * group_size + my_index
    seq_len = row_count * group_size
    query_width = HQ * HD
    kv_width = HK * HD
    small_size = 2 * D + query_width + 2 * kv_width
    rest_length = small_size - kv_width
    rest_piece = rest_length // device_count
    value_piece = kv_width // device_count
    small_piece = small_size // device_count
    part = FF // n_dp
    part_wide = padded(part, LANES)
    in_rows = query_weight.shape[0]
    in_give = padded(in_rows + 2, ROWS)
    down_rows = down_weight.shape[0]

    small_rows = [small_weight.astype(low)] + split_low(small_second)
    small_rows = jnp.concatenate(small_rows).reshape(2, 2 * small_piece)
    small_rows = jnp.pad(small_rows, ((0, 0), (0, 2 * kv_width - 2 * small_piece)))
    keyval_block = jnp.concatenate([keyval_weight.astype(low), small_rows], axis=0)
    keyval_block = jnp.pad(keyval_block, ((0, in_give - in_rows - 2), (0, 0)))
    keyval_column = gather_column(keyval_block)
    keyval_own = gather_chips(keyval_column)
    keyval_full, small_all = gather_rows(keyval_own, flip(keyval_own, 1), in_rows)
    small_all = small_all[:, :, : 2 * small_piece].reshape(2, device_count, 2, small_piece)
    small_values = small_all[0, :, 0].reshape(small_size)
    small_second_all = (small_all[0, :, 1] + small_all[1, :, 0] + small_all[1, :, 1]).reshape(
        small_size
    )
    both_block = jnp.concatenate([query_weight.astype(low), output_weight.astype(low)], axis=1)
    both_block = jnp.pad(both_block, ((0, in_give - in_rows), (0, 0)))
    both_column = gather_column(after(both_block, keyval_column))
    both_own = gather_chips(after(both_column, keyval_full))
    both_other = flip(both_own, 1)
    cot_all = lax.all_gather(after(cotangent, both_own), "dp", axis=0, tiled=True)
    gateup_pieces = cut_columns(gateup_weight, n_dp, part_wide, in_give)
    gateup_column = lax.all_to_all(after(gateup_pieces, keyval_column), "dp", 0, 0, tiled=True)
    down_block = jnp.pad(down_weight.astype(low), ((0, padded(down_rows, ROWS) - down_rows), (0, 0)))
    down_pieces = group_pieces(after(down_block, keyval_column))
    me_group = my_index.astype(jnp.int32)[None]
    down_part = stack_rows(down_pieces, 1, down_rows, me_group, part_wide)

    gain_one = small_values[:D]
    gain_two = small_values[D : 2 * D]
    bias_qkv = small_values[2 * D :]
    place_row = positions[0]
    local_index = my_index * row_count + jnp.arange(row_count, dtype=jnp.int32)
    local_places = lax.dynamic_slice_in_dim(place_row, my_index * row_count, row_count, 0)
    starts = (local_index - local_places).reshape(2, half).astype(jnp.int32)
    starts = jnp.broadcast_to(starts[:, None, :], (2, 8, half))
    meta = jnp.stack([my_index, my_index]).astype(jnp.int32)
    angles = rotary_angles(local_places)
    cosine, sine_table = jnp.cos(angles), jnp.sin(angles)
    cos_wide = jnp.concatenate([cosine] * 4, axis=1)
    sin_wide = jnp.concatenate([-sine_table, sine_table] * 2, axis=1)

    def swap(values):
        quarter = HD // 2
        pieces = [values[:, i * quarter : (i + 1) * quarter] for i in range(2 * HK)]
        return jnp.concatenate([pieces[i ^ 1] for i in range(2 * HK)], axis=1)

    act_in = tokens.astype(wide)
    inv_one = lax.rsqrt(jnp.mean(act_in * act_in, axis=1, keepdims=True) + norm_eps)
    scaled_one = act_in * inv_one
    normed_one = (scaled_one * gain_one).astype(low)
    keyval_pre = (
        jnp.dot(normed_one, keyval_full, preferred_element_type=wide) + bias_qkv[query_width:]
    )
    key_pre = keyval_pre[:, :kv_width]
    key_low = (key_pre * cos_wide + swap(key_pre) * sin_wide).astype(low)
    keyval_low = jnp.concatenate([key_low, keyval_pre[:, kv_width:].astype(low)], axis=1)
    keyval_low = after(keyval_low, gateup_column, down_pieces)
    both_full, _ = gather_rows(after(both_own, keyval_low), both_other, in_rows)
    query_full, output_full = both_full[:, :query_width], both_full[:, query_width:]
    keyval_parts = group_pieces(keyval_low)
    keyval_parts = [keyval_parts[-s % group_size] for s in range(group_size)]
    query_pre = (
        jnp.dot(normed_one, query_full, preferred_element_type=wide) + bias_qkv[:query_width]
    )
    keyval_parts = after(keyval_parts, query_pre)
    gateup_column = after(gateup_column, *keyval_parts).reshape(n_dp * in_give, 2 * part_wide)
    gateup_pieces = group_pieces(gateup_column)
    attn_float, log_total, query_low = attention_forward(
        query_pre, cos_wide, sin_wide, starts, keyval_parts, meta
    )
    attn_float = after(attn_float, gateup_pieces)
    gateup_part = stack_rows(gateup_pieces, n_dp, in_rows, me_group, D)
    attn_low = attn_float.astype(low)
    middle = act_in + jnp.dot(attn_low, output_full, preferred_element_type=wide)
    inv_two = lax.rsqrt(jnp.mean(middle * middle, axis=1, keepdims=True) + norm_eps)
    scaled_two = middle * inv_two
    normed_two = (scaled_two * gain_two).astype(low)

    chips = n_dp // 2
    kept, sides, back = None, {0: normed_two}, {}
    for k in range(1, chips):
        if n_dp != 8 or k != 3:
            sides[k] = flip(normed_two, 2 * k)

    def visit(k, kept):
        place = jnp.stack([my_dp ^ (2 * k), my_dp ^ (2 * k + 1)]).astype(jnp.int32)
        back_a, back_b, *kept = feed_forward(
            sides[k], flip(sides[k], 1), cot_all, gateup_part, down_part, place, kept
        )
        back[k] = (back_a, flip(back_b, 1))
        return kept

    if n_dp == 8:
        kept = visit(0, kept)
        sides[1], sides[2] = after((sides[1], sides[2]), kept)
        across = [flip(sides[1][:half], 4), flip(sides[2][half:], 2)]
        kept = visit(1, kept)
        sides[3] = jnp.concatenate(across, axis=0)
        kept = visit(3, kept)
        corner = add_up(back[3]).astype(low)
        across = [flip(corner[:half], 2), flip(corner[half:], 4)]
        kept = visit(2, kept)
        nothing = jnp.zeros_like(across[0])
        x_sum = add_up([*back[1], jnp.concatenate([nothing, across[1]], axis=0)]).astype(low)
        y_sum = add_up([*back[2], jnp.concatenate([across[0], nothing], axis=0)]).astype(low)
        kept, y_sum = after((kept, y_sum))
        returned = [*back[0], flip(x_sum, 2), flip(y_sum, 4)]
    else:
        for k in range(chips):
            kept = visit(k, kept)
        returned = list(back[0])
        returned += [flip(add_up(back[k]).astype(low), 2 * k) for k in range(1, chips)]
    out_left, out_right, hidden_all, gate_all, normed_all = kept
    pieces = (n_dp // 2, 2, group_size)
    device = jnp.stack([my_dp & 1, my_dp >> 1, my_index]).astype(jnp.int32)
    (gateup_term,) = weight_gradient(normed_all, gate_all, pieces, in_rows, device)
    gateup_got = group_send(gateup_term)
    (down_term,) = weight_gradient(hidden_all, cot_all, (1, 1, group_size), down_rows, device)
    down_got = group_send(down_term)
    returned = after(returned, gateup_term, down_term)
    grad_normed_two = add_up(returned)
    out_left = lax.psum_scatter(after(out_left, returned), "dp", scatter_dimension=0, tiled=True)

    grad_out = cotangent.astype(wide)
    gain_scaled_two = grad_normed_two * gain_two
    gain_two_term = jnp.sum(grad_normed_two * scaled_two, axis=0)
    grad_middle = grad_out + inv_two * (
        gain_scaled_two - scaled_two * jnp.mean(gain_scaled_two * scaled_two, axis=1, keepdims=True)
    )
    grad_middle_low = grad_middle.astype(low)
    grad_attn_low = lax.dot_general(
        grad_middle_low, output_full, NT, preferred_element_type=wide
    ).astype(low)
    both_terms = weight_gradient(
        attn_low, grad_middle_low, pieces, in_rows, device, split=True, column=1, columns=2
    )
    grad_query_pre, *keyval_terms = attention_backward(
        query_low,
        grad_attn_low,
        attn_float,
        log_total,
        starts,
        cosine.T,
        sine_table.T,
        keyval_parts,
        meta,
    )
    grad_query_pre, keyval_terms = after(
        (grad_query_pre, keyval_terms), down_got, gateup_got[:-1], out_left
    )
    keyval_got = [keyval_terms[0]] + [shift(keyval_terms[s], s) for s in range(1, group_size)]
    out_right = lax.psum_scatter(
        after(out_right, grad_query_pre), "dp", scatter_dimension=0, tiled=True
    )
    both_terms = weight_gradient(
        normed_one, grad_query_pre, pieces, in_rows, device, split=True, columns=2, into=both_terms
    )
    both_total = scatter_chips(*both_terms)
    grad_normed_one = lax.dot_general(grad_query_pre, query_full, NT, preferred_element_type=wide)
    keyval_grads = add_up(keyval_got)
    down_grad = add_up(after(down_got, keyval_grads))[:down_rows]
    gateup_sum = add_up(after(gateup_got, keyval_grads)).reshape(n_dp, -1, 2 * part_wide)
    gateup_sum = lax.all_to_all(gateup_sum.astype(low), "dp", 0, 0, tiled=True)
    gateup_grad, gateup_second_out, gateup_weight_out = update_columns(
        gateup_sum, gateup_first, gateup_second, gateup_weight
    )
    key_grads, value_grads = keyval_grads[:, :kv_width], keyval_grads[:, kv_width:]
    key_grads = key_grads * cos_wide - swap(key_grads) * sin_wide
    grad_keyval_pre = jnp.concatenate([key_grads, value_grads], axis=1).astype(low)
    bias_term = jnp.concatenate(
        [
            jnp.sum(grad_query_pre.astype(wide), axis=0),
            jnp.sum(grad_keyval_pre.astype(wide), axis=0),
        ]
    )
    grad_normed_one = grad_normed_one + lax.dot_general(
        grad_keyval_pre, keyval_full, NT, preferred_element_type=wide
    )
    gain_scaled_one = grad_normed_one * gain_one
    gain_one_term = jnp.sum(grad_normed_one * scaled_one, axis=0)
    grad_input = grad_middle + inv_one * (
        gain_scaled_one - scaled_one * jnp.mean(gain_scaled_one * scaled_one, axis=1, keepdims=True)
    )
    tokens_grad = grad_input.astype(low)
    out_sum = jnp.concatenate([out_left, out_right], axis=1).astype(wide)
    layer_out = (middle + out_sum).astype(low)
    small_term = jnp.concatenate([gain_one_term, gain_two_term, bias_term])

    small_blocks = jnp.concatenate(
        [
            small_term.reshape(device_count, small_piece),
            small_term[:rest_length].reshape(device_count, rest_piece),
            small_term[rest_length:].reshape(device_count, value_piece),
        ],
        axis=1,
    )
    small_width = small_blocks.shape[1]
    small_two = jnp.stack(split_low(small_blocks)[:2], axis=1)
    small_two = jnp.pad(small_two, ((0, 0), (0, 0), (0, 2 * kv_width - small_width)))
    small_two = jnp.pad(small_two, ((0, 0), (in_rows, in_give - in_rows - 2), (0, 0)))
    last_terms = weight_gradient(
        normed_one, grad_keyval_pre, pieces, in_rows, device, split=True, extra=small_two
    )
    last_total = scatter_chips(*last_terms)
    some = last_total.shape[1] - both_total.shape[1]
    both_total = jnp.pad(both_total, ((0, 0), (0, some), (0, 0)))
    every_sum = add_up(group_send(jnp.concatenate([both_total, last_total], axis=2)))
    query_grad = every_sum[:in_rows, :query_width]
    output_grad = every_sum[:in_rows, query_width : query_width + D]
    last_sum = every_sum[:, query_width + D :]
    keyval_grad = last_sum[:in_rows]
    small_sum = last_sum[in_rows, :small_width] + last_sum[in_rows + 1, :small_width]
    small_grad = small_sum[:small_piece]
    rest_grad = small_sum[small_piece : small_piece + rest_piece]
    value_grad = small_sum[small_piece + rest_piece :]

    query_second_out, query_weight_out = adamw_step(
        query_grad, query_first, query_second, query_weight, rate_proj, decay_rate
    )
    keyval_second_out, keyval_weight_out = adamw_step(
        keyval_grad, keyval_first, keyval_second, keyval_weight, rate_proj, decay_rate
    )
    output_second_out, output_weight_out = adamw_step(
        output_grad, output_first, output_second, output_weight, rate_out, decay_rate
    )
    down_second_out, down_weight_out = adamw_step(
        down_grad, down_first, down_second, down_weight, rate_proj, decay_rate
    )
    _, small_weight_out = adamw_step(
        small_grad, small_first, small_second, small_weight, rate_small, 0.0
    )
    rest_second = lax.dynamic_slice_in_dim(
        small_second_all, flat_index * rest_piece, rest_piece, 0
    )
    value_second = lax.dynamic_slice_in_dim(
        small_second_all, rest_length + flat_index * value_piece, value_piece, 0
    )
    small_second_out = beta_two * rest_second + (1.0 - beta_two) * rest_grad * rest_grad
    value_bias_second_out = beta_two * value_second + (1.0 - beta_two) * value_grad * value_grad
    return (
        layer_out,
        tokens_grad,
        query_grad,
        query_second_out,
        query_weight_out,
        keyval_grad,
        keyval_second_out,
        keyval_weight_out,
        output_grad,
        output_second_out,
        output_weight_out,
        gateup_grad,
        gateup_second_out,
        gateup_weight_out,
        down_grad,
        down_second_out,
        down_weight_out,
        small_grad,
        small_second_out,
        value_bias_second_out,
        small_weight_out,
    )


def solution(mesh):
    rows = P(("dp", "group"), None)
    line = P(("dp", "group"))
    in_specs = (rows, P("dp", None)) + (rows,) * 16 + (line,) * 3
    out_specs = (rows,) * 17 + (line,) * 4
    return jax.shard_map(body, mesh=mesh, in_specs=in_specs, out_specs=out_specs, check_vma=False)
```

```python
import functools

import jax
import jax.numpy as jnp
from jax import lax
from jax.experimental import pallas as pl
from jax.experimental.pallas import tpu as pltpu
from jax.sharding import PartitionSpec as P

D = 896
HQ = 14
HK = 2
HD = 64
FF = 4864
STEP = 10


theta_base = 1000000.0
norm_eps = 1e-06
beta_one = 0.9
beta_two = 0.95
adam_eps = 1e-08
decay_rate = 0.1
rate_proj = 0.02
rate_out = 0.5
rate_small = 0.2
masked_score = -1e30

low = jnp.bfloat16
wide = jnp.float32


MIB = 1024 * 1024
LANES = 128
ROWS = 16
NT = (((1,), (1,)), ((), ()))
TN = (((0,), (0,)), ((), ()))


def padded(size, unit):
    return -(-size // unit) * unit


def rotary_angles(places):
    half_size = HD // 2
    inv_freq = theta_base ** (-(jnp.arange(half_size, dtype=wide) * 2.0) / HD)
    return places.astype(wide)[:, None] * inv_freq[None, :]


def adamw_step(gradient, first_old, second_old, weight, step_rate, decay_factor):
    first_new = beta_one * first_old + (1.0 - beta_one) * gradient
    second_new = beta_two * second_old + (1.0 - beta_two) * gradient * gradient
    first_hat = first_new / (1.0 - beta_one**STEP)
    second_hat = second_new / (1.0 - beta_two**STEP)
    updated = weight - step_rate * (
        first_hat / (jnp.sqrt(second_hat) + adam_eps) + decay_factor * weight
    )
    return (second_new, updated)


def params(limit=56):
    return pltpu.CompilerParams(
        vmem_limit_bytes=limit * MIB, dimension_semantics=("arbitrary",)
    )


def cost(micros):
    return pl.CostEstimate(flops=int(micros * 10**9), bytes_accessed=10**6, transcendentals=0)


def split_heads(pair, number):
    lane = lax.broadcasted_iota(jnp.int32, pair.shape, 1)
    zero = jnp.zeros_like(pair)
    turned = pltpu.roll(pair, HD, 1)
    low_a = 2 * number < HQ // HK
    low_b = 2 * number + 1 < HQ // HK
    first = jnp.where((lane < HD) == low_a, jnp.where(low_a, pair, turned), zero)
    second = jnp.where((lane < HD) == low_b, jnp.where(low_b, turned, pair), zero)
    return jnp.concatenate([first, second], axis=0)


def join_heads(both, number, half):
    low_a = 2 * number < HQ // HK
    low_b = 2 * number + 1 < HQ // HK
    first = jnp.where(low_a, both[:HD, :half], both[HD:, :half])
    second = jnp.where(low_b, both[:HD, half:], both[HD:, half:])
    return first, second


def key_mask(start, first_key, first_query, half, causal):
    key_row = lax.broadcasted_iota(jnp.int32, (half, half), 0)
    ok = key_row >= start - first_key
    if causal:
        ok &= key_row <= lax.broadcasted_iota(jnp.int32, (1, half), 1) + (first_query - first_key)
    return jnp.concatenate([ok, ok], axis=1)


def query_mask(start, first_key, first_query, half, causal):
    key = lax.broadcasted_iota(jnp.int32, (half, half), 1)
    ok = key >= jnp.concatenate([start - first_key] * (half // LANES), axis=1)
    if causal:
        ok &= key <= lax.broadcasted_iota(jnp.int32, (half, half), 0) + (first_query - first_key)
    return jnp.concatenate([ok, ok], axis=0)


def visit_blocks(meta, start_ref, half, pieces, visit):
    mine = meta[0]
    first_query = mine * 2 * half
    turned = start_ref.shape[2] == LANES
    mask_of = query_mask if turned else key_mask
    start_of = lambda sel: start_ref[sel] if turned else start_ref[sel, 0:1, :]
    for sel, block in ((0, 0), (1, 0), (1, 1)):
        mask = mask_of(
            start_of(sel), first_query + block * half, first_query + sel * half, half, sel == block
        )
        visit(sel, 0, block, mask)
    for piece in range(1, pieces):
        first_key = (mine - piece) * 2 * half

        def region(cut):
            for block in range(2):
                for sel in range(2):
                    if cut and block == 0:
                        mask = mask_of(start_of(sel), first_key, first_query, half, False)
                    else:
                        mask = start_of(sel) <= first_key + block * half
                        mask = jnp.concatenate([mask, mask], axis=0 if turned else 1)
                    visit(sel, piece, block, mask)

        pl.when(mine == piece)(functools.partial(region, True))
        pl.when(mine > piece)(functools.partial(region, False))


def forward_kernel(pieces, meta, pre_ref, cos_ref, sin_ref, start_ref, starts_ref, *refs):
    kv_refs = refs[:pieces]
    o_ref, lse_ref, q_ref, two_ref, top_ref, sum_ref, acc_ref = refs[pieces:]
    number = pl.program_id(0)
    rows = pre_ref.shape[0]
    half = rows // 2
    pre = pre_ref[...]
    lane = lax.broadcasted_iota(jnp.int32, pre.shape, 1)
    swapped = jnp.where(
        lane % HD < HD // 2, pltpu.roll(pre, LANES - HD // 2, 1), pltpu.roll(pre, HD // 2, 1)
    )
    turned = (pre * cos_ref[...] + swapped * sin_ref[...]).astype(low)
    turned = (turned.astype(wide) * (1.0 / HD**0.5)).astype(low)
    q_ref[...] = turned
    for which in range(2):
        two_ref[which] = split_heads(turned[which * half : (which + 1) * half, :], number)
    top_ref[...] = jnp.full_like(top_ref, masked_score)
    sum_ref[...] = jnp.zeros_like(sum_ref)
    acc_ref[...] = jnp.zeros_like(acc_ref)

    def scores_of(sel, piece, block):
        part = slice(block * half, (block + 1) * half)
        return lax.dot_general(
            two_ref[sel], kv_refs[piece][part, :LANES], NT, preferred_element_type=wide
        )

    def find_top(sel, piece, block, mask):
        scores = scores_of(sel, piece, block)
        if mask.shape[1] > LANES:
            scores = jnp.where(mask, scores, masked_score)
        peak = functools.reduce(jnp.maximum, [scores[:, i : i + LANES] for i in range(0, half, LANES)])
        if mask.shape[1] <= LANES:
            peak = jnp.where(mask, peak, masked_score)
        top_ref[sel] = jnp.maximum(top_ref[sel], peak)

    def sum_up(sel, piece, block, mask):
        part = slice(block * half, (block + 1) * half)
        scores = scores_of(sel, piece, block)
        level = top_ref[sel]
        if mask.shape[1] > LANES:
            scores = jnp.where(mask, scores, masked_score)
        else:
            level = jnp.where(mask, level, -masked_score)
        weights = [jnp.exp(scores[:, i : i + LANES] - level) for i in range(0, half, LANES)]
        sum_ref[sel] += functools.reduce(jnp.add, weights)
        acc_ref[sel] += jnp.dot(
            jnp.concatenate(weights, axis=1).astype(low),
            kv_refs[piece][part, LANES:],
            preferred_element_type=wide,
        )

    visit_blocks(meta, starts_ref, half, pieces, find_top)
    for which in range(2):
        top_ref[which] = jnp.broadcast_to(
            jnp.max(top_ref[which], axis=1, keepdims=True), top_ref.shape[1:]
        )
    visit_blocks(meta, starts_ref, half, pieces, sum_up)
    lane = lax.broadcasted_iota(jnp.int32, (half, LANES), 1)
    low_a = 2 * number < HQ // HK
    low_b = 2 * number + 1 < HQ // HK
    pick = jnp.where(lax.broadcasted_iota(jnp.int32, (8, LANES), 1) == 0, 1.0, 0.0).astype(wide)
    for which in range(2):
        total = jnp.sum(sum_ref[which], axis=1, keepdims=True)
        out = acc_ref[which] / total
        first, second = out[:half], out[half:]
        first = jnp.where(low_a, first, pltpu.roll(first, HD, 1))
        second = jnp.where(low_b, pltpu.roll(second, HD, 1), second)
        o_ref[which * half : (which + 1) * half, :] = jnp.where(lane < HD, first, second)
        lse = top_ref[which] + jnp.log(total)
        lse_ref[0, :, which * rows : (which + 1) * rows] = lax.dot_general(
            pick, lse, NT, precision=lax.Precision.HIGHEST, preferred_element_type=wide
        )


def attention_forward(pre, cos_wide, sin_wide, starts, kv_pieces, meta):
    rows, width = pre.shape
    pairs, pieces = width // LANES, len(kv_pieces)
    pair = pl.BlockSpec((rows, LANES), lambda p, m: (0, p))
    whole = lambda a: pl.BlockSpec(a.shape, lambda p, m: (0,) * a.ndim)
    starts_wide = jnp.broadcast_to(starts[:, 0, :, None], (2, rows // 2, LANES))
    operands = (cos_wide, sin_wide, starts, starts_wide, *kv_pieces)
    spec = pltpu.PrefetchScalarGridSpec(
        num_scalar_prefetch=1,
        grid=(pairs,),
        in_specs=[pair] + [whole(a) for a in operands],
        out_specs=[pair, pl.BlockSpec((1, 8, 2 * rows), lambda p, m: (p, 0, 0)), pair],
        scratch_shapes=[
            pltpu.VMEM((2, rows, LANES), low),
            pltpu.VMEM((2, rows, LANES), wide),
            pltpu.VMEM((2, rows, LANES), wide),
            pltpu.VMEM((2, rows, LANES), wide),
        ],
    )
    return pl.pallas_call(
        functools.partial(forward_kernel, pieces),
        grid_spec=spec,
        out_shape=[
            jax.ShapeDtypeStruct((rows, width), wide),
            jax.ShapeDtypeStruct((pairs, 8, 2 * rows), wide),
            jax.ShapeDtypeStruct((rows, width), low),
        ],
        compiler_params=params(48),
        cost_estimate=cost(40),
        name="attention_forward",
    )(meta, pre, *operands)


def backward_kernel(pieces, meta, q_ref, do_ref, o_ref, lse_ref, start_ref, cos_ref, sin_ref, *refs):
    kv_refs = refs[:pieces]
    dq_ref = refs[pieces]
    out_refs = refs[pieces + 1 : 2 * pieces + 1]
    kt_ref, two_ref, dot_ref, delta_ref, acc_ref, dkv_ref = refs[2 * pieces + 1 :]
    number = pl.program_id(0)
    rows = q_ref.shape[0]
    half = rows // 2

    @pl.when(number == 0)
    def _():
        dkv_ref[...] = jnp.zeros_like(dkv_ref)
        for piece in range(pieces):
            kt_ref[piece] = kv_refs[piece][:, :LANES].astype(wide).T.astype(low)

    acc_ref[...] = jnp.zeros_like(acc_ref)
    lane = lax.broadcasted_iota(jnp.int32, (8, LANES), 1)
    pick_a = jnp.where(lane < HD, 1.0, 0.0).astype(wide)
    pick_b = 1.0 - pick_a
    for which in range(2):
        part = slice(which * half, (which + 1) * half)
        two_ref[which] = split_heads(q_ref[part, :], number)
        dot_ref[which] = split_heads(do_ref[part, :], number)
        product = do_ref[part, :].astype(wide) * o_ref[part, :]
        delta_ref[which] = jnp.concatenate(
            [
                lax.dot_general(
                    pick, product, NT, precision=lax.Precision.HIGHEST, preferred_element_type=wide
                )
                for pick in (pick_a, pick_b)
            ],
            axis=1,
        )

    def visit(sel, piece, block, mask):
        part = slice(block * half, (block + 1) * half)
        two, dot = two_ref[sel], dot_ref[sel]
        keys, values = kv_refs[piece][part, :LANES], kv_refs[piece][part, LANES:]
        scores = lax.dot_general(keys, two, NT, preferred_element_type=wide)
        grad_weights = lax.dot_general(values, dot, NT, preferred_element_type=wide)
        lse = lse_ref[0, 0:1, sel * rows : (sel + 1) * rows]
        if mask.shape[0] > 1:
            weights = jnp.where(mask, jnp.exp(scores - lse), 0.0)
        else:
            weights = jnp.exp(scores - jnp.where(mask, lse, -masked_score))
        grad_scores = (weights * (grad_weights - delta_ref[sel, 0:1, :])).astype(low)
        dkv_ref[piece, part, LANES:] += jnp.dot(
            weights.astype(low), dot, preferred_element_type=wide
        )
        dkv_ref[piece, part, :LANES] += jnp.dot(grad_scores, two, preferred_element_type=wide)
        acc_ref[sel] += jnp.dot(kt_ref[piece, :, part], grad_scores, preferred_element_type=wide)

    visit_blocks(meta, start_ref, half, pieces, visit)
    for which in range(2):
        part = slice(which * half, (which + 1) * half)
        cos, sin = cos_ref[:, part], sin_ref[:, part]
        turned = []
        for head in join_heads(acc_ref[which] * (1.0 / HD**0.5), number, half):
            upper, lower = head[: HD // 2], head[HD // 2 :]
            turned += [upper * cos + lower * sin, lower * cos - upper * sin]
        dq_ref[part, :] = jnp.concatenate(turned, axis=0).T.astype(low)

    @pl.when(number == pl.num_programs(0) - 1)
    def _():
        for piece in range(pieces):
            out_refs[piece][...] = dkv_ref[piece].astype(out_refs[piece].dtype)


def attention_backward(q, do, o, lse, starts, cos_turned, sin_turned, kv_pieces, meta):
    rows, width = q.shape
    pairs, pieces = width // LANES, len(kv_pieces)
    pair = pl.BlockSpec((rows, LANES), lambda p, m: (0, p))
    whole = lambda a: pl.BlockSpec(a.shape, lambda p, m: (0,) * a.ndim)
    fixed = (starts, cos_turned, sin_turned, *kv_pieces)
    spec = pltpu.PrefetchScalarGridSpec(
        num_scalar_prefetch=1,
        grid=(pairs,),
        in_specs=[pair, pair, pair, pl.BlockSpec((1, 8, 2 * rows), lambda p, m: (p, 0, 0))]
        + [whole(a) for a in fixed],
        out_specs=[pair] + [whole(a) for a in kv_pieces],
        scratch_shapes=[
            pltpu.VMEM((pieces, LANES, rows), low),
            pltpu.VMEM((2, rows, LANES), low),
            pltpu.VMEM((2, rows, LANES), low),
            pltpu.VMEM((2, 8, rows), wide),
            pltpu.VMEM((2, LANES, rows), wide),
            pltpu.VMEM((pieces, rows, 2 * LANES), wide),
        ],
    )
    return pl.pallas_call(
        functools.partial(backward_kernel, pieces),
        grid_spec=spec,
        out_shape=[jax.ShapeDtypeStruct((rows, width), low)]
        + [
            jax.ShapeDtypeStruct((rows, 2 * LANES), wide if piece == 0 else low)
            for piece in range(pieces)
        ],
        compiler_params=params(48),
        cost_estimate=cost(40),
        name="attention_backward",
    )(meta, q, do, o, lse, *fixed)


def feed_kernel(
    steps, fresh, place, n_a, n_b, cot_ref, gateup_ref, down_ref, *refs
):
    refs = refs[0 if fresh else 4 :]
    back_a, back_b, out_ref, hidden_ref, grad_ref, kept_ref = refs
    width = down_ref.shape[0]
    first = pl.program_id(0) < steps // 2
    normed = jnp.where(first, n_a[...], n_b[...])
    cot = cot_ref[...]
    gate = jnp.dot(normed, gateup_ref[:, :width], preferred_element_type=wide)
    up = jnp.dot(normed, gateup_ref[:, width:], preferred_element_type=wide)
    grad_hidden = lax.dot_general(cot, down_ref[...], NT, preferred_element_type=wide)
    sigmoid = jax.nn.sigmoid(gate)
    act = gate * sigmoid
    hidden = (act * up).astype(low)
    grad_gate = (grad_hidden * up * sigmoid * (1.0 + gate * (1.0 - sigmoid))).astype(low)
    grad_up = (grad_hidden * act).astype(low)
    kept_ref[...] = normed
    hidden_ref[...] = hidden
    grad_ref[:, :width] = grad_gate
    grad_ref[:, width:] = grad_up
    out_ref[...] = jnp.dot(hidden, down_ref[...], preferred_element_type=wide).astype(low)
    back = lax.dot_general(grad_gate, gateup_ref[:, :width], NT, preferred_element_type=wide)
    back = back + lax.dot_general(grad_up, gateup_ref[:, width:], NT, preferred_element_type=wide)

    @pl.when(first)
    def _():
        back_a[...] = back.astype(low)

    @pl.when(jnp.logical_not(first))
    def _():
        back_b[...] = back.astype(low)


def feed_forward(n_a, n_b, cot_all, gateup, down, place, kept, block=256):
    rows, d = n_a.shape
    total, width = cot_all.shape[0], down.shape[0]
    block = min(block, rows)
    each = rows // block
    steps = 2 * each
    spot = lambda i, place: (place[i // each] * each + i % each, 0)
    whole = lambda a: pl.BlockSpec(a.shape, lambda i, place: (0, 0))
    halves = [
        pl.BlockSpec((block, d), lambda i, place: (jnp.minimum(i, each - 1), 0)),
        pl.BlockSpec((block, d), lambda i, place: (jnp.maximum(i - each, 0), 0)),
    ]
    in_specs = halves + [
        pl.BlockSpec((block, d), spot),
        whole(gateup),
        whole(down),
    ]
    fresh = kept is None
    if not fresh:
        in_specs += [pl.BlockSpec(memory_space=pl.ANY)] * 4
    spec = pltpu.PrefetchScalarGridSpec(
        num_scalar_prefetch=1,
        grid=(steps,),
        in_specs=in_specs,
        out_specs=halves
        + [pl.BlockSpec((block, n), spot) for n in (d, width, 2 * width, d)],
    )
    shapes = [(rows, d)] * 2 + [(total, n) for n in (d, width, 2 * width, d)]
    return pl.pallas_call(
        functools.partial(feed_kernel, steps, fresh),
        grid_spec=spec,
        out_shape=[jax.ShapeDtypeStruct(s, low) for s in shapes],
        input_output_aliases={} if fresh else {6 + i: 2 + i for i in range(4)},
        compiler_params=params(),
        cost_estimate=cost(15),
        name="feed_forward",
    )(place, n_a, n_b, cot_all, gateup, down, *(() if fresh else kept))


def weight_kernel(steps, shape, take, give, split, fill, where, x_ref, y_ref, *refs):
    outputs = 2 if split else 1
    acc_ref = refs[-1]
    out_refs = refs[-1 - outputs : -1]
    chips, cores, groups = shape
    step = pl.program_id(0)
    size = x_ref.shape[1]
    product = lax.dot_general(x_ref[...], y_ref[...], TN, preferred_element_type=wide)

    @pl.when(step == 0)
    def _():
        acc_ref[:size] = product
        acc_ref[size:] = jnp.zeros_like(acc_ref[size:])

    @pl.when(step > 0)
    def _():
        acc_ref[:size] += product

    keep = lax.broadcasted_iota(jnp.int32, (give, 1), 0) < take

    def write(mine):
        for chip in range(chips):
            for core in range(cores):
                for group in range(groups):
                    low_edge = ((chip * cores + core) * groups + group) * take
                    value = jnp.where(keep, acc_ref[low_edge : low_edge + give], 0.0)
                    if fill:
                        value += refs[0][low_edge // take].astype(wide)
                    value = value.astype(low)
                    at = lax.rem(group + groups - where[2], groups)
                    if split:
                        out_refs[core ^ mine][chip ^ where[1], at] = value
                    else:
                        row = (chip * cores + core) * give
                        out_refs[0][at, row : row + give] = value

    if split:
        for mine in range(cores):
            pl.when((step == steps - 1) & (where[0] == mine))(functools.partial(write, mine))
    else:
        pl.when(step == steps - 1)(functools.partial(write, 0))


def weight_gradient(
    x, y, shape, take, where, split=False, block=1024, column=0, columns=1, into=None, extra=None,
    micros=0.2,
):
    total, size = x.shape
    width = y.shape[1]
    give = padded(take, ROWS) if extra is None else extra.shape[1]
    block = min(block, total)
    steps = total // block
    chips, cores, groups = shape
    if split:
        out = pl.BlockSpec((chips, groups, give, width), lambda i, w: (0, 0, 0, column))
        shapes = [(chips, groups, give, columns * width)] * 2
    else:
        out = pl.BlockSpec((groups, chips * cores * give, width), lambda i, w: (0, 0, 0))
        shapes = [(groups, chips * cores * give, width)]
    fill = extra is not None
    into = [] if into is None else into
    return pl.pallas_call(
        functools.partial(weight_kernel, steps, shape, take, give, split, fill),
        grid_spec=pltpu.PrefetchScalarGridSpec(
            num_scalar_prefetch=1,
            grid=(steps,),
            in_specs=[
                pl.BlockSpec((block, size), lambda i, w: (i, 0)),
                pl.BlockSpec((block, width), lambda i, w: (i, 0)),
            ]
            + [pl.BlockSpec(extra.shape, lambda i, w: (0, 0, 0)) for _ in range(fill)]
            + [pl.BlockSpec(memory_space=pl.ANY)] * len(into),
            out_specs=[out] * len(shapes),
            scratch_shapes=[pltpu.VMEM((padded(size, 8) + give, width), wide)],
        ),
        out_shape=[jax.ShapeDtypeStruct(shape, low) for shape in shapes],
        input_output_aliases={3 + fill + i: i for i in range(len(into))},
        compiler_params=params(),
        cost_estimate=cost(micros),
        name="weight_gradient",
    )(where, x, y, *([extra] if fill else []), *into)


def finish_kernel(
    shape, take, give, cuts, pieces, where, normed_ref, scaled_ref, inv_ref, gain_ref, query_ref,
    query_weight_ref, middle_ref, weight_ref, cos_ref, sin_ref, small_ref, *refs
):
    got_refs = refs[:pieces]
    keep_ref, send_ref, out_ref, acc_ref, row_ref, cut_ref = refs[pieces:]
    chips, cores, groups = shape
    size = normed_ref.shape[1]
    total = got_refs[0][...]
    for ref in got_refs[1:]:
        total = total + ref[...].astype(wide)
    keys, values = total[:, :LANES], total[:, LANES:]
    lane = lax.broadcasted_iota(jnp.int32, keys.shape, 1)
    swapped = jnp.where(
        lane % HD < HD // 2, pltpu.roll(keys, LANES - HD // 2, 1), pltpu.roll(keys, HD // 2, 1)
    )
    keys = keys * cos_ref[...] - swapped * sin_ref[...]
    grads = jnp.concatenate([keys, values], axis=1).astype(low)
    acc_ref[:size] = lax.dot_general(
        normed_ref[...], grads, TN, preferred_element_type=wide
    )
    grad = lax.dot_general(
        query_ref[...], query_weight_ref[...], NT, preferred_element_type=wide
    ) + lax.dot_general(grads, weight_ref[...], NT, preferred_element_type=wide)
    scaled = scaled_ref[...]
    row_ref[:, :size] = jnp.sum(grad * scaled, axis=0, keepdims=True)
    row_ref[:, size : size + small_ref.shape[1]] = small_ref[...]
    row_ref[:, size + small_ref.shape[1] :] = jnp.sum(grads.astype(wide), axis=0, keepdims=True)
    grad = grad * gain_ref[...]
    mean = jnp.sum(grad * scaled, axis=1, keepdims=True) * (1.0 / size)
    out_ref[...] = (middle_ref[...] + inv_ref[...] * (grad - scaled * mean)).astype(low)
    cut_ref[...] = jnp.zeros_like(cut_ref)
    for i in range(chips * cores * groups):
        at = 0
        for first, width in cuts:
            begin = first + i * width
            cut_ref[i : i + 1, at : at + width] = row_ref[:, begin : begin + width]
            at += width
    high = cut_ref[...].astype(low).astype(wide)
    rest = cut_ref[...] - high
    row = lax.broadcasted_iota(jnp.int32, (give, 1), 0)

    def write(mine):
        for chip in range(chips):
            for core in range(cores):
                for group in range(groups):
                    i = (chip * cores + core) * groups + group
                    value = jnp.where(row < take, acc_ref[i * take : i * take + give], 0.0)
                    value = jnp.where(row == take, high[i : i + 1], value)
                    value = jnp.where(row == take + 1, rest[i : i + 1], value)
                    at = lax.rem(group + groups - where[2], groups)
                    target = send_ref if core ^ mine else keep_ref
                    target[chip ^ where[1], at] = value.astype(low)

    for mine in range(cores):
        pl.when(where[0] == mine)(functools.partial(write, mine))


def finish_keyval(shape, take, give, cuts, where, got, operands):
    chips, cores, groups = shape
    rows, size = operands[0].shape
    width = got[0].shape[1]
    total = size + operands[10].shape[1] + width
    whole = lambda a: pl.BlockSpec(a.shape, lambda i, w: (0,) * a.ndim)
    pieces = pl.BlockSpec((chips, groups, give, width), lambda i, w: (0, 0, 0, 0))
    return pl.pallas_call(
        functools.partial(finish_kernel, shape, take, give, cuts, len(got)),
        grid_spec=pltpu.PrefetchScalarGridSpec(
            num_scalar_prefetch=1,
            grid=(1,),
            in_specs=[whole(a) for a in (*operands, *got)],
            out_specs=[pieces, pieces, pl.BlockSpec((rows, size), lambda i, w: (0, 0))],
            scratch_shapes=[
                pltpu.VMEM((padded(size, 8) + give, width), wide),
                pltpu.VMEM((1, total), wide),
                pltpu.VMEM((padded(chips * cores * groups, 8), width), wide),
            ],
        ),
        out_shape=[jax.ShapeDtypeStruct((chips, groups, give, width), low)] * 2
        + [jax.ShapeDtypeStruct((rows, size), low)],
        compiler_params=params(),
        cost_estimate=cost(20),
        name="finish_keyval",
    )(where, *operands, *got)


def assemble_kernel(
    n_dp, n_group, take, give, meta, own_ref, other_ref, o_ref, small_ref, at_ref, acc_ref
):
    me, mine = meta[0], meta[1]
    for r in range(n_dp):
        source = own_ref if r % 2 == 0 else other_ref
        for s in range(n_group):
            row = (r // 2 * n_group + s) * give
            z = lax.rem(mine + s, n_group)
            at_ref[(me ^ r) * n_group + z] = source[row : row + give].astype(wide)
    for i in range(n_dp * n_group):
        acc_ref[i * take : i * take + give] = at_ref[i]
        for j in range(2):
            small_ref[j, i : i + 1] = at_ref[i, take + j : take + j + 1]
    size = o_ref.shape[0]
    o_ref[...] = acc_ref[:size].astype(low)


def assemble(own, other, n_dp, n_group, take, give, me, mine, column, width):
    size = n_dp * n_group * take
    return pl.pallas_call(
        functools.partial(assemble_kernel, n_dp, n_group, take, give),
        grid_spec=pltpu.PrefetchScalarGridSpec(
            num_scalar_prefetch=1,
            grid=(1,),
            in_specs=[pl.BlockSpec((own.shape[0], width), lambda i, m: (0, column))] * 2,
            out_specs=[
                pl.BlockSpec((size, width), lambda i, m: (0, 0)),
                pl.BlockSpec((2, n_dp * n_group, width), lambda i, m: (0, 0, 0)),
            ],
            scratch_shapes=[
                pltpu.VMEM((n_dp * n_group, give, width), wide),
                pltpu.VMEM((size + give, width), wide),
            ],
        ),
        out_shape=[
            jax.ShapeDtypeStruct((size, width), low),
            jax.ShapeDtypeStruct((2, n_dp * n_group, width), wide),
        ],
        compiler_params=params(),
        cost_estimate=cost(1),
        name="assemble_rows",
    )(jnp.stack([me, mine]).astype(jnp.int32), own, other)


def sum_kernel(*refs):
    total = refs[0][...].astype(wide)
    for ref in refs[1:-1]:
        total = total + ref[...].astype(wide)
    refs[-1][...] = total.astype(low)


def sum_pieces(pieces):
    rows, width = pieces[0].shape
    block = rows // 2
    spec = pl.BlockSpec((block, width), lambda i: (i, 0))
    return pl.pallas_call(
        sum_kernel,
        grid=(2,),
        in_specs=[spec] * len(pieces),
        out_specs=spec,
        out_shape=jax.ShapeDtypeStruct((rows, width), low),
        compiler_params=params(),
        cost_estimate=cost(0.1),
        name="sum_pieces",
    )(*pieces)


def stack_kernel(outer, count, take, give, meta, *refs):
    o_ref, at_ref, acc_ref = refs[count:]
    for s in range(count):
        z = lax.rem(meta[0] + s, count)
        for i in range(outer):
            at_ref[i * count + z] = refs[s][i * give : (i + 1) * give].astype(wide)
    for i in range(outer * count):
        acc_ref[i * take : i * take + give] = at_ref[i]
    size = outer * count * take
    o_ref[:size] = acc_ref[:size].astype(low)
    if o_ref.shape[0] > size:
        o_ref[size:] = jnp.zeros_like(o_ref[size:])


def stack_rows(pieces, outer, take, me, rows):
    count, width = len(pieces), pieces[0].shape[1]
    give = pieces[0].shape[0] // outer
    whole = lambda r: pl.BlockSpec((r, width), lambda i, m: (0, 0))
    return pl.pallas_call(
        functools.partial(stack_kernel, outer, count, take, give),
        grid_spec=pltpu.PrefetchScalarGridSpec(
            num_scalar_prefetch=1,
            grid=(1,),
            in_specs=[whole(outer * give)] * count,
            out_specs=whole(rows),
            scratch_shapes=[
                pltpu.VMEM((outer * count, give, width), wide),
                pltpu.VMEM((padded(outer * count * take, 8) + give, width), wide),
            ],
        ),
        out_shape=jax.ShapeDtypeStruct((rows, width), low),
        compiler_params=params(),
        cost_estimate=cost(1),
        name="stack_rows",
    )(me, *pieces)


def cut_kernel(count, part, part_wide, w_ref, o_ref, buffer_ref):
    rows = w_ref.shape[0]
    buffer_ref[...] = jnp.zeros_like(buffer_ref)
    for p in range(count):
        for j in range(2):
            column = (j * count + p) * part
            buffer_ref[:rows, j * part_wide : j * part_wide + part] = w_ref[
                :, column : column + part
            ]
        o_ref[p] = buffer_ref[...].astype(low)


def cut_columns(weight, count, part_wide, give):
    rows, width = weight.shape
    part = width // (2 * count)
    shape = (count, give, 2 * part_wide)
    return pl.pallas_call(
        functools.partial(cut_kernel, count, part, part_wide),
        grid=(1,),
        in_specs=[pl.BlockSpec(weight.shape, lambda i: (0, 0))],
        out_specs=pl.BlockSpec(shape, lambda i: (0, 0, 0)),
        out_shape=jax.ShapeDtypeStruct(shape, low),
        scratch_shapes=[pltpu.VMEM((give, 2 * part_wide), wide)],
        compiler_params=params(),
        cost_estimate=cost(1),
        name="cut_columns",
    )(weight)


def update_kernel(count, part, part_wide, g_ref, m_ref, v_ref, w_ref, go_ref, vo_ref, wo_ref):
    rows = w_ref.shape[0]
    for p in range(count):
        piece = g_ref[p].astype(wide)
        for j in range(2):
            column = (j * count + p) * part
            go_ref[:, column : column + part] = piece[
                :rows, j * part_wide : j * part_wide + part
            ]
    vo_ref[...], wo_ref[...] = adamw_step(
        go_ref[...], m_ref[...], v_ref[...], w_ref[...], rate_proj, decay_rate
    )


def update_columns(pieces, first, second, weight):
    count, _, width = pieces.shape
    spec = pl.BlockSpec(weight.shape, lambda i: (0, 0))
    return pl.pallas_call(
        functools.partial(
            update_kernel, count, weight.shape[1] // (2 * count), width // 2
        ),
        grid=(1,),
        in_specs=[pl.BlockSpec(pieces.shape, lambda i: (0, 0, 0))] + [spec] * 3,
        out_specs=[spec] * 3,
        out_shape=[jax.ShapeDtypeStruct(weight.shape, wide)] * 3,
        compiler_params=params(),
        cost_estimate=cost(1),
        name="update_columns",
    )(pieces, first, second, weight)


def flip(value, mask):
    count = lax.axis_size("dp")
    return lax.ppermute(value, "dp", [(i, i ^ mask) for i in range(count)])


def shift(value, step):
    count = lax.axis_size("group")
    return lax.ppermute(value, "group", [((i + step) % count, i) for i in range(count)])


def shift_within(value, step):
    count = lax.axis_size("group")
    pairs = [(i + step, i) for i in range(count) if 0 <= i + step < count]
    return lax.ppermute(value, "group", pairs)


def after(value, *others):
    return lax.optimization_barrier((value, *others))[0]


def group_pieces(block, steps=None):
    return [block] + [shift(block, s) for s in range(1, lax.axis_size("group"))]


def group_send(blocks):
    count = lax.axis_size("group")
    return [blocks[0]] + [shift(blocks[count - s].astype(low), s) for s in range(1, count)]


def add_up(terms):
    return functools.reduce(jnp.add, [term.astype(wide) for term in terms])


def gather_chips(column):
    evens = [column] + [flip(column, r) for r in range(2, lax.axis_size("dp"), 2)]
    return jnp.concatenate(evens, axis=0)


def gather_rows(own, other, take, column=0, columns=1):
    n_dp, n_group = lax.axis_size("dp"), lax.axis_size("group")
    give = own.shape[0] // (n_dp // 2 * n_group)
    return assemble(
        own, other, n_dp, n_group, take, give, lax.axis_index("dp"), lax.axis_index("group"),
        column, own.shape[1] // columns,
    )


def scatter_pair(keep, send):
    return keep.astype(wide) + flip(send, 1).astype(wide)


def scatter_chips(pair):
    got = [flip(pair[r].astype(low), 2 * r) for r in range(1, pair.shape[0])]
    return add_up([pair[0]] + got)


def split_low(value):
    first = lax.reduce_precision(value, 8, 7)
    rest = value - first
    second = lax.reduce_precision(rest, 8, 7)
    return [first.astype(low), second.astype(low), (rest - second).astype(low)]


def body(
    tokens,
    positions,
    cotangent,
    query_weight,
    query_first,
    query_second,
    keyval_weight,
    keyval_first,
    keyval_second,
    output_weight,
    output_first,
    output_second,
    gateup_weight,
    gateup_first,
    gateup_second,
    down_weight,
    down_first,
    down_second,
    small_weight,
    small_first,
    small_second,
):
    row_count = tokens.shape[0]
    half = row_count // 2
    n_dp = lax.axis_size("dp")
    group_size = lax.axis_size("group")
    device_count = n_dp * group_size
    my_dp = lax.axis_index("dp")
    my_index = lax.axis_index("group")
    flat_index = my_dp * group_size + my_index
    seq_len = row_count * group_size
    query_width = HQ * HD
    kv_width = HK * HD
    small_size = 2 * D + query_width + 2 * kv_width
    rest_length = small_size - kv_width
    rest_piece = rest_length // device_count
    value_piece = kv_width // device_count
    small_piece = small_size // device_count
    part = FF // n_dp
    part_wide = padded(part, LANES)
    in_rows = query_weight.shape[0]
    in_give = padded(in_rows + 2, ROWS)
    down_rows = down_weight.shape[0]

    small_rows = [small_weight.astype(low)] + split_low(small_second)
    small_rows = jnp.concatenate(small_rows).reshape(2, 2 * small_piece)
    small_rows = jnp.pad(small_rows, ((0, 0), (0, 2 * kv_width - 2 * small_piece)))
    keyval_block = jnp.concatenate([keyval_weight.astype(low), small_rows], axis=0)
    keyval_block = jnp.pad(keyval_block, ((0, in_give - in_rows - 2), (0, 0)))
    both_block = jnp.concatenate([query_weight.astype(low), output_weight.astype(low)], axis=1)
    both_block = jnp.pad(both_block, ((0, in_give - in_rows), (0, 0)))
    gateup_pieces = cut_columns(gateup_weight, n_dp, part_wide, in_give)
    every_pieces = group_pieces(jnp.concatenate([keyval_block, both_block], axis=1))
    every_column = jnp.concatenate(after(every_pieces, gateup_pieces), axis=0)
    keyval_column = every_column[:, : 2 * kv_width]
    both_column = every_column[:, 2 * kv_width :]
    keyval_own = gather_chips(keyval_column)
    keyval_full, small_all = gather_rows(
        keyval_own, flip(keyval_own, 1), in_rows
    )
    small_all = small_all[:, :, : 2 * small_piece].reshape(2, device_count, 2, small_piece)
    small_values = small_all[0, :, 0].reshape(small_size)
    small_second_all = (small_all[0, :, 1] + small_all[1, :, 0] + small_all[1, :, 1]).reshape(
        small_size
    )

    down_part = lax.all_gather(down_weight.astype(low), "group", axis=0, tiled=True)
    down_part = jnp.pad(down_part, ((0, part_wide - part), (0, 0)))
    me_group = my_index.astype(jnp.int32)[None]

    gain_one = small_values[:D]
    gain_two = small_values[D : 2 * D]
    bias_qkv = small_values[2 * D :]
    place_row = positions[0]
    local_index = my_index * row_count + jnp.arange(row_count, dtype=jnp.int32)
    local_places = lax.dynamic_slice_in_dim(place_row, my_index * row_count, row_count, 0)
    starts = (local_index - local_places).reshape(2, half).astype(jnp.int32)
    starts = jnp.broadcast_to(starts[:, None, :], (2, 8, half))
    meta = jnp.stack([my_index, my_index]).astype(jnp.int32)
    angles = rotary_angles(local_places)
    cosine, sine_table = jnp.cos(angles), jnp.sin(angles)
    cos_wide = jnp.concatenate([cosine] * 4, axis=1)
    sin_wide = jnp.concatenate([-sine_table, sine_table] * 2, axis=1)

    def swap(values):
        quarter = HD // 2
        pieces = [values[:, i * quarter : (i + 1) * quarter] for i in range(2 * HK)]
        return jnp.concatenate([pieces[i ^ 1] for i in range(2 * HK)], axis=1)

    act_in = tokens.astype(wide)
    inv_one = lax.rsqrt(jnp.mean(act_in * act_in, axis=1, keepdims=True) + norm_eps)
    scaled_one = act_in * inv_one
    normed_one = (scaled_one * gain_one).astype(low)
    keyval_pre = (
        jnp.dot(normed_one, keyval_full, preferred_element_type=wide) + bias_qkv[query_width:]
    )
    key_pre = keyval_pre[:, :kv_width]
    key_low = (key_pre * cos_wide + swap(key_pre) * sin_wide).astype(low)
    keyval_low = jnp.concatenate([key_low, keyval_pre[:, kv_width:].astype(low)], axis=1)
    keyval_parts = [keyval_low] + [shift_within(keyval_low, -s) for s in range(1, group_size)]
    both_own = gather_chips(after(both_column, keyval_low))
    gateup_column = lax.all_to_all(after(gateup_pieces, keyval_low), "dp", 0, 0, tiled=True)
    gateup_column = gateup_column.reshape(n_dp * in_give, 2 * part_wide)
    both_own, keyval_parts, gateup_column, down_part = after(
        (both_own, keyval_parts, gateup_column, down_part)
    )
    cot_all = lax.all_gather(after(cotangent, both_own), "dp", axis=0, tiled=True)
    both_other = flip(both_own, 1)
    query_full, _ = gather_rows(both_own, both_other, in_rows, 0, 2)
    output_full, _ = gather_rows(both_own, both_other, in_rows, 1, 2)
    query_pre = (
        jnp.dot(normed_one, query_full, preferred_element_type=wide) + bias_qkv[:query_width]
    )
    gateup_pieces = group_pieces(gateup_column)
    attn_float, log_total, query_low = attention_forward(
        query_pre, cos_wide, sin_wide, starts, keyval_parts, meta
    )
    attn_float = after(attn_float, gateup_pieces)
    attn_low = attn_float.astype(low)
    middle = act_in + jnp.dot(attn_low, output_full, preferred_element_type=wide)
    inv_two = lax.rsqrt(jnp.mean(middle * middle, axis=1, keepdims=True) + norm_eps)
    scaled_two = middle * inv_two
    normed_two = (scaled_two * gain_two).astype(low)

    gateup_pieces = after(gateup_pieces, normed_two)
    gateup_part = stack_rows(gateup_pieces, n_dp, in_rows, me_group, D)
    chips = n_dp // 2
    pieces, down_shape = (chips, 2, group_size), (1, 1, group_size)
    device = jnp.stack([my_dp & 1, my_dp >> 1, my_index]).astype(jnp.int32)
    kept, sides, back = None, {0: normed_two}, {}
    for k in range(1, chips):
        if n_dp != 8 or k != 3:
            sides[k] = flip(normed_two, 2 * k)

    def visit(k, kept):
        place = jnp.stack([my_dp ^ (2 * k), my_dp ^ (2 * k + 1)]).astype(jnp.int32)
        back_a, back_b, *kept = feed_forward(
            sides[k], flip(sides[k], 1), cot_all, gateup_part, down_part, place, kept
        )
        back[k] = (back_a, flip(back_b, 1))
        return kept

    if n_dp == 8:
        kept = visit(0, kept)
        sides[1], sides[2] = after((sides[1], sides[2]), kept)
        across = [flip(sides[1][:half], 4), flip(sides[2][half:], 2)]
        kept = visit(1, kept)
        sides[3] = jnp.concatenate(after(across, kept), axis=0)
        kept = visit(3, kept)
        corner = add_up(back[3]).astype(low)
        across = [flip(corner[:half], 2), flip(corner[half:], 4)]
        kept = visit(2, kept)
        (down_term,) = weight_gradient(kept[1], cot_all, down_shape, down_rows, device)
        across = after(across, down_term)
        nothing = jnp.zeros_like(across[0])
        x_sum = add_up([*back[1], jnp.concatenate([nothing, across[1]], axis=0)]).astype(low)
        y_sum = add_up([*back[2], jnp.concatenate([across[0], nothing], axis=0)]).astype(low)
        kept, y_sum = after((kept, y_sum))
        returned = [*back[0], flip(x_sum, 2), flip(y_sum, 4)]
    else:
        for k in range(chips):
            kept = visit(k, kept)
        (down_term,) = weight_gradient(kept[1], cot_all, down_shape, down_rows, device)
        returned = list(back[0])
        returned += [flip(add_up(back[k]).astype(low), 2 * k) for k in range(1, chips)]
    out_all, _, gate_all, normed_all = kept
    down_got = group_send(down_term)
    (gateup_term,) = weight_gradient(normed_all, gate_all, pieces, in_rows, device)
    gateup_got = group_send(gateup_term)
    returned, gateup_got[0], down_got = after((returned, gateup_got[0], down_got))
    grad_normed_two = add_up(returned)
    out_sum = lax.psum_scatter(after(out_all, returned), "dp", scatter_dimension=0, tiled=True)

    grad_out = cotangent.astype(wide)
    gain_scaled_two = grad_normed_two * gain_two
    gain_two_term = jnp.sum(grad_normed_two * scaled_two, axis=0)
    grad_middle = grad_out + inv_two * (
        gain_scaled_two - scaled_two * jnp.mean(gain_scaled_two * scaled_two, axis=1, keepdims=True)
    )
    grad_middle_low = grad_middle.astype(low)
    grad_attn_low = lax.dot_general(
        grad_middle_low, output_full, NT, preferred_element_type=wide
    ).astype(low)
    both_terms = weight_gradient(
        attn_low, grad_middle_low, pieces, in_rows, device, split=True, column=1, columns=2
    )
    grad_attn_low = after(grad_attn_low, both_terms)
    grad_query_pre, *keyval_terms = attention_backward(
        query_low,
        grad_attn_low,
        attn_float,
        log_total,
        starts,
        cosine.T,
        sine_table.T,
        keyval_parts,
        meta,
    )
    grad_query_pre, keyval_terms = after(
        (grad_query_pre, keyval_terms), gateup_got
    )
    keyval_got = [keyval_terms[0]]
    keyval_got += [shift_within(keyval_terms[s], s) for s in range(1, group_size)]
    both_terms = weight_gradient(
        normed_one, grad_query_pre, pieces, in_rows, device, split=True, columns=2, into=both_terms
    )
    both_pair = scatter_pair(both_terms[0], after(both_terms[1], keyval_got, out_sum))
    both_total = scatter_chips(both_pair)
    keyval_got = after(keyval_got, both_pair)
    bias_term = jnp.sum(grad_query_pre.astype(wide), axis=0)
    *last_terms, tokens_grad = finish_keyval(
        pieces,
        in_rows,
        in_give,
        ((0, small_piece), (0, rest_piece), (rest_length, value_piece)),
        device,
        keyval_got,
        (
            normed_one,
            scaled_one,
            inv_one,
            gain_one[None],
            grad_query_pre,
            query_full,
            grad_middle,
            keyval_full,
            cos_wide,
            sin_wide,
            jnp.concatenate([gain_two_term, bias_term])[None],
        ),
    )
    small_width = small_piece + rest_piece + value_piece
    gateup_sum = sum_pieces(after(gateup_got, last_terms)).reshape(n_dp, -1, 2 * part_wide)
    gateup_sum = lax.all_to_all(gateup_sum, "dp", 0, 0, tiled=True)
    last_terms, gateup_sum = after((last_terms, gateup_sum), both_total)
    last_total = scatter_chips(scatter_pair(*last_terms))
    down_got = after(down_got, last_total)
    late_middle, out_sum = after((middle, out_sum), last_total)
    layer_out = (late_middle + out_sum.astype(wide)).astype(low)
    down_grad = add_up(down_got)[:down_rows]
    gateup_grad, gateup_second_out, gateup_weight_out = update_columns(
        gateup_sum, gateup_first, gateup_second, gateup_weight
    )
    some = last_total.shape[1] - both_total.shape[1]
    both_total = jnp.pad(both_total, ((0, 0), (0, some), (0, 0)))
    down_second_out, down_weight_out = adamw_step(
        down_grad, down_first, down_second, down_weight, rate_proj, decay_rate
    )
    every_got = group_send(jnp.concatenate([both_total, last_total], axis=2))
    every_got, gateup_second_out, down_second_out, layer_out = after(
        (every_got, gateup_second_out, down_second_out, layer_out)
    )
    every_sum = add_up(every_got)
    query_grad = every_sum[:in_rows, :query_width]
    output_grad = every_sum[:in_rows, query_width : query_width + D]
    last_sum = every_sum[:, query_width + D :]
    keyval_grad = last_sum[:in_rows]
    small_sum = last_sum[in_rows, :small_width] + last_sum[in_rows + 1, :small_width]
    small_grad = small_sum[:small_piece]
    rest_grad = small_sum[small_piece : small_piece + rest_piece]
    value_grad = small_sum[small_piece + rest_piece :]

    query_second_out, query_weight_out = adamw_step(
        query_grad, query_first, query_second, query_weight, rate_proj, decay_rate
    )
    keyval_second_out, keyval_weight_out = adamw_step(
        keyval_grad, keyval_first, keyval_second, keyval_weight, rate_proj, decay_rate
    )
    output_second_out, output_weight_out = adamw_step(
        output_grad, output_first, output_second, output_weight, rate_out, decay_rate
    )
    _, small_weight_out = adamw_step(
        small_grad, small_first, small_second, small_weight, rate_small, 0.0
    )
    rest_second = lax.dynamic_slice_in_dim(
        small_second_all, flat_index * rest_piece, rest_piece, 0
    )
    value_second = lax.dynamic_slice_in_dim(
        small_second_all, rest_length + flat_index * value_piece, value_piece, 0
    )
    small_second_out = beta_two * rest_second + (1.0 - beta_two) * rest_grad * rest_grad
    value_bias_second_out = beta_two * value_second + (1.0 - beta_two) * value_grad * value_grad
    return (
        layer_out,
        tokens_grad,
        query_grad,
        query_second_out,
        query_weight_out,
        keyval_grad,
        keyval_second_out,
        keyval_weight_out,
        output_grad,
        output_second_out,
        output_weight_out,
        gateup_grad,
        gateup_second_out,
        gateup_weight_out,
        down_grad,
        down_second_out,
        down_weight_out,
        small_grad,
        small_second_out,
        value_bias_second_out,
        small_weight_out,
    )


def solution(mesh):
    rows = P(("dp", "group"), None)
    line = P(("dp", "group"))
    in_specs = (rows, P("dp", None)) + (rows,) * 16 + (line,) * 3
    out_specs = (rows,) * 17 + (line,) * 4
    return jax.shard_map(body, mesh=mesh, in_specs=in_specs, out_specs=out_specs, check_vma=False)
```

```python
import functools

import jax
import jax.numpy as jnp
from jax import lax
from jax.experimental import pallas as pl
from jax.experimental.pallas import tpu as pltpu
from jax.sharding import PartitionSpec as P

D = 896
HQ = 14
HK = 2
HD = 64
FF = 4864
STEP = 10


theta_base = 1000000.0
norm_eps = 1e-06
beta_one = 0.9
beta_two = 0.95
adam_eps = 1e-08
decay_rate = 0.1
rate_proj = 0.02
rate_out = 0.5
rate_small = 0.2
masked_score = -1e30

low = jnp.bfloat16
wide = jnp.float32


MIB = 1024 * 1024
LANES = 128
ROWS = 16
NT = (((1,), (1,)), ((), ()))
TN = (((0,), (0,)), ((), ()))


def padded(size, unit):
    return -(-size // unit) * unit


def rotary_angles(places):
    half_size = HD // 2
    inv_freq = theta_base ** (-(jnp.arange(half_size, dtype=wide) * 2.0) / HD)
    return places.astype(wide)[:, None] * inv_freq[None, :]


def adamw_step(gradient, first_old, second_old, weight, step_rate, decay_factor):
    first_new = beta_one * first_old + (1.0 - beta_one) * gradient
    second_new = beta_two * second_old + (1.0 - beta_two) * gradient * gradient
    first_hat = first_new / (1.0 - beta_one**STEP)
    second_hat = second_new / (1.0 - beta_two**STEP)
    updated = weight - step_rate * (
        first_hat / (jnp.sqrt(second_hat) + adam_eps) + decay_factor * weight
    )
    return (second_new, updated)


def params(limit=56):
    return pltpu.CompilerParams(
        vmem_limit_bytes=limit * MIB, dimension_semantics=("arbitrary",)
    )


def cost(micros):
    return pl.CostEstimate(flops=int(micros * 10**9), bytes_accessed=10**6, transcendentals=0)


def split_heads(pair, number):
    lane = lax.broadcasted_iota(jnp.int32, pair.shape, 1)
    zero = jnp.zeros_like(pair)
    turned = pltpu.roll(pair, HD, 1)
    low_a = 2 * number < HQ // HK
    low_b = 2 * number + 1 < HQ // HK
    first = jnp.where((lane < HD) == low_a, jnp.where(low_a, pair, turned), zero)
    second = jnp.where((lane < HD) == low_b, jnp.where(low_b, turned, pair), zero)
    return jnp.concatenate([first, second], axis=0)


def join_heads(both, number, half):
    low_a = 2 * number < HQ // HK
    low_b = 2 * number + 1 < HQ // HK
    first = jnp.where(low_a, both[:HD, :half], both[HD:, :half])
    second = jnp.where(low_b, both[:HD, half:], both[HD:, half:])
    return first, second


def key_mask(start, first_key, first_query, half, causal):
    key_row = lax.broadcasted_iota(jnp.int32, (half, half), 0)
    ok = key_row >= start - first_key
    if causal:
        ok &= key_row <= lax.broadcasted_iota(jnp.int32, (1, half), 1) + (first_query - first_key)
    return jnp.concatenate([ok, ok], axis=1)


def query_mask(start, first_key, first_query, half, causal):
    key = lax.broadcasted_iota(jnp.int32, (half, half), 1)
    ok = key >= jnp.concatenate([start - first_key] * (half // LANES), axis=1)
    if causal:
        ok &= key <= lax.broadcasted_iota(jnp.int32, (half, half), 0) + (first_query - first_key)
    return jnp.concatenate([ok, ok], axis=0)


def visit_blocks(meta, start_ref, half, pieces, visit):
    mine = meta[2]
    first_query = mine * 2 * half
    turned = start_ref.shape[2] == LANES
    mask_of = query_mask if turned else key_mask
    start_of = lambda sel: start_ref[sel] if turned else start_ref[sel, 0:1, :]
    for sel, block in ((0, 0), (1, 0), (1, 1)):
        mask = mask_of(
            start_of(sel), first_query + block * half, first_query + sel * half, half, sel == block
        )
        visit(sel, 0, block, mask)
    for piece in range(1, pieces):
        first_key = (mine - piece) * 2 * half

        def region(cut):
            for block in range(2):
                for sel in range(2):
                    if cut and block == 0:
                        mask = mask_of(start_of(sel), first_key, first_query, half, False)
                    else:
                        mask = start_of(sel) <= first_key + block * half
                        mask = jnp.concatenate([mask, mask], axis=0 if turned else 1)
                    visit(sel, piece, block, mask)

        pl.when(mine == piece)(functools.partial(region, True))
        pl.when(mine > piece)(functools.partial(region, False))


def forward_kernel(pieces, meta, pre_ref, cos_ref, sin_ref, start_ref, starts_ref, *refs):
    kv_refs = refs[:pieces]
    o_ref, lse_ref, q_ref, two_ref, top_ref, sum_ref, acc_ref = refs[pieces:]
    number = pl.program_id(0)
    rows = pre_ref.shape[0]
    half = rows // 2
    pre = pre_ref[...]
    lane = lax.broadcasted_iota(jnp.int32, pre.shape, 1)
    swapped = jnp.where(
        lane % HD < HD // 2, pltpu.roll(pre, LANES - HD // 2, 1), pltpu.roll(pre, HD // 2, 1)
    )
    turned = (pre * cos_ref[...] + swapped * sin_ref[...]).astype(low)
    turned = (turned.astype(wide) * (1.0 / HD**0.5)).astype(low)
    q_ref[...] = turned
    for which in range(2):
        two_ref[which] = split_heads(turned[which * half : (which + 1) * half, :], number)
    top_ref[...] = jnp.full_like(top_ref, masked_score)
    sum_ref[...] = jnp.zeros_like(sum_ref)
    acc_ref[...] = jnp.zeros_like(acc_ref)

    def scores_of(sel, piece, block):
        part = slice(block * half, (block + 1) * half)
        return lax.dot_general(
            two_ref[sel], kv_refs[piece][part, :LANES], NT, preferred_element_type=wide
        )

    def find_top(sel, piece, block, mask):
        scores = scores_of(sel, piece, block)
        if mask.shape[1] > LANES:
            scores = jnp.where(mask, scores, masked_score)
        peak = functools.reduce(jnp.maximum, [scores[:, i : i + LANES] for i in range(0, half, LANES)])
        if mask.shape[1] <= LANES:
            peak = jnp.where(mask, peak, masked_score)
        top_ref[sel] = jnp.maximum(top_ref[sel], peak)

    def sum_up(sel, piece, block, mask):
        part = slice(block * half, (block + 1) * half)
        scores = scores_of(sel, piece, block)
        level = top_ref[sel]
        if mask.shape[1] > LANES:
            scores = jnp.where(mask, scores, masked_score)
        else:
            level = jnp.where(mask, level, -masked_score)
        weights = [jnp.exp(scores[:, i : i + LANES] - level) for i in range(0, half, LANES)]
        sum_ref[sel] += functools.reduce(jnp.add, weights)
        acc_ref[sel] += jnp.dot(
            jnp.concatenate(weights, axis=1).astype(low),
            kv_refs[piece][part, LANES:],
            preferred_element_type=wide,
        )

    visit_blocks(meta, starts_ref, half, pieces, find_top)
    for which in range(2):
        top_ref[which] = jnp.broadcast_to(
            jnp.max(top_ref[which], axis=1, keepdims=True), top_ref.shape[1:]
        )
    visit_blocks(meta, starts_ref, half, pieces, sum_up)
    lane = lax.broadcasted_iota(jnp.int32, (half, LANES), 1)
    low_a = 2 * number < HQ // HK
    low_b = 2 * number + 1 < HQ // HK
    pick = jnp.where(lax.broadcasted_iota(jnp.int32, (8, LANES), 1) == 0, 1.0, 0.0).astype(wide)
    for which in range(2):
        total = jnp.sum(sum_ref[which], axis=1, keepdims=True)
        out = acc_ref[which] / total
        first, second = out[:half], out[half:]
        first = jnp.where(low_a, first, pltpu.roll(first, HD, 1))
        second = jnp.where(low_b, pltpu.roll(second, HD, 1), second)
        o_ref[which * half : (which + 1) * half, :] = jnp.where(lane < HD, first, second)
        lse = top_ref[which] + jnp.log(total)
        lse_ref[0, :, which * rows : (which + 1) * rows] = lax.dot_general(
            pick, lse, NT, precision=lax.Precision.HIGHEST, preferred_element_type=wide
        )


def attention_forward(pre, cos_wide, sin_wide, starts, kv_pieces, meta):
    rows, width = pre.shape
    pairs, pieces = width // LANES, len(kv_pieces)
    pair = pl.BlockSpec((rows, LANES), lambda p, m: (0, p))
    whole = lambda a: pl.BlockSpec(a.shape, lambda p, m: (0,) * a.ndim)
    starts_wide = jnp.broadcast_to(starts[:, 0, :, None], (2, rows // 2, LANES))
    operands = (cos_wide, sin_wide, starts, starts_wide, *kv_pieces)
    spec = pltpu.PrefetchScalarGridSpec(
        num_scalar_prefetch=1,
        grid=(pairs,),
        in_specs=[pair] + [whole(a) for a in operands],
        out_specs=[pair, pl.BlockSpec((1, 8, 2 * rows), lambda p, m: (p, 0, 0)), pair],
        scratch_shapes=[
            pltpu.VMEM((2, rows, LANES), low),
            pltpu.VMEM((2, rows, LANES), wide),
            pltpu.VMEM((2, rows, LANES), wide),
            pltpu.VMEM((2, rows, LANES), wide),
        ],
    )
    return pl.pallas_call(
        functools.partial(forward_kernel, pieces),
        grid_spec=spec,
        out_shape=[
            jax.ShapeDtypeStruct((rows, width), wide),
            jax.ShapeDtypeStruct((pairs, 8, 2 * rows), wide),
            jax.ShapeDtypeStruct((rows, width), low),
        ],
        compiler_params=params(48),
        cost_estimate=cost(40),
        name="attention_forward",
    )(meta, pre, *operands)


def backward_kernel(pieces, meta, q_ref, do_ref, o_ref, lse_ref, start_ref, cos_ref, sin_ref, *refs):
    kv_refs = refs[:pieces]
    dq_ref = refs[pieces]
    out_refs = refs[pieces + 1 : 2 * pieces + 1]
    kt_ref, two_ref, dot_ref, delta_ref, acc_ref, dkv_ref = refs[2 * pieces + 1 :]
    number = pl.program_id(0)
    rows = q_ref.shape[0]
    half = rows // 2

    @pl.when(number == 0)
    def _():
        dkv_ref[...] = jnp.zeros_like(dkv_ref)
        for piece in range(pieces):
            kt_ref[piece] = kv_refs[piece][:, :LANES].astype(wide).T.astype(low)

    acc_ref[...] = jnp.zeros_like(acc_ref)
    lane = lax.broadcasted_iota(jnp.int32, (8, LANES), 1)
    pick_a = jnp.where(lane < HD, 1.0, 0.0).astype(wide)
    pick_b = 1.0 - pick_a
    for which in range(2):
        part = slice(which * half, (which + 1) * half)
        two_ref[which] = split_heads(q_ref[part, :], number)
        dot_ref[which] = split_heads(do_ref[part, :], number)
        product = do_ref[part, :].astype(wide) * o_ref[part, :]
        delta_ref[which] = jnp.concatenate(
            [
                lax.dot_general(
                    pick, product, NT, precision=lax.Precision.HIGHEST, preferred_element_type=wide
                )
                for pick in (pick_a, pick_b)
            ],
            axis=1,
        )

    def visit(sel, piece, block, mask):
        part = slice(block * half, (block + 1) * half)
        two, dot = two_ref[sel], dot_ref[sel]
        keys, values = kv_refs[piece][part, :LANES], kv_refs[piece][part, LANES:]
        scores = lax.dot_general(keys, two, NT, preferred_element_type=wide)
        grad_weights = lax.dot_general(values, dot, NT, preferred_element_type=wide)
        lse = lse_ref[0, 0:1, sel * rows : (sel + 1) * rows]
        if mask.shape[0] > 1:
            weights = jnp.where(mask, jnp.exp(scores - lse), 0.0)
        else:
            weights = jnp.exp(scores - jnp.where(mask, lse, -masked_score))
        grad_scores = (weights * (grad_weights - delta_ref[sel, 0:1, :])).astype(low)
        dkv_ref[piece, part, LANES:] += jnp.dot(
            weights.astype(low), dot, preferred_element_type=wide
        )
        dkv_ref[piece, part, :LANES] += jnp.dot(grad_scores, two, preferred_element_type=wide)
        acc_ref[sel] += jnp.dot(kt_ref[piece, :, part], grad_scores, preferred_element_type=wide)

    visit_blocks(meta, start_ref, half, pieces, visit)
    for which in range(2):
        part = slice(which * half, (which + 1) * half)
        cos, sin = cos_ref[:, part], sin_ref[:, part]
        turned = []
        for head in join_heads(acc_ref[which] * (1.0 / HD**0.5), number, half):
            upper, lower = head[: HD // 2], head[HD // 2 :]
            turned += [upper * cos + lower * sin, lower * cos - upper * sin]
        dq_ref[part, :] = jnp.concatenate(turned, axis=0).T.astype(low)

    @pl.when(number == pl.num_programs(0) - 1)
    def _():
        for piece in range(pieces):
            out_refs[piece][...] = dkv_ref[piece].astype(out_refs[piece].dtype)


def attention_backward(q, do, o, lse, starts, cos_turned, sin_turned, kv_pieces, meta):
    rows, width = q.shape
    pairs, pieces = width // LANES, len(kv_pieces)
    pair = pl.BlockSpec((rows, LANES), lambda p, m: (0, p))
    whole = lambda a: pl.BlockSpec(a.shape, lambda p, m: (0,) * a.ndim)
    fixed = (starts, cos_turned, sin_turned, *kv_pieces)
    spec = pltpu.PrefetchScalarGridSpec(
        num_scalar_prefetch=1,
        grid=(pairs,),
        in_specs=[pair, pair, pair, pl.BlockSpec((1, 8, 2 * rows), lambda p, m: (p, 0, 0))]
        + [whole(a) for a in fixed],
        out_specs=[pair] + [whole(a) for a in kv_pieces],
        scratch_shapes=[
            pltpu.VMEM((pieces, LANES, rows), low),
            pltpu.VMEM((2, rows, LANES), low),
            pltpu.VMEM((2, rows, LANES), low),
            pltpu.VMEM((2, 8, rows), wide),
            pltpu.VMEM((2, LANES, rows), wide),
            pltpu.VMEM((pieces, rows, 2 * LANES), wide),
        ],
    )
    return pl.pallas_call(
        functools.partial(backward_kernel, pieces),
        grid_spec=spec,
        out_shape=[jax.ShapeDtypeStruct((rows, width), low)]
        + [
            jax.ShapeDtypeStruct((rows, 2 * LANES), wide if piece == 0 else low)
            for piece in range(pieces)
        ],
        compiler_params=params(48),
        cost_estimate=cost(40),
        name="attention_backward",
    )(meta, q, do, o, lse, *fixed)


def feed_kernel(
    steps, fresh, device, n_a, n_b, cot_ref, gateup_ref, down_ref, *refs
):
    refs = refs[0 if fresh else 4 :]
    back_a, back_b, out_ref, hidden_ref, grad_ref, kept_ref = refs
    width = down_ref.shape[0]
    first = pl.program_id(0) < steps // 2
    normed = jnp.where(first, n_a[...], n_b[...])
    cot = cot_ref[...]
    gate = jnp.dot(normed, gateup_ref[:, :width], preferred_element_type=wide)
    up = jnp.dot(normed, gateup_ref[:, width:], preferred_element_type=wide)
    grad_hidden = lax.dot_general(cot, down_ref[...], NT, preferred_element_type=wide)
    sigmoid = jax.nn.sigmoid(gate)
    act = gate * sigmoid
    hidden = (act * up).astype(low)
    grad_gate = (grad_hidden * up * sigmoid * (1.0 + gate * (1.0 - sigmoid))).astype(low)
    grad_up = (grad_hidden * act).astype(low)
    kept_ref[...] = normed
    hidden_ref[...] = hidden
    grad_ref[:, :width] = grad_gate
    grad_ref[:, width:] = grad_up
    out_ref[...] = jnp.dot(hidden, down_ref[...], preferred_element_type=wide).astype(low)
    back = lax.dot_general(grad_gate, gateup_ref[:, :width], NT, preferred_element_type=wide)
    back = back + lax.dot_general(grad_up, gateup_ref[:, width:], NT, preferred_element_type=wide)

    @pl.when(first)
    def _():
        back_a[...] = back.astype(low)

    @pl.when(jnp.logical_not(first))
    def _():
        back_b[...] = back.astype(low)


def feed_forward(n_a, n_b, cot_all, gateup, down, device, kept, chip, block=256):
    rows, d = n_a.shape
    total, width = cot_all.shape[0], down.shape[0]
    block = min(block, rows)
    each = rows // block
    steps = 2 * each
    spot = lambda i, device: ((device[3] ^ (2 * chip + i // each)) * each + i % each, 0)
    whole = lambda a: pl.BlockSpec(a.shape, lambda i, device: (0, 0))
    halves = [
        pl.BlockSpec((block, d), lambda i, device: (jnp.minimum(i, each - 1), 0)),
        pl.BlockSpec((block, d), lambda i, device: (jnp.maximum(i - each, 0), 0)),
    ]
    in_specs = halves + [
        pl.BlockSpec((block, d), spot),
        whole(gateup),
        whole(down),
    ]
    fresh = kept is None
    if not fresh:
        in_specs += [pl.BlockSpec(memory_space=pl.ANY)] * 4
    spec = pltpu.PrefetchScalarGridSpec(
        num_scalar_prefetch=1,
        grid=(steps,),
        in_specs=in_specs,
        out_specs=halves
        + [pl.BlockSpec((block, n), spot) for n in (d, width, 2 * width, d)],
    )
    shapes = [(rows, d)] * 2 + [(total, n) for n in (d, width, 2 * width, d)]
    return pl.pallas_call(
        functools.partial(feed_kernel, steps, fresh),
        grid_spec=spec,
        out_shape=[jax.ShapeDtypeStruct(s, low) for s in shapes],
        input_output_aliases={} if fresh else {6 + i: 2 + i for i in range(4)},
        compiler_params=params(),
        cost_estimate=cost(15),
        name="feed_forward",
    )(device, n_a, n_b, cot_all, gateup, down, *(() if fresh else kept))


def weight_kernel(steps, shape, take, give, split, where, x_ref, y_ref, *refs):
    chips, cores, groups = shape
    outputs = 2 if split else groups
    acc_ref = refs[-1]
    out_refs = refs[-1 - outputs : -1]
    step = pl.program_id(0)
    size = x_ref.shape[1]
    product = lax.dot_general(x_ref[...], y_ref[...], TN, preferred_element_type=wide)

    @pl.when(step == 0)
    def _():
        acc_ref[:size] = product
        acc_ref[size:] = jnp.zeros_like(acc_ref[size:])

    @pl.when(step > 0)
    def _():
        acc_ref[:size] += product

    keep = lax.broadcasted_iota(jnp.int32, (give, 1), 0) < take

    def write(mine):
        for chip in range(chips):
            for core in range(cores):
                for group in range(groups):
                    low_edge = ((chip * cores + core) * groups + group) * take
                    value = jnp.where(keep, acc_ref[low_edge : low_edge + give], 0.0).astype(low)
                    if split:
                        at = lax.rem(group + groups - where[2], groups)
                        out_refs[core ^ mine][chip ^ where[1], at] = value
                    else:
                        row = (chip * cores + core) * give
                        out_refs[(group - mine) % groups][row : row + give] = value

    for mine in range(cores if split else groups):
        here = where[0 if split else 2] == mine
        pl.when((step == steps - 1) & here)(functools.partial(write, mine))


def weight_gradient(
    x, y, shape, take, where, split=False, block=1024, column=0, columns=1, into=()
):
    total, size = x.shape
    width = y.shape[1]
    give = padded(take, ROWS)
    block = min(block, total)
    steps = total // block
    chips, cores, groups = shape
    if split:
        out = pl.BlockSpec((chips, groups, give, width), lambda i, w: (0, 0, 0, column))
        shapes = [(chips, groups, give, columns * width)] * 2
    else:
        out = pl.BlockSpec((chips * cores * give, width), lambda i, w: (0, 0))
        shapes = [(chips * cores * give, width)] * groups
    return pl.pallas_call(
        functools.partial(weight_kernel, steps, shape, take, give, split),
        grid_spec=pltpu.PrefetchScalarGridSpec(
            num_scalar_prefetch=1,
            grid=(steps,),
            in_specs=[
                pl.BlockSpec((block, size), lambda i, w: (i, 0)),
                pl.BlockSpec((block, width), lambda i, w: (i, 0)),
            ]
            + [pl.BlockSpec(memory_space=pl.ANY)] * len(into),
            out_specs=[out] * len(shapes),
            scratch_shapes=[pltpu.VMEM((padded(size, 8) + give, width), wide)],
        ),
        out_shape=[jax.ShapeDtypeStruct(shape, low) for shape in shapes],
        input_output_aliases={3 + i: i for i in range(len(into))},
        compiler_params=params(),
        cost_estimate=cost(0.2),
        name="weight_gradient",
    )(where, x, y, *into)


def feed_back_kernel(
    shape, take, give, where, a_ref, b_ref, c_ref, d_ref, middle_ref, inv_ref, gain_ref, cot_ref,
    attn_ref, weight_ref, grad_ref, do_ref, gain_out, keep_ref, send_ref, acc_ref
):
    chips, cores, groups = shape
    size = attn_ref.shape[1]
    grad = a_ref[...].astype(wide) + b_ref[...].astype(wide)
    grad = grad + (c_ref[...].astype(wide) + d_ref[...].astype(wide))
    inv = inv_ref[...]
    scaled = middle_ref[...] * inv
    gain_out[...] = jnp.sum(grad * scaled, axis=0, keepdims=True)
    grad = grad * gain_ref[...]
    mean = jnp.sum(grad * scaled, axis=1, keepdims=True) * (1.0 / size)
    grad = cot_ref[...].astype(wide) + inv * (grad - scaled * mean)
    grad_ref[...] = grad
    grad_low = grad.astype(low)
    do_ref[...] = lax.dot_general(
        grad_low, weight_ref[...], NT, preferred_element_type=wide
    ).astype(low)
    acc_ref[:size] = lax.dot_general(attn_ref[...], grad_low, TN, preferred_element_type=wide)
    keep = lax.broadcasted_iota(jnp.int32, (give, 1), 0) < take

    def write(mine):
        for chip in range(chips):
            for core in range(cores):
                for group in range(groups):
                    low_edge = ((chip * cores + core) * groups + group) * take
                    value = jnp.where(keep, acc_ref[low_edge : low_edge + give], 0.0)
                    at = lax.rem(group + groups - where[2], groups)
                    target = send_ref if core ^ mine else keep_ref
                    target[chip ^ where[1], at] = value.astype(low)

    for mine in range(cores):
        pl.when(where[0] == mine)(functools.partial(write, mine))


def feed_back(shape, take, where, operands):
    chips, cores, groups = shape
    rows, size = operands[8].shape
    give = padded(take, ROWS)
    whole = lambda shape: pl.BlockSpec(shape, lambda i, w: (0,) * len(shape))
    pieces = pl.BlockSpec((chips, groups, give, size), lambda i, w: (0, 0, 0, 1))
    return pl.pallas_call(
        functools.partial(feed_back_kernel, shape, take, give),
        grid_spec=pltpu.PrefetchScalarGridSpec(
            num_scalar_prefetch=1,
            grid=(1,),
            in_specs=[whole(a.shape) for a in operands],
            out_specs=[whole((rows, size)), whole((rows, size)), whole((1, size)), pieces, pieces],
            scratch_shapes=[pltpu.VMEM((padded(size, 8) + give, size), wide)],
        ),
        out_shape=[
            jax.ShapeDtypeStruct((rows, size), wide),
            jax.ShapeDtypeStruct((rows, size), low),
            jax.ShapeDtypeStruct((1, size), wide),
        ]
        + [jax.ShapeDtypeStruct((chips, groups, give, 2 * size), low)] * 2,
        compiler_params=params(),
        cost_estimate=cost(1),
        name="feed_back",
    )(where, *operands)


def finish_kernel(
    shape, take, give, cuts, pieces, where, normed_ref, scaled_ref, inv_ref, gain_ref, query_ref,
    query_weight_ref, middle_ref, weight_ref, cos_ref, sin_ref, small_ref, *refs
):
    got_refs = refs[:pieces]
    keep_ref, send_ref, out_ref, acc_ref, row_ref, cut_ref = refs[pieces:]
    chips, cores, groups = shape
    size = normed_ref.shape[1]
    total = got_refs[0][...]
    for ref in got_refs[1:]:
        total = total + ref[...].astype(wide)
    keys, values = total[:, :LANES], total[:, LANES:]
    lane = lax.broadcasted_iota(jnp.int32, keys.shape, 1)
    swapped = jnp.where(
        lane % HD < HD // 2, pltpu.roll(keys, LANES - HD // 2, 1), pltpu.roll(keys, HD // 2, 1)
    )
    keys = keys * cos_ref[...] - swapped * sin_ref[...]
    grads = jnp.concatenate([keys, values], axis=1).astype(low)
    acc_ref[:size] = lax.dot_general(
        normed_ref[...], grads, TN, preferred_element_type=wide
    )
    grad = lax.dot_general(
        query_ref[...], query_weight_ref[...], NT, preferred_element_type=wide
    ) + lax.dot_general(grads, weight_ref[...], NT, preferred_element_type=wide)
    scaled = scaled_ref[...]
    row_ref[:, :size] = jnp.sum(grad * scaled, axis=0, keepdims=True)
    row_ref[:, size : size + small_ref.shape[1]] = small_ref[...]
    row_ref[:, size + small_ref.shape[1] :] = jnp.sum(grads.astype(wide), axis=0, keepdims=True)
    grad = grad * gain_ref[...]
    mean = jnp.sum(grad * scaled, axis=1, keepdims=True) * (1.0 / size)
    out_ref[...] = (middle_ref[...] + inv_ref[...] * (grad - scaled * mean)).astype(low)
    cut_ref[...] = jnp.zeros_like(cut_ref)
    for i in range(chips * cores * groups):
        at = 0
        for first, width in cuts:
            begin = first + i * width
            cut_ref[i : i + 1, at : at + width] = row_ref[:, begin : begin + width]
            at += width
    high = cut_ref[...].astype(low).astype(wide)
    rest = cut_ref[...] - high
    row = lax.broadcasted_iota(jnp.int32, (give, 1), 0)

    def write(mine):
        for chip in range(chips):
            for core in range(cores):
                for group in range(groups):
                    i = (chip * cores + core) * groups + group
                    value = jnp.where(row < take, acc_ref[i * take : i * take + give], 0.0)
                    value = jnp.where(row == take, high[i : i + 1], value)
                    value = jnp.where(row == take + 1, rest[i : i + 1], value)
                    at = lax.rem(group + groups - where[2], groups)
                    target = send_ref if core ^ mine else keep_ref
                    target[chip ^ where[1], at] = value.astype(low)

    for mine in range(cores):
        pl.when(where[0] == mine)(functools.partial(write, mine))


def finish_keyval(shape, take, give, cuts, where, got, operands):
    chips, cores, groups = shape
    rows, size = operands[0].shape
    width = got[0].shape[1]
    total = size + operands[10].shape[1] + width
    whole = lambda a: pl.BlockSpec(a.shape, lambda i, w: (0,) * a.ndim)
    pieces = pl.BlockSpec((chips, groups, give, width), lambda i, w: (0, 0, 0, 0))
    return pl.pallas_call(
        functools.partial(finish_kernel, shape, take, give, cuts, len(got)),
        grid_spec=pltpu.PrefetchScalarGridSpec(
            num_scalar_prefetch=1,
            grid=(1,),
            in_specs=[whole(a) for a in (*operands, *got)],
            out_specs=[pieces, pieces, pl.BlockSpec((rows, size), lambda i, w: (0, 0))],
            scratch_shapes=[
                pltpu.VMEM((padded(size, 8) + give, width), wide),
                pltpu.VMEM((1, total), wide),
                pltpu.VMEM((padded(chips * cores * groups, 8), width), wide),
            ],
        ),
        out_shape=[jax.ShapeDtypeStruct((chips, groups, give, width), low)] * 2
        + [jax.ShapeDtypeStruct((rows, size), low)],
        compiler_params=params(),
        cost_estimate=cost(20),
        name="finish_keyval",
    )(where, *operands, *got)


def place_rows(n_dp, n_group, take, give, device, own_ref, other_ref, at_ref, acc_ref):
    me, mine = device[3], device[2]
    for r in range(n_dp):
        source = own_ref if r % 2 == 0 else other_ref
        for s in range(n_group):
            row = (r // 2 * n_group + s) * give
            z = lax.rem(mine + s, n_group)
            at_ref[(me ^ r) * n_group + z] = source[row : row + give].astype(wide)
    for i in range(n_dp * n_group):
        acc_ref[i * take : i * take + give] = at_ref[i]


def assemble_kernel(sizes, device, own_ref, other_ref, o_ref, small_ref, at_ref, acc_ref):
    place_rows(*sizes, device, own_ref, other_ref, at_ref, acc_ref)
    count, take = sizes[0] * sizes[1], sizes[2]
    for i in range(count):
        for j in range(2):
            small_ref[j, i : i + 1] = at_ref[i, take + j : take + j + 1]
    o_ref[...] = acc_ref[: o_ref.shape[0]].astype(low)


def project_kernel(
    sizes, device, own_ref, other_ref, normed_ref, bias_ref, o_ref, pre_ref, at_ref, acc_ref
):
    place_rows(*sizes, device, own_ref, other_ref, at_ref, acc_ref)
    o_ref[...] = acc_ref[: o_ref.shape[0]].astype(low)
    pre_ref[...] = (
        jnp.dot(normed_ref[...], o_ref[...], preferred_element_type=wide) + bias_ref[...]
    )


def attend_kernel(
    sizes, device, own_ref, other_ref, attn_ref, tokens_ref, gain_ref, o_ref, low_ref, middle_ref,
    inv_ref, normed_ref, at_ref, acc_ref
):
    place_rows(*sizes, device, own_ref, other_ref, at_ref, acc_ref)
    o_ref[...] = acc_ref[: o_ref.shape[0]].astype(low)
    attn = attn_ref[...].astype(low)
    low_ref[...] = attn
    middle = tokens_ref[...].astype(wide) + jnp.dot(
        attn, o_ref[...], preferred_element_type=wide
    )
    middle_ref[...] = middle
    mean = jnp.sum(middle * middle, axis=1, keepdims=True) * (1.0 / middle.shape[1])
    inv = lax.rsqrt(mean + norm_eps)
    inv_ref[...] = inv
    normed_ref[...] = (middle * inv * gain_ref[...]).astype(low)


def assembled(kernel, name, device, own, other, take, operands, outputs, column=0, columns=1):
    n_dp, n_group = lax.axis_size("dp"), lax.axis_size("group")
    give = own.shape[0] // (n_dp // 2 * n_group)
    width = own.shape[1] // columns
    size = n_dp * n_group * take
    whole = lambda shape: pl.BlockSpec(shape, lambda i, m: (0,) * len(shape))
    outputs = [((size, width), low)] + outputs
    return pl.pallas_call(
        functools.partial(kernel, (n_dp, n_group, take, give)),
        grid_spec=pltpu.PrefetchScalarGridSpec(
            num_scalar_prefetch=1,
            grid=(1,),
            in_specs=[pl.BlockSpec((own.shape[0], width), lambda i, m: (0, column))] * 2
            + [whole(a.shape) for a in operands],
            out_specs=[whole(shape) for shape, _ in outputs],
            scratch_shapes=[
                pltpu.VMEM((n_dp * n_group, give, width), wide),
                pltpu.VMEM((size + give, width), wide),
            ],
        ),
        out_shape=[jax.ShapeDtypeStruct(*output) for output in outputs],
        compiler_params=params(),
        cost_estimate=cost(1),
        name=name,
    )(device, own, other, *operands)


def sum_kernel(*refs):
    total = refs[0][...].astype(wide)
    for ref in refs[1:-1]:
        total = total + ref[...].astype(wide)
    refs[-1][...] = total.astype(low)


def sum_pieces(pieces):
    rows, width = pieces[0].shape
    block = rows // 2
    spec = pl.BlockSpec((block, width), lambda i: (i, 0))
    return pl.pallas_call(
        sum_kernel,
        grid=(2,),
        in_specs=[spec] * len(pieces),
        out_specs=spec,
        out_shape=jax.ShapeDtypeStruct((rows, width), low),
        compiler_params=params(),
        cost_estimate=cost(0.1),
        name="sum_pieces",
    )(*pieces)


def return_kernel(near_ref, far_ref, *refs):
    x_a, x_b, y_a, y_b, x_out, y_out = refs
    top = pl.program_id(0) == 0
    near, far = near_ref[...].astype(wide), far_ref[...].astype(wide)
    x_sum = x_a[...].astype(wide) + x_b[...].astype(wide)
    y_sum = y_a[...].astype(wide) + y_b[...].astype(wide)
    x_out[...] = jnp.where(top, x_sum, x_sum + far).astype(low)
    y_out[...] = jnp.where(top, y_sum + near, y_sum).astype(low)


def return_sums(across, x_parts, y_parts):
    half, width = across[0].shape
    spec = pl.BlockSpec((half, width), lambda i: (i, 0))
    one = pl.BlockSpec((half, width), lambda i: (0, 0))
    return pl.pallas_call(
        return_kernel,
        grid=(2,),
        in_specs=[one, one] + [spec] * 4,
        out_specs=[spec] * 2,
        out_shape=[jax.ShapeDtypeStruct((2 * half, width), low)] * 2,
        compiler_params=params(),
        cost_estimate=cost(0.1),
        name="return_sums",
    )(*across, *x_parts, *y_parts)


def pack_kernel(keyval_ref, query_ref, output_ref, small_ref, second_ref, o_ref, buffer_ref):
    rows = query_ref.shape[0]
    piece = small_ref.shape[1]
    buffer_ref[...] = jnp.zeros_like(buffer_ref)
    at = 0
    for ref in (keyval_ref, query_ref, output_ref):
        buffer_ref[:rows, at : at + ref.shape[1]] = ref[...]
        at += ref.shape[1]
    second = second_ref[...]
    first = second.astype(low).astype(wide)
    rest = second - first
    middle = rest.astype(low).astype(wide)
    buffer_ref[rows : rows + 1, :piece] = small_ref[...]
    buffer_ref[rows : rows + 1, piece : 2 * piece] = first
    buffer_ref[rows + 1 : rows + 2, :piece] = middle
    buffer_ref[rows + 1 : rows + 2, piece : 2 * piece] = rest - middle
    o_ref[...] = buffer_ref[...].astype(low)


def pack_rows(keyval, query, output, small, second, give):
    arrays = (keyval, query, output, small[None], second[None])
    width = sum(a.shape[1] for a in arrays[:3])
    return pl.pallas_call(
        pack_kernel,
        grid=(1,),
        in_specs=[pl.BlockSpec(a.shape, lambda i: (0, 0)) for a in arrays],
        out_specs=pl.BlockSpec((give, width), lambda i: (0, 0)),
        out_shape=jax.ShapeDtypeStruct((give, width), low),
        scratch_shapes=[pltpu.VMEM((give, width), wide)],
        compiler_params=params(),
        cost_estimate=cost(0.5),
        name="pack_rows",
    )(*arrays)


def stack_kernel(outer, count, take, give, meta, *refs):
    o_ref, at_ref, acc_ref = refs[count:]
    for s in range(count):
        z = lax.rem(meta[2] + s, count)
        for i in range(outer):
            at_ref[i * count + z] = refs[s][i * give : (i + 1) * give].astype(wide)
    for i in range(outer * count):
        acc_ref[i * take : i * take + give] = at_ref[i]
    size = outer * count * take
    o_ref[:size] = acc_ref[:size].astype(low)
    if o_ref.shape[0] > size:
        o_ref[size:] = jnp.zeros_like(o_ref[size:])


def stack_rows(pieces, outer, take, me, rows):
    count, width = len(pieces), pieces[0].shape[1]
    give = pieces[0].shape[0] // outer
    whole = lambda r: pl.BlockSpec((r, width), lambda i, m: (0, 0))
    return pl.pallas_call(
        functools.partial(stack_kernel, outer, count, take, give),
        grid_spec=pltpu.PrefetchScalarGridSpec(
            num_scalar_prefetch=1,
            grid=(1,),
            in_specs=[whole(outer * give)] * count,
            out_specs=whole(rows),
            scratch_shapes=[
                pltpu.VMEM((outer * count, give, width), wide),
                pltpu.VMEM((padded(outer * count * take, 8) + give, width), wide),
            ],
        ),
        out_shape=jax.ShapeDtypeStruct((rows, width), low),
        compiler_params=params(),
        cost_estimate=cost(1),
        name="stack_rows",
    )(me, *pieces)


def cut_kernel(count, part, part_wide, w_ref, o_ref, buffer_ref):
    rows = w_ref.shape[0]
    buffer_ref[...] = jnp.zeros_like(buffer_ref)
    for p in range(count):
        for j in range(2):
            column = (j * count + p) * part
            buffer_ref[:rows, j * part_wide : j * part_wide + part] = w_ref[
                :, column : column + part
            ]
        o_ref[p] = buffer_ref[...].astype(low)


def cut_columns(weight, count, part_wide, give):
    rows, width = weight.shape
    part = width // (2 * count)
    shape = (count, give, 2 * part_wide)
    return pl.pallas_call(
        functools.partial(cut_kernel, count, part, part_wide),
        grid=(1,),
        in_specs=[pl.BlockSpec(weight.shape, lambda i: (0, 0))],
        out_specs=pl.BlockSpec(shape, lambda i: (0, 0, 0)),
        out_shape=jax.ShapeDtypeStruct(shape, low),
        scratch_shapes=[pltpu.VMEM((give, 2 * part_wide), wide)],
        compiler_params=params(),
        cost_estimate=cost(1),
        name="cut_columns",
    )(weight)


def update_kernel(count, part, part_wide, g_ref, m_ref, v_ref, w_ref, go_ref, vo_ref, wo_ref):
    rows = w_ref.shape[0]
    for p in range(count):
        piece = g_ref[p].astype(wide)
        for j in range(2):
            column = (j * count + p) * part
            go_ref[:, column : column + part] = piece[
                :rows, j * part_wide : j * part_wide + part
            ]
    vo_ref[...], wo_ref[...] = adamw_step(
        go_ref[...], m_ref[...], v_ref[...], w_ref[...], rate_proj, decay_rate
    )


def update_columns(pieces, first, second, weight):
    count, _, width = pieces.shape
    spec = pl.BlockSpec(weight.shape, lambda i: (0, 0))
    return pl.pallas_call(
        functools.partial(
            update_kernel, count, weight.shape[1] // (2 * count), width // 2
        ),
        grid=(1,),
        in_specs=[pl.BlockSpec(pieces.shape, lambda i: (0, 0, 0))] + [spec] * 3,
        out_specs=[spec] * 3,
        out_shape=[jax.ShapeDtypeStruct(weight.shape, wide)] * 3,
        compiler_params=params(),
        cost_estimate=cost(1),
        name="update_columns",
    )(pieces, first, second, weight)


def flip(value, mask):
    count = lax.axis_size("dp")
    return lax.ppermute(value, "dp", [(i, i ^ mask) for i in range(count)])


def shift(value, step):
    count = lax.axis_size("group")
    return lax.ppermute(value, "group", [((i + step) % count, i) for i in range(count)])


def shift_within(value, step):
    count = lax.axis_size("group")
    pairs = [(i + step, i) for i in range(count) if 0 <= i + step < count]
    return lax.ppermute(value, "group", pairs)


def after(value, *others):
    return lax.optimization_barrier((value, *others))[0]


def group_pieces(block, steps=None):
    return [block] + [shift(block, s) for s in range(1, lax.axis_size("group"))]


def group_send(blocks):
    count = lax.axis_size("group")
    return [blocks[0]] + [shift(blocks[count - s].astype(low), s) for s in range(1, count)]


def add_up(terms):
    return functools.reduce(jnp.add, [term.astype(wide) for term in terms])


def gather_chips(column):
    evens = [column] + [flip(column, r) for r in range(2, lax.axis_size("dp"), 2)]
    return jnp.concatenate(evens, axis=0)


def scatter_pair(keep, send):
    return keep.astype(wide) + flip(send, 1).astype(wide)


def scatter_chips(pair):
    got = [flip(pair[r].astype(low), 2 * r) for r in range(1, pair.shape[0])]
    return add_up([pair[0]] + got)


def body(
    tokens,
    positions,
    cotangent,
    query_weight,
    query_first,
    query_second,
    keyval_weight,
    keyval_first,
    keyval_second,
    output_weight,
    output_first,
    output_second,
    gateup_weight,
    gateup_first,
    gateup_second,
    down_weight,
    down_first,
    down_second,
    small_weight,
    small_first,
    small_second,
):
    row_count = tokens.shape[0]
    half = row_count // 2
    n_dp = lax.axis_size("dp")
    group_size = lax.axis_size("group")
    device_count = n_dp * group_size
    my_dp = lax.axis_index("dp")
    my_index = lax.axis_index("group")
    flat_index = my_dp * group_size + my_index
    seq_len = row_count * group_size
    query_width = HQ * HD
    kv_width = HK * HD
    small_size = 2 * D + query_width + 2 * kv_width
    rest_length = small_size - kv_width
    rest_piece = rest_length // device_count
    value_piece = kv_width // device_count
    small_piece = small_size // device_count
    part = FF // n_dp
    part_wide = padded(part, LANES)
    in_rows = query_weight.shape[0]
    device = jnp.stack([my_dp & 1, my_dp >> 1, my_index, my_dp]).astype(jnp.int32)
    in_give = padded(in_rows + 2, ROWS)
    down_rows = down_weight.shape[0]

    every_block = pack_rows(
        keyval_weight, query_weight, output_weight, small_weight, small_second, in_give
    )
    gateup_pieces = cut_columns(gateup_weight, n_dp, part_wide, in_give)
    every_pieces = group_pieces(every_block)
    every_column = jnp.concatenate(after(every_pieces, gateup_pieces), axis=0)
    keyval_column = every_column[:, : 2 * kv_width]
    both_column = every_column[:, 2 * kv_width :]
    keyval_own = gather_chips(keyval_column)
    small_shape = (2, device_count, 2 * kv_width)
    keyval_full, small_all = assembled(
        assemble_kernel, "assemble_rows", device, keyval_own, flip(keyval_own, 1), in_rows, (),
        [(small_shape, wide)],
    )
    small_all = small_all[:, :, : 2 * small_piece].reshape(2, device_count, 2, small_piece)
    small_values = small_all[0, :, 0].reshape(small_size)
    small_second_all = (small_all[0, :, 1] + small_all[1, :, 0] + small_all[1, :, 1]).reshape(
        small_size
    )

    down_part = lax.all_gather(down_weight.astype(low), "group", axis=0, tiled=True)
    down_part = jnp.pad(down_part, ((0, part_wide - part), (0, 0)))

    gain_one = small_values[:D]
    gain_two = small_values[D : 2 * D]
    bias_qkv = small_values[2 * D :]
    place_row = positions[0]
    local_index = my_index * row_count + jnp.arange(row_count, dtype=jnp.int32)
    local_places = lax.dynamic_slice_in_dim(place_row, my_index * row_count, row_count, 0)
    starts = (local_index - local_places).reshape(2, half).astype(jnp.int32)
    starts = jnp.broadcast_to(starts[:, None, :], (2, 8, half))
    angles = rotary_angles(local_places)
    cosine, sine_table = jnp.cos(angles), jnp.sin(angles)
    cos_wide = jnp.concatenate([cosine] * 4, axis=1)
    sin_wide = jnp.concatenate([-sine_table, sine_table] * 2, axis=1)

    def swap(values):
        quarter = HD // 2
        pieces = [values[:, i * quarter : (i + 1) * quarter] for i in range(2 * HK)]
        return jnp.concatenate([pieces[i ^ 1] for i in range(2 * HK)], axis=1)

    act_in = tokens.astype(wide)
    inv_one = lax.rsqrt(jnp.mean(act_in * act_in, axis=1, keepdims=True) + norm_eps)
    scaled_one = act_in * inv_one
    normed_one = (scaled_one * gain_one).astype(low)
    keyval_pre = (
        jnp.dot(normed_one, keyval_full, preferred_element_type=wide) + bias_qkv[query_width:]
    )
    key_pre = keyval_pre[:, :kv_width]
    key_low = (key_pre * cos_wide + swap(key_pre) * sin_wide).astype(low)
    keyval_low = jnp.concatenate([key_low, keyval_pre[:, kv_width:].astype(low)], axis=1)
    keyval_parts = [keyval_low] + [shift_within(keyval_low, -s) for s in range(1, group_size)]
    both_own = gather_chips(after(both_column, keyval_low))
    gateup_column = lax.all_to_all(after(gateup_pieces, keyval_low), "dp", 0, 0, tiled=True)
    gateup_column = gateup_column.reshape(n_dp * in_give, 2 * part_wide)
    both_own, keyval_parts, gateup_column, down_part = after(
        (both_own, keyval_parts, gateup_column, down_part)
    )
    cot_all = lax.all_gather(after(cotangent, both_own), "dp", axis=0, tiled=True)
    both_other = flip(both_own, 1)
    query_full, query_pre = assembled(
        project_kernel, "project_query", device, both_own, both_other, in_rows,
        (normed_one, bias_qkv[None, :query_width]), [((row_count, query_width), wide)], 0, 2,
    )
    gateup_pieces = group_pieces(gateup_column)
    attn_float, log_total, query_low = attention_forward(
        query_pre, cos_wide, sin_wide, starts, keyval_parts, device
    )
    attn_float = after(attn_float, gateup_pieces)
    output_full, attn_low, middle, inv_two, normed_two = assembled(
        attend_kernel, "attention_output", device, both_own, both_other, in_rows,
        (attn_float, tokens, gain_two[None]),
        [
            ((row_count, query_width), low),
            ((row_count, D), wide),
            ((row_count, 1), wide),
            ((row_count, D), low),
        ],
        1, 2,
    )

    gateup_pieces = after(gateup_pieces, normed_two)
    gateup_part = stack_rows(gateup_pieces, n_dp, in_rows, device, D)
    chips = n_dp // 2
    pieces, down_shape = (chips, 2, group_size), (1, 1, group_size)
    kept, sides, back = None, {0: normed_two}, {}
    for k in range(1, chips):
        if n_dp != 8 or k != 3:
            sides[k] = flip(normed_two, 2 * k)

    def visit(k, kept):
        back_a, back_b, *kept = feed_forward(
            sides[k], flip(sides[k], 1), cot_all, gateup_part, down_part, device, kept, k
        )
        back[k] = (back_a, flip(back_b, 1))
        return kept

    if n_dp == 8:
        kept = visit(0, kept)
        sides[1], sides[2] = after((sides[1], sides[2]), kept)
        across = [flip(sides[1][:half], 4), flip(sides[2][half:], 2)]
        kept = visit(1, kept)
        sides[3] = jnp.concatenate(after(across, kept), axis=0)
        kept = visit(3, kept)
        corner = add_up(back[3]).astype(low)
        across = [flip(corner[:half], 2), flip(corner[half:], 4)]
        kept = visit(2, kept)
        down_term = weight_gradient(kept[1], cot_all, down_shape, down_rows, device)
        across = after(across, down_term)
        x_sum, y_sum = return_sums(across, back[1], back[2])
        kept, y_sum = after((kept, y_sum))
        returned = [*back[0], flip(x_sum, 2), flip(y_sum, 4)]
    else:
        for k in range(chips):
            kept = visit(k, kept)
        down_term = weight_gradient(kept[1], cot_all, down_shape, down_rows, device)
        returned = list(back[0])
        returned += [flip(add_up(back[k]).astype(low), 2 * k) for k in range(1, chips)]
    out_all, _, gate_all, normed_all = kept
    down_got = group_send(down_term)
    gateup_term = weight_gradient(normed_all, gate_all, pieces, in_rows, device)
    gateup_got = group_send(gateup_term)
    returned, gateup_got[0], down_got = after((returned, gateup_got[0], down_got))
    out_sum = lax.psum_scatter(after(out_all, returned), "dp", scatter_dimension=0, tiled=True)

    if len(returned) > 4:
        returned = returned[:3] + [add_up(returned[3:])]
    grad_middle, grad_attn_low, gain_two_term, *both_terms = feed_back(
        pieces,
        in_rows,
        device,
        (
            *returned,
            middle,
            inv_two,
            gain_two[None],
            cotangent,
            attn_low,
            output_full,
        ),
    )
    grad_query_pre, *keyval_terms = attention_backward(
        query_low,
        grad_attn_low,
        attn_float,
        log_total,
        starts,
        cosine.T,
        sine_table.T,
        keyval_parts,
        device,
    )
    grad_query_pre, keyval_terms, gateup_got = after((grad_query_pre, keyval_terms, gateup_got))
    keyval_got = [keyval_terms[0]]
    keyval_got += [shift_within(keyval_terms[s], s) for s in range(1, group_size)]
    both_terms = weight_gradient(
        normed_one, grad_query_pre, pieces, in_rows, device, split=True, columns=2, into=both_terms
    )
    gateup_sum = sum_pieces(after(gateup_got, both_terms)).reshape(n_dp, -1, 2 * part_wide)
    to_send, gateup_sum = after((both_terms[1], gateup_sum), keyval_got, out_sum)
    both_pair = scatter_pair(both_terms[0], to_send)
    gateup_sum = lax.all_to_all(gateup_sum, "dp", 0, 0, tiled=True)
    both_total = scatter_chips(both_pair)
    keyval_got, gateup_sum = after((keyval_got, gateup_sum), both_pair)
    bias_term = jnp.sum(grad_query_pre.astype(wide), axis=0)
    *last_terms, tokens_grad = finish_keyval(
        pieces,
        in_rows,
        in_give,
        ((0, small_piece), (0, rest_piece), (rest_length, value_piece)),
        device,
        keyval_got,
        (
            normed_one,
            scaled_one,
            inv_one,
            gain_one[None],
            grad_query_pre,
            query_full,
            grad_middle,
            keyval_full,
            cos_wide,
            sin_wide,
            jnp.concatenate([gain_two_term, bias_term[None]], axis=1),
        ),
    )
    small_width = small_piece + rest_piece + value_piece
    gateup_grad, gateup_second_out, gateup_weight_out = update_columns(
        after(gateup_sum, last_terms), gateup_first, gateup_second, gateup_weight
    )
    last_terms, gateup_second_out = after((last_terms, gateup_second_out), both_total)
    last_total = scatter_chips(scatter_pair(*last_terms))
    down_got = after(down_got, last_total)
    late_middle, out_sum = after((middle, out_sum), last_total)
    layer_out = (late_middle + out_sum.astype(wide)).astype(low)
    down_grad = add_up(down_got)[:down_rows]
    some = last_total.shape[1] - both_total.shape[1]
    both_total = jnp.pad(both_total, ((0, 0), (0, some), (0, 0)))
    down_second_out, down_weight_out = adamw_step(
        down_grad, down_first, down_second, down_weight, rate_proj, decay_rate
    )
    every_got = group_send(jnp.concatenate([both_total, last_total], axis=2))
    every_got, down_second_out, layer_out = after((every_got, down_second_out, layer_out))
    every_sum = add_up(every_got)
    query_grad = every_sum[:in_rows, :query_width]
    output_grad = every_sum[:in_rows, query_width : query_width + D]
    last_sum = every_sum[:, query_width + D :]
    keyval_grad = last_sum[:in_rows]
    small_sum = last_sum[in_rows, :small_width] + last_sum[in_rows + 1, :small_width]
    small_grad = small_sum[:small_piece]
    rest_grad = small_sum[small_piece : small_piece + rest_piece]
    value_grad = small_sum[small_piece + rest_piece :]

    query_second_out, query_weight_out = adamw_step(
        query_grad, query_first, query_second, query_weight, rate_proj, decay_rate
    )
    keyval_second_out, keyval_weight_out = adamw_step(
        keyval_grad, keyval_first, keyval_second, keyval_weight, rate_proj, decay_rate
    )
    output_second_out, output_weight_out = adamw_step(
        output_grad, output_first, output_second, output_weight, rate_out, decay_rate
    )
    _, small_weight_out = adamw_step(
        small_grad, small_first, small_second, small_weight, rate_small, 0.0
    )
    rest_second = lax.dynamic_slice_in_dim(
        small_second_all, flat_index * rest_piece, rest_piece, 0
    )
    value_second = lax.dynamic_slice_in_dim(
        small_second_all, rest_length + flat_index * value_piece, value_piece, 0
    )
    small_second_out = beta_two * rest_second + (1.0 - beta_two) * rest_grad * rest_grad
    value_bias_second_out = beta_two * value_second + (1.0 - beta_two) * value_grad * value_grad
    return (
        layer_out,
        tokens_grad,
        query_grad,
        query_second_out,
        query_weight_out,
        keyval_grad,
        keyval_second_out,
        keyval_weight_out,
        output_grad,
        output_second_out,
        output_weight_out,
        gateup_grad,
        gateup_second_out,
        gateup_weight_out,
        down_grad,
        down_second_out,
        down_weight_out,
        small_grad,
        small_second_out,
        value_bias_second_out,
        small_weight_out,
    )


def solution(mesh):
    rows = P(("dp", "group"), None)
    line = P(("dp", "group"))
    in_specs = (rows, P("dp", None)) + (rows,) * 16 + (line,) * 3
    out_specs = (rows,) * 17 + (line,) * 4
    return jax.shard_map(body, mesh=mesh, in_specs=in_specs, out_specs=out_specs, check_vma=False)
```

```python
import functools

import jax
import jax.numpy as jnp
from jax import lax
from jax.experimental import pallas as pl
from jax.experimental.pallas import tpu as pltpu
from jax.sharding import PartitionSpec as P

D = 896
HQ = 14
HK = 2
HD = 64
FF = 4864
STEP = 10


theta_base = 1000000.0
norm_eps = 1e-06
beta_one = 0.9
beta_two = 0.95
adam_eps = 1e-08
decay_rate = 0.1
rate_proj = 0.02
rate_out = 0.5
rate_small = 0.2
masked_score = -1e30

low = jnp.bfloat16
wide = jnp.float32


MIB = 1024 * 1024
LANES = 128
ROWS = 16
NT = (((1,), (1,)), ((), ()))
TN = (((0,), (0,)), ((), ()))


def padded(size, unit):
    return -(-size // unit) * unit


def rotary_angles(places):
    half_size = HD // 2
    inv_freq = theta_base ** (-(jnp.arange(half_size, dtype=wide) * 2.0) / HD)
    return places.astype(wide)[:, None] * inv_freq[None, :]


def adamw_step(gradient, first_old, second_old, weight, step_rate, decay_factor):
    first_new = beta_one * first_old + (1.0 - beta_one) * gradient
    second_new = beta_two * second_old + (1.0 - beta_two) * gradient * gradient
    first_hat = first_new / (1.0 - beta_one**STEP)
    second_hat = second_new / (1.0 - beta_two**STEP)
    updated = weight - step_rate * (
        first_hat / (jnp.sqrt(second_hat) + adam_eps) + decay_factor * weight
    )
    return (second_new, updated)


def params(limit=56):
    return pltpu.CompilerParams(
        vmem_limit_bytes=limit * MIB, dimension_semantics=("arbitrary",)
    )


def cost(micros):
    return pl.CostEstimate(flops=int(micros * 10**9), bytes_accessed=10**6, transcendentals=0)


def split_heads(pair, number):
    lane = lax.broadcasted_iota(jnp.int32, pair.shape, 1)
    zero = jnp.zeros_like(pair)
    turned = pltpu.roll(pair, HD, 1)
    low_a = 2 * number < HQ // HK
    low_b = 2 * number + 1 < HQ // HK
    first = jnp.where((lane < HD) == low_a, jnp.where(low_a, pair, turned), zero)
    second = jnp.where((lane < HD) == low_b, jnp.where(low_b, turned, pair), zero)
    return jnp.concatenate([first, second], axis=0)


def join_heads(both, number, half):
    low_a = 2 * number < HQ // HK
    low_b = 2 * number + 1 < HQ // HK
    first = jnp.where(low_a, both[:HD, :half], both[HD:, :half])
    second = jnp.where(low_b, both[:HD, half:], both[HD:, half:])
    return first, second


def key_mask(start, first_key, first_query, half, causal):
    key_row = lax.broadcasted_iota(jnp.int32, (half, half), 0)
    ok = key_row >= start - first_key
    if causal:
        ok &= key_row <= lax.broadcasted_iota(jnp.int32, (1, half), 1) + (first_query - first_key)
    return jnp.concatenate([ok, ok], axis=1)


def query_mask(start, first_key, first_query, half, causal):
    key = lax.broadcasted_iota(jnp.int32, (half, half), 1)
    ok = key >= jnp.concatenate([start - first_key] * (half // LANES), axis=1)
    if causal:
        ok &= key <= lax.broadcasted_iota(jnp.int32, (half, half), 0) + (first_query - first_key)
    return jnp.concatenate([ok, ok], axis=0)


def visit_blocks(meta, start_ref, half, pieces, visit):
    mine = meta[2]
    first_query = mine * 2 * half
    turned = start_ref.shape[2] == LANES
    mask_of = query_mask if turned else key_mask
    start_of = lambda sel: start_ref[sel] if turned else start_ref[sel, 0:1, :]
    for sel, block in ((0, 0), (1, 0), (1, 1)):
        mask = mask_of(
            start_of(sel), first_query + block * half, first_query + sel * half, half, sel == block
        )
        visit(sel, 0, block, mask)
    for piece in range(1, pieces):
        first_key = (mine - piece) * 2 * half

        def region(cut):
            for block in range(2):
                for sel in range(2):
                    if cut and block == 0:
                        mask = mask_of(start_of(sel), first_key, first_query, half, False)
                    else:
                        mask = start_of(sel) <= first_key + block * half
                        mask = jnp.concatenate([mask, mask], axis=0 if turned else 1)
                    visit(sel, piece, block, mask)

        pl.when(mine == piece)(functools.partial(region, True))
        pl.when(mine > piece)(functools.partial(region, False))


def forward_kernel(pieces, meta, pre_ref, cos_ref, sin_ref, start_ref, starts_ref, *refs):
    kv_refs = refs[:pieces]
    o_ref, lse_ref, q_ref, two_ref, top_ref, sum_ref, acc_ref = refs[pieces:]
    number = pl.program_id(0)
    rows = pre_ref.shape[0]
    half = rows // 2
    pre = pre_ref[...]
    lane = lax.broadcasted_iota(jnp.int32, pre.shape, 1)
    swapped = jnp.where(
        lane % HD < HD // 2, pltpu.roll(pre, LANES - HD // 2, 1), pltpu.roll(pre, HD // 2, 1)
    )
    turned = (pre * cos_ref[...] + swapped * sin_ref[...]).astype(low)
    turned = (turned.astype(wide) * (1.0 / HD**0.5)).astype(low)
    q_ref[...] = turned
    for which in range(2):
        two_ref[which] = split_heads(turned[which * half : (which + 1) * half, :], number)
    top_ref[...] = jnp.full_like(top_ref, masked_score)
    sum_ref[...] = jnp.zeros_like(sum_ref)
    acc_ref[...] = jnp.zeros_like(acc_ref)

    def scores_of(sel, piece, block):
        part = slice(block * half, (block + 1) * half)
        return lax.dot_general(
            two_ref[sel], kv_refs[piece][part, :LANES], NT, preferred_element_type=wide
        )

    def find_top(sel, piece, block, mask):
        scores = scores_of(sel, piece, block)
        if mask.shape[1] > LANES:
            scores = jnp.where(mask, scores, masked_score)
        peak = functools.reduce(jnp.maximum, [scores[:, i : i + LANES] for i in range(0, half, LANES)])
        if mask.shape[1] <= LANES:
            peak = jnp.where(mask, peak, masked_score)
        top_ref[sel] = jnp.maximum(top_ref[sel], peak)

    def sum_up(sel, piece, block, mask):
        part = slice(block * half, (block + 1) * half)
        scores = scores_of(sel, piece, block)
        level = top_ref[sel]
        if mask.shape[1] > LANES:
            scores = jnp.where(mask, scores, masked_score)
        else:
            level = jnp.where(mask, level, -masked_score)
        weights = [jnp.exp(scores[:, i : i + LANES] - level) for i in range(0, half, LANES)]
        sum_ref[sel] += functools.reduce(jnp.add, weights)
        acc_ref[sel] += jnp.dot(
            jnp.concatenate(weights, axis=1).astype(low),
            kv_refs[piece][part, LANES:],
            preferred_element_type=wide,
        )

    visit_blocks(meta, starts_ref, half, pieces, find_top)
    for which in range(2):
        top_ref[which] = jnp.broadcast_to(
            jnp.max(top_ref[which], axis=1, keepdims=True), top_ref.shape[1:]
        )
    visit_blocks(meta, starts_ref, half, pieces, sum_up)
    lane = lax.broadcasted_iota(jnp.int32, (half, LANES), 1)
    low_a = 2 * number < HQ // HK
    low_b = 2 * number + 1 < HQ // HK
    pick = jnp.where(lax.broadcasted_iota(jnp.int32, (8, LANES), 1) == 0, 1.0, 0.0).astype(wide)
    for which in range(2):
        total = jnp.sum(sum_ref[which], axis=1, keepdims=True)
        out = acc_ref[which] / total
        first, second = out[:half], out[half:]
        first = jnp.where(low_a, first, pltpu.roll(first, HD, 1))
        second = jnp.where(low_b, pltpu.roll(second, HD, 1), second)
        o_ref[which * half : (which + 1) * half, :] = jnp.where(lane < HD, first, second)
        lse = top_ref[which] + jnp.log(total)
        lse_ref[0, :, which * rows : (which + 1) * rows] = lax.dot_general(
            pick, lse, NT, precision=lax.Precision.HIGHEST, preferred_element_type=wide
        )


def attention_forward(pre, cos_wide, sin_wide, starts, kv_pieces, meta):
    rows, width = pre.shape
    pairs, pieces = width // LANES, len(kv_pieces)
    pair = pl.BlockSpec((rows, LANES), lambda p, m: (0, p))
    whole = lambda a: pl.BlockSpec(a.shape, lambda p, m: (0,) * a.ndim)
    starts_wide = jnp.broadcast_to(starts[:, 0, :, None], (2, rows // 2, LANES))
    operands = (cos_wide, sin_wide, starts, starts_wide, *kv_pieces)
    spec = pltpu.PrefetchScalarGridSpec(
        num_scalar_prefetch=1,
        grid=(pairs,),
        in_specs=[pair] + [whole(a) for a in operands],
        out_specs=[pair, pl.BlockSpec((1, 8, 2 * rows), lambda p, m: (p, 0, 0)), pair],
        scratch_shapes=[
            pltpu.VMEM((2, rows, LANES), low),
            pltpu.VMEM((2, rows, LANES), wide),
            pltpu.VMEM((2, rows, LANES), wide),
            pltpu.VMEM((2, rows, LANES), wide),
        ],
    )
    return pl.pallas_call(
        functools.partial(forward_kernel, pieces),
        grid_spec=spec,
        out_shape=[
            jax.ShapeDtypeStruct((rows, width), wide),
            jax.ShapeDtypeStruct((pairs, 8, 2 * rows), wide),
            jax.ShapeDtypeStruct((rows, width), low),
        ],
        compiler_params=params(48),
        cost_estimate=cost(40),
        name="attention_forward",
    )(meta, pre, *operands)


def backward_kernel(pieces, meta, q_ref, do_ref, o_ref, lse_ref, start_ref, cos_ref, sin_ref, *refs):
    kv_refs = refs[:pieces]
    dq_ref = refs[pieces]
    out_refs = refs[pieces + 1 : 2 * pieces + 1]
    kt_ref, two_ref, dot_ref, delta_ref, acc_ref, dkv_ref = refs[2 * pieces + 1 :]
    number = pl.program_id(0)
    rows = q_ref.shape[0]
    half = rows // 2

    @pl.when(number == 0)
    def _():
        dkv_ref[...] = jnp.zeros_like(dkv_ref)
        for piece in range(pieces):
            kt_ref[piece] = kv_refs[piece][:, :LANES].astype(wide).T.astype(low)

    acc_ref[...] = jnp.zeros_like(acc_ref)
    lane = lax.broadcasted_iota(jnp.int32, (8, LANES), 1)
    pick_a = jnp.where(lane < HD, 1.0, 0.0).astype(wide)
    pick_b = 1.0 - pick_a
    for which in range(2):
        part = slice(which * half, (which + 1) * half)
        two_ref[which] = split_heads(q_ref[part, :], number)
        dot_ref[which] = split_heads(do_ref[part, :], number)
        product = do_ref[part, :].astype(wide) * o_ref[part, :]
        delta_ref[which] = jnp.concatenate(
            [
                lax.dot_general(
                    pick, product, NT, precision=lax.Precision.HIGHEST, preferred_element_type=wide
                )
                for pick in (pick_a, pick_b)
            ],
            axis=1,
        )

    def visit(sel, piece, block, mask):
        part = slice(block * half, (block + 1) * half)
        two, dot = two_ref[sel], dot_ref[sel]
        keys, values = kv_refs[piece][part, :LANES], kv_refs[piece][part, LANES:]
        scores = lax.dot_general(keys, two, NT, preferred_element_type=wide)
        grad_weights = lax.dot_general(values, dot, NT, preferred_element_type=wide)
        lse = lse_ref[0, 0:1, sel * rows : (sel + 1) * rows]
        if mask.shape[0] > 1:
            weights = jnp.where(mask, jnp.exp(scores - lse), 0.0)
        else:
            weights = jnp.exp(scores - jnp.where(mask, lse, -masked_score))
        grad_scores = (weights * (grad_weights - delta_ref[sel, 0:1, :])).astype(low)
        dkv_ref[piece, part, LANES:] += jnp.dot(
            weights.astype(low), dot, preferred_element_type=wide
        )
        dkv_ref[piece, part, :LANES] += jnp.dot(grad_scores, two, preferred_element_type=wide)
        acc_ref[sel] += jnp.dot(kt_ref[piece, :, part], grad_scores, preferred_element_type=wide)

    visit_blocks(meta, start_ref, half, pieces, visit)
    for which in range(2):
        part = slice(which * half, (which + 1) * half)
        cos, sin = cos_ref[:, part], sin_ref[:, part]
        turned = []
        for head in join_heads(acc_ref[which] * (1.0 / HD**0.5), number, half):
            upper, lower = head[: HD // 2], head[HD // 2 :]
            turned += [upper * cos + lower * sin, lower * cos - upper * sin]
        dq_ref[part, :] = jnp.concatenate(turned, axis=0).T.astype(low)

    @pl.when(number == pl.num_programs(0) - 1)
    def _():
        for piece in range(pieces):
            out_refs[piece][...] = dkv_ref[piece].astype(out_refs[piece].dtype)


def attention_backward(q, do, o, lse, starts, cos_turned, sin_turned, kv_pieces, meta):
    rows, width = q.shape
    pairs, pieces = width // LANES, len(kv_pieces)
    pair = pl.BlockSpec((rows, LANES), lambda p, m: (0, p))
    whole = lambda a: pl.BlockSpec(a.shape, lambda p, m: (0,) * a.ndim)
    fixed = (starts, cos_turned, sin_turned, *kv_pieces)
    spec = pltpu.PrefetchScalarGridSpec(
        num_scalar_prefetch=1,
        grid=(pairs,),
        in_specs=[pair, pair, pair, pl.BlockSpec((1, 8, 2 * rows), lambda p, m: (p, 0, 0))]
        + [whole(a) for a in fixed],
        out_specs=[pair] + [whole(a) for a in kv_pieces],
        scratch_shapes=[
            pltpu.VMEM((pieces, LANES, rows), low),
            pltpu.VMEM((2, rows, LANES), low),
            pltpu.VMEM((2, rows, LANES), low),
            pltpu.VMEM((2, 8, rows), wide),
            pltpu.VMEM((2, LANES, rows), wide),
            pltpu.VMEM((pieces, rows, 2 * LANES), wide),
        ],
    )
    return pl.pallas_call(
        functools.partial(backward_kernel, pieces),
        grid_spec=spec,
        out_shape=[jax.ShapeDtypeStruct((rows, width), low)]
        + [
            jax.ShapeDtypeStruct((rows, 2 * LANES), wide if piece == 0 else low)
            for piece in range(pieces)
        ],
        compiler_params=params(48),
        cost_estimate=cost(40),
        name="attention_backward",
    )(meta, q, do, o, lse, *fixed)


def feed_kernel(
    steps, fresh, device, n_a, n_b, cot_ref, gateup_ref, down_ref, *refs
):
    refs = refs[0 if fresh else 4 :]
    back_a, back_b, out_ref, hidden_ref, grad_ref, kept_ref = refs
    width = down_ref.shape[0]
    first = pl.program_id(0) < steps // 2
    normed = jnp.where(first, n_a[...], n_b[...])
    cot = cot_ref[...]
    gate = jnp.dot(normed, gateup_ref[:, :width], preferred_element_type=wide)
    up = jnp.dot(normed, gateup_ref[:, width:], preferred_element_type=wide)
    grad_hidden = lax.dot_general(cot, down_ref[...], NT, preferred_element_type=wide)
    sigmoid = jax.nn.sigmoid(gate)
    act = gate * sigmoid
    hidden = (act * up).astype(low)
    grad_gate = (grad_hidden * up * sigmoid * (1.0 + gate * (1.0 - sigmoid))).astype(low)
    grad_up = (grad_hidden * act).astype(low)
    kept_ref[...] = normed
    hidden_ref[...] = hidden
    grad_ref[:, :width] = grad_gate
    grad_ref[:, width:] = grad_up
    out_ref[...] = jnp.dot(hidden, down_ref[...], preferred_element_type=wide).astype(low)
    back = lax.dot_general(grad_gate, gateup_ref[:, :width], NT, preferred_element_type=wide)
    back = back + lax.dot_general(grad_up, gateup_ref[:, width:], NT, preferred_element_type=wide)

    @pl.when(first)
    def _():
        back_a[...] = back.astype(low)

    @pl.when(jnp.logical_not(first))
    def _():
        back_b[...] = back.astype(low)


def feed_forward(n_a, n_b, cot_all, gateup, down, device, kept, chip, block=256):
    rows, d = n_a.shape
    total, width = cot_all.shape[0], down.shape[0]
    block = min(block, rows)
    each = rows // block
    steps = 2 * each
    spot = lambda i, device: ((device[3] ^ (2 * chip + i // each)) * each + i % each, 0)
    whole = lambda a: pl.BlockSpec(a.shape, lambda i, device: (0, 0))
    halves = [
        pl.BlockSpec((block, d), lambda i, device: (jnp.minimum(i, each - 1), 0)),
        pl.BlockSpec((block, d), lambda i, device: (jnp.maximum(i - each, 0), 0)),
    ]
    in_specs = halves + [
        pl.BlockSpec((block, d), spot),
        whole(gateup),
        whole(down),
    ]
    fresh = kept is None
    if not fresh:
        in_specs += [pl.BlockSpec(memory_space=pl.ANY)] * 4
    spec = pltpu.PrefetchScalarGridSpec(
        num_scalar_prefetch=1,
        grid=(steps,),
        in_specs=in_specs,
        out_specs=halves
        + [pl.BlockSpec((block, n), spot) for n in (d, width, 2 * width, d)],
    )
    shapes = [(rows, d)] * 2 + [(total, n) for n in (d, width, 2 * width, d)]
    return pl.pallas_call(
        functools.partial(feed_kernel, steps, fresh),
        grid_spec=spec,
        out_shape=[jax.ShapeDtypeStruct(s, low) for s in shapes],
        input_output_aliases={} if fresh else {6 + i: 2 + i for i in range(4)},
        compiler_params=params(),
        cost_estimate=cost(15),
        name="feed_forward",
    )(device, n_a, n_b, cot_all, gateup, down, *(() if fresh else kept))


def weight_kernel(steps, shape, take, give, split, where, x_ref, y_ref, *refs):
    chips, cores, groups = shape
    outputs = 2 if split else groups
    acc_ref = refs[-1]
    out_refs = refs[-1 - outputs : -1]
    step = pl.program_id(0)
    size = x_ref.shape[1]
    product = lax.dot_general(x_ref[...], y_ref[...], TN, preferred_element_type=wide)

    @pl.when(step == 0)
    def _():
        acc_ref[:size] = product
        acc_ref[size:] = jnp.zeros_like(acc_ref[size:])

    @pl.when(step > 0)
    def _():
        acc_ref[:size] += product

    keep = lax.broadcasted_iota(jnp.int32, (give, 1), 0) < take

    def write(mine):
        for chip in range(chips):
            for core in range(cores):
                for group in range(groups):
                    low_edge = ((chip * cores + core) * groups + group) * take
                    value = jnp.where(keep, acc_ref[low_edge : low_edge + give], 0.0).astype(low)
                    if split:
                        at = lax.rem(group + groups - where[2], groups)
                        out_refs[core ^ mine][chip ^ where[1], at] = value
                    else:
                        row = (chip * cores + core) * give
                        out_refs[(group - mine) % groups][row : row + give] = value

    for mine in range(cores if split else groups):
        here = where[0 if split else 2] == mine
        pl.when((step == steps - 1) & here)(functools.partial(write, mine))


def weight_gradient(
    x, y, shape, take, where, split=False, block=1024, column=0, columns=1, into=()
):
    total, size = x.shape
    width = y.shape[1]
    give = padded(take, ROWS)
    block = min(block, total)
    steps = total // block
    chips, cores, groups = shape
    if split:
        out = pl.BlockSpec((chips, groups, give, width), lambda i, w: (0, 0, 0, column))
        shapes = [(chips, groups, give, columns * width)] * 2
    else:
        out = pl.BlockSpec((chips * cores * give, width), lambda i, w: (0, 0))
        shapes = [(chips * cores * give, width)] * groups
    return pl.pallas_call(
        functools.partial(weight_kernel, steps, shape, take, give, split),
        grid_spec=pltpu.PrefetchScalarGridSpec(
            num_scalar_prefetch=1,
            grid=(steps,),
            in_specs=[
                pl.BlockSpec((block, size), lambda i, w: (i, 0)),
                pl.BlockSpec((block, width), lambda i, w: (i, 0)),
            ]
            + [pl.BlockSpec(memory_space=pl.ANY)] * len(into),
            out_specs=[out] * len(shapes),
            scratch_shapes=[pltpu.VMEM((padded(size, 8) + give, width), wide)],
        ),
        out_shape=[jax.ShapeDtypeStruct(shape, low) for shape in shapes],
        input_output_aliases={3 + i: i for i in range(len(into))},
        compiler_params=params(),
        cost_estimate=cost(0.2),
        name="weight_gradient",
    )(where, x, y, *into)


def feed_back_kernel(
    shape, take, give, where, a_ref, b_ref, c_ref, d_ref, middle_ref, inv_ref, gain_ref, cot_ref,
    attn_ref, weight_ref, grad_ref, do_ref, gain_out, keep_ref, send_ref, acc_ref
):
    chips, cores, groups = shape
    size = attn_ref.shape[1]
    step = pl.program_id(0)

    @pl.when(step == 0)
    def _():
        gain_out[...] = jnp.zeros_like(gain_out)
        acc_ref[...] = jnp.zeros_like(acc_ref)

    grad = a_ref[...].astype(wide) + b_ref[...].astype(wide)
    grad = grad + (c_ref[...].astype(wide) + d_ref[...].astype(wide))
    inv = inv_ref[...]
    scaled = middle_ref[...] * inv
    gain_out[...] += jnp.sum(grad * scaled, axis=0, keepdims=True)
    grad = grad * gain_ref[...]
    mean = jnp.sum(grad * scaled, axis=1, keepdims=True) * (1.0 / size)
    grad = cot_ref[...].astype(wide) + inv * (grad - scaled * mean)
    grad_ref[...] = grad
    grad_low = grad.astype(low)
    do_ref[...] = lax.dot_general(
        grad_low, weight_ref[...], NT, preferred_element_type=wide
    ).astype(low)
    acc_ref[:size] += lax.dot_general(attn_ref[...], grad_low, TN, preferred_element_type=wide)
    keep = lax.broadcasted_iota(jnp.int32, (give, 1), 0) < take

    def write(mine):
        for chip in range(chips):
            for core in range(cores):
                for group in range(groups):
                    low_edge = ((chip * cores + core) * groups + group) * take
                    value = jnp.where(keep, acc_ref[low_edge : low_edge + give], 0.0)
                    at = lax.rem(group + groups - where[2], groups)
                    target = send_ref if core ^ mine else keep_ref
                    target[chip ^ where[1], at] = value.astype(low)

    for mine in range(cores):
        here = (step == pl.num_programs(0) - 1) & (where[0] == mine)
        pl.when(here)(functools.partial(write, mine))


def feed_back(shape, take, where, operands):
    chips, cores, groups = shape
    rows, size = operands[8].shape
    give = padded(take, ROWS)
    block = min(256, rows)
    part = lambda n: pl.BlockSpec((block, n), lambda i, w: (i, 0))
    spec = lambda a: part(a.shape[1]) if a.shape[0] == rows else whole(a.shape)
    whole = lambda shape: pl.BlockSpec(shape, lambda i, w: (0,) * len(shape))
    pieces = pl.BlockSpec((chips, groups, give, size), lambda i, w: (0, 0, 0, 1))
    return pl.pallas_call(
        functools.partial(feed_back_kernel, shape, take, give),
        grid_spec=pltpu.PrefetchScalarGridSpec(
            num_scalar_prefetch=1,
            grid=(rows // block,),
            in_specs=[spec(a) for a in operands],
            out_specs=[part(size), part(size), whole((1, size)), pieces, pieces],
            scratch_shapes=[pltpu.VMEM((padded(size, 8) + give, size), wide)],
        ),
        out_shape=[
            jax.ShapeDtypeStruct((rows, size), wide),
            jax.ShapeDtypeStruct((rows, size), low),
            jax.ShapeDtypeStruct((1, size), wide),
        ]
        + [jax.ShapeDtypeStruct((chips, groups, give, 2 * size), low)] * 2,
        compiler_params=params(),
        cost_estimate=cost(1),
        name="feed_back",
    )(where, *operands)


def finish_kernel(
    shape, take, give, cuts, pieces, where, normed_ref, scaled_ref, inv_ref, gain_ref, query_ref,
    query_weight_ref, middle_ref, weight_ref, cos_ref, sin_ref, small_ref, *refs
):
    got_refs = refs[:pieces]
    keep_ref, send_ref, out_ref, acc_ref, row_ref, cut_ref = refs[pieces:]
    chips, cores, groups = shape
    size = normed_ref.shape[1]
    total = got_refs[0][...]
    for ref in got_refs[1:]:
        total = total + ref[...].astype(wide)
    keys, values = total[:, :LANES], total[:, LANES:]
    lane = lax.broadcasted_iota(jnp.int32, keys.shape, 1)
    swapped = jnp.where(
        lane % HD < HD // 2, pltpu.roll(keys, LANES - HD // 2, 1), pltpu.roll(keys, HD // 2, 1)
    )
    keys = keys * cos_ref[...] - swapped * sin_ref[...]
    grads = jnp.concatenate([keys, values], axis=1).astype(low)
    acc_ref[:size] = lax.dot_general(
        normed_ref[...], grads, TN, preferred_element_type=wide
    )
    grad = lax.dot_general(
        query_ref[...], query_weight_ref[...], NT, preferred_element_type=wide
    ) + lax.dot_general(grads, weight_ref[...], NT, preferred_element_type=wide)
    scaled = scaled_ref[...]
    row_ref[:, :size] = jnp.sum(grad * scaled, axis=0, keepdims=True)
    row_ref[:, size : size + small_ref.shape[1]] = small_ref[...]
    row_ref[:, size + small_ref.shape[1] :] = jnp.sum(grads.astype(wide), axis=0, keepdims=True)
    grad = grad * gain_ref[...]
    mean = jnp.sum(grad * scaled, axis=1, keepdims=True) * (1.0 / size)
    out_ref[...] = (middle_ref[...] + inv_ref[...] * (grad - scaled * mean)).astype(low)
    cut_ref[...] = jnp.zeros_like(cut_ref)
    for i in range(chips * cores * groups):
        at = 0
        for first, width in cuts:
            begin = first + i * width
            cut_ref[i : i + 1, at : at + width] = row_ref[:, begin : begin + width]
            at += width
    high = cut_ref[...].astype(low).astype(wide)
    rest = cut_ref[...] - high
    row = lax.broadcasted_iota(jnp.int32, (give, 1), 0)

    def write(mine):
        for chip in range(chips):
            for core in range(cores):
                for group in range(groups):
                    i = (chip * cores + core) * groups + group
                    value = jnp.where(row < take, acc_ref[i * take : i * take + give], 0.0)
                    value = jnp.where(row == take, high[i : i + 1], value)
                    value = jnp.where(row == take + 1, rest[i : i + 1], value)
                    at = lax.rem(group + groups - where[2], groups)
                    target = send_ref if core ^ mine else keep_ref
                    target[chip ^ where[1], at] = value.astype(low)

    for mine in range(cores):
        pl.when(where[0] == mine)(functools.partial(write, mine))


def finish_keyval(shape, take, give, cuts, where, got, operands):
    chips, cores, groups = shape
    rows, size = operands[0].shape
    width = got[0].shape[1]
    total = size + operands[10].shape[1] + width
    whole = lambda a: pl.BlockSpec(a.shape, lambda i, w: (0,) * a.ndim)
    pieces = pl.BlockSpec((chips, groups, give, width), lambda i, w: (0, 0, 0, 0))
    return pl.pallas_call(
        functools.partial(finish_kernel, shape, take, give, cuts, len(got)),
        grid_spec=pltpu.PrefetchScalarGridSpec(
            num_scalar_prefetch=1,
            grid=(1,),
            in_specs=[whole(a) for a in (*operands, *got)],
            out_specs=[pieces, pieces, pl.BlockSpec((rows, size), lambda i, w: (0, 0))],
            scratch_shapes=[
                pltpu.VMEM((padded(size, 8) + give, width), wide),
                pltpu.VMEM((1, total), wide),
                pltpu.VMEM((padded(chips * cores * groups, 8), width), wide),
            ],
        ),
        out_shape=[jax.ShapeDtypeStruct((chips, groups, give, width), low)] * 2
        + [jax.ShapeDtypeStruct((rows, size), low)],
        compiler_params=params(),
        cost_estimate=cost(20),
        name="finish_keyval",
    )(where, *operands, *got)


def place_rows(n_dp, n_group, take, give, device, own_ref, other_ref, at_ref, acc_ref):
    me, mine = device[3], device[2]
    for r in range(n_dp):
        source = own_ref if r % 2 == 0 else other_ref
        for s in range(n_group):
            row = (r // 2 * n_group + s) * give
            z = lax.rem(mine + s, n_group)
            at_ref[(me ^ r) * n_group + z] = source[row : row + give].astype(wide)
    for i in range(n_dp * n_group):
        acc_ref[i * take : i * take + give] = at_ref[i]


def keyval_kernel(
    piece, sizes, device, own_ref, other_ref, tokens_ref, cos_ref, sin_ref, o_ref, small_ref,
    second_ref, inv_ref, scaled_ref, normed_ref, keyval_ref, at_ref, acc_ref
):
    place_rows(*sizes, device, own_ref, other_ref, at_ref, acc_ref)
    count, take = sizes[0] * sizes[1], sizes[2]
    o_ref[...] = acc_ref[: o_ref.shape[0]].astype(low)
    for i in range(count):
        first = at_ref[i, take : take + 1]
        rest = at_ref[i, take + 1 : take + 2]
        cut = slice(i * piece, (i + 1) * piece)
        small_ref[:, cut] = first[:, :piece]
        second_ref[:, cut] = (
            first[:, piece : 2 * piece] + rest[:, :piece] + rest[:, piece : 2 * piece]
        )
    tokens = tokens_ref[...].astype(wide)
    size, width = tokens.shape[1], o_ref.shape[1]
    mean = jnp.sum(tokens * tokens, axis=1, keepdims=True) * (1.0 / size)
    inv = lax.rsqrt(mean + norm_eps)
    inv_ref[...] = inv
    scaled = tokens * inv
    scaled_ref[...] = scaled
    normed = (scaled * small_ref[:, :size]).astype(low)
    normed_ref[...] = normed
    pre = jnp.dot(normed, o_ref[...], preferred_element_type=wide)
    pre = pre + small_ref[:, small_ref.shape[1] - width :]
    keys = pre[:, :LANES]
    lane = lax.broadcasted_iota(jnp.int32, keys.shape, 1)
    swapped = jnp.where(
        lane % HD < HD // 2, pltpu.roll(keys, LANES - HD // 2, 1), pltpu.roll(keys, HD // 2, 1)
    )
    keyval_ref[:, :LANES] = (keys * cos_ref[...] + swapped * sin_ref[...]).astype(low)
    keyval_ref[:, LANES:] = pre[:, LANES:].astype(low)


def project_kernel(
    sizes, device, own_ref, other_ref, normed_ref, bias_ref, o_ref, pre_ref, at_ref, acc_ref
):
    place_rows(*sizes, device, own_ref, other_ref, at_ref, acc_ref)
    o_ref[...] = acc_ref[: o_ref.shape[0]].astype(low)
    pre_ref[...] = (
        jnp.dot(normed_ref[...], o_ref[...], preferred_element_type=wide) + bias_ref[...]
    )


def attend_kernel(
    sizes, device, own_ref, other_ref, attn_ref, tokens_ref, gain_ref, o_ref, low_ref, middle_ref,
    inv_ref, normed_ref, at_ref, acc_ref
):
    place_rows(*sizes, device, own_ref, other_ref, at_ref, acc_ref)
    o_ref[...] = acc_ref[: o_ref.shape[0]].astype(low)
    attn = attn_ref[...].astype(low)
    low_ref[...] = attn
    middle = tokens_ref[...].astype(wide) + jnp.dot(
        attn, o_ref[...], preferred_element_type=wide
    )
    middle_ref[...] = middle
    mean = jnp.sum(middle * middle, axis=1, keepdims=True) * (1.0 / middle.shape[1])
    inv = lax.rsqrt(mean + norm_eps)
    inv_ref[...] = inv
    normed_ref[...] = (middle * inv * gain_ref[...]).astype(low)


def assembled(kernel, name, device, own, other, take, operands, outputs, column=0, columns=1):
    n_dp, n_group = lax.axis_size("dp"), lax.axis_size("group")
    give = own.shape[0] // (n_dp // 2 * n_group)
    width = own.shape[1] // columns
    size = n_dp * n_group * take
    whole = lambda shape: pl.BlockSpec(shape, lambda i, m: (0,) * len(shape))
    outputs = [((size, width), low)] + outputs
    return pl.pallas_call(
        functools.partial(kernel, (n_dp, n_group, take, give)),
        grid_spec=pltpu.PrefetchScalarGridSpec(
            num_scalar_prefetch=1,
            grid=(1,),
            in_specs=[pl.BlockSpec((own.shape[0], width), lambda i, m: (0, column))] * 2
            + [whole(a.shape) for a in operands],
            out_specs=[whole(shape) for shape, _ in outputs],
            scratch_shapes=[
                pltpu.VMEM((n_dp * n_group, give, width), wide),
                pltpu.VMEM((size + give, width), wide),
            ],
        ),
        out_shape=[jax.ShapeDtypeStruct(*output) for output in outputs],
        compiler_params=params(),
        cost_estimate=cost(0.1),
        name=name,
    )(device, own, other, *operands)


def sum_kernel(*refs):
    total = refs[0][...].astype(wide)
    for ref in refs[1:-1]:
        total = total + ref[...].astype(wide)
    refs[-1][...] = total.astype(low)


def sum_pieces(pieces):
    rows, width = pieces[0].shape
    block = rows // 2
    spec = pl.BlockSpec((block, width), lambda i: (i, 0))
    return pl.pallas_call(
        sum_kernel,
        grid=(2,),
        in_specs=[spec] * len(pieces),
        out_specs=spec,
        out_shape=jax.ShapeDtypeStruct((rows, width), low),
        compiler_params=params(),
        cost_estimate=cost(0.1),
        name="sum_pieces",
    )(*pieces)


def return_kernel(near_ref, far_ref, *refs):
    x_a, x_b, y_a, y_b, x_out, y_out = refs
    top = pl.program_id(0) == 0
    near, far = near_ref[...].astype(wide), far_ref[...].astype(wide)
    x_sum = x_a[...].astype(wide) + x_b[...].astype(wide)
    y_sum = y_a[...].astype(wide) + y_b[...].astype(wide)
    x_out[...] = jnp.where(top, x_sum, x_sum + far).astype(low)
    y_out[...] = jnp.where(top, y_sum + near, y_sum).astype(low)


def return_sums(across, x_parts, y_parts):
    half, width = across[0].shape
    spec = pl.BlockSpec((half, width), lambda i: (i, 0))
    one = pl.BlockSpec((half, width), lambda i: (0, 0))
    return pl.pallas_call(
        return_kernel,
        grid=(2,),
        in_specs=[one, one] + [spec] * 4,
        out_specs=[spec] * 2,
        out_shape=[jax.ShapeDtypeStruct((2 * half, width), low)] * 2,
        compiler_params=params(),
        cost_estimate=cost(0.1),
        name="return_sums",
    )(*across, *x_parts, *y_parts)


def pack_kernel(keyval_ref, query_ref, output_ref, small_ref, second_ref, o_ref, buffer_ref):
    rows = query_ref.shape[0]
    piece = small_ref.shape[1]
    buffer_ref[...] = jnp.zeros_like(buffer_ref)
    at = 0
    for ref in (keyval_ref, query_ref, output_ref):
        buffer_ref[:rows, at : at + ref.shape[1]] = ref[...]
        at += ref.shape[1]
    second = second_ref[...]
    first = second.astype(low).astype(wide)
    rest = second - first
    middle = rest.astype(low).astype(wide)
    buffer_ref[rows : rows + 1, :piece] = small_ref[...]
    buffer_ref[rows : rows + 1, piece : 2 * piece] = first
    buffer_ref[rows + 1 : rows + 2, :piece] = middle
    buffer_ref[rows + 1 : rows + 2, piece : 2 * piece] = rest - middle
    o_ref[...] = buffer_ref[...].astype(low)


def pack_rows(keyval, query, output, small, second, give):
    arrays = (keyval, query, output, small[None], second[None])
    width = sum(a.shape[1] for a in arrays[:3])
    return pl.pallas_call(
        pack_kernel,
        grid=(1,),
        in_specs=[pl.BlockSpec(a.shape, lambda i: (0, 0)) for a in arrays],
        out_specs=pl.BlockSpec((give, width), lambda i: (0, 0)),
        out_shape=jax.ShapeDtypeStruct((give, width), low),
        scratch_shapes=[pltpu.VMEM((give, width), wide)],
        compiler_params=params(),
        cost_estimate=cost(0.5),
        name="pack_rows",
    )(*arrays)


def fill_kernel(x_ref, o_ref):
    rows = x_ref.shape[0]
    o_ref[:rows] = x_ref[...]
    o_ref[rows:] = jnp.zeros_like(o_ref[rows:])


def fill_rows(block, rows):
    return pl.pallas_call(
        fill_kernel,
        grid=(1,),
        in_specs=[pl.BlockSpec(block.shape, lambda i: (0, 0))],
        out_specs=pl.BlockSpec((rows, block.shape[1]), lambda i: (0, 0)),
        out_shape=jax.ShapeDtypeStruct((rows, block.shape[1]), block.dtype),
        compiler_params=params(),
        cost_estimate=cost(20),
        name="fill_rows",
    )(block)


def stack_kernel(outer, count, take, give, meta, *refs):
    o_ref, at_ref, acc_ref = refs[count:]
    for s in range(count):
        z = lax.rem(meta[2] + s, count)
        for i in range(outer):
            at_ref[i * count + z] = refs[s][i * give : (i + 1) * give].astype(wide)
    for i in range(outer * count):
        acc_ref[i * take : i * take + give] = at_ref[i]
    size = outer * count * take
    o_ref[:size] = acc_ref[:size].astype(low)
    if o_ref.shape[0] > size:
        o_ref[size:] = jnp.zeros_like(o_ref[size:])


def stack_rows(pieces, outer, take, me, rows):
    count, width = len(pieces), pieces[0].shape[1]
    give = pieces[0].shape[0] // outer
    whole = lambda r: pl.BlockSpec((r, width), lambda i, m: (0, 0))
    return pl.pallas_call(
        functools.partial(stack_kernel, outer, count, take, give),
        grid_spec=pltpu.PrefetchScalarGridSpec(
            num_scalar_prefetch=1,
            grid=(1,),
            in_specs=[whole(outer * give)] * count,
            out_specs=whole(rows),
            scratch_shapes=[
                pltpu.VMEM((outer * count, give, width), wide),
                pltpu.VMEM((padded(outer * count * take, 8) + give, width), wide),
            ],
        ),
        out_shape=jax.ShapeDtypeStruct((rows, width), low),
        compiler_params=params(),
        cost_estimate=cost(1),
        name="stack_rows",
    )(me, *pieces)


def cut_kernel(count, part, part_wide, w_ref, o_ref, buffer_ref):
    rows = w_ref.shape[0]
    buffer_ref[...] = jnp.zeros_like(buffer_ref)
    for p in range(count):
        for j in range(2):
            column = (j * count + p) * part
            buffer_ref[:rows, j * part_wide : j * part_wide + part] = w_ref[
                :, column : column + part
            ]
        o_ref[p] = buffer_ref[...].astype(low)


def cut_columns(weight, count, part_wide, give):
    rows, width = weight.shape
    part = width // (2 * count)
    shape = (count, give, 2 * part_wide)
    return pl.pallas_call(
        functools.partial(cut_kernel, count, part, part_wide),
        grid=(1,),
        in_specs=[pl.BlockSpec(weight.shape, lambda i: (0, 0))],
        out_specs=pl.BlockSpec(shape, lambda i: (0, 0, 0)),
        out_shape=jax.ShapeDtypeStruct(shape, low),
        scratch_shapes=[pltpu.VMEM((give, 2 * part_wide), wide)],
        compiler_params=params(),
        cost_estimate=cost(1),
        name="cut_columns",
    )(weight)


def update_kernel(count, part, part_wide, g_ref, m_ref, v_ref, w_ref, go_ref, vo_ref, wo_ref):
    rows = w_ref.shape[0]
    for p in range(count):
        piece = g_ref[p].astype(wide)
        for j in range(2):
            column = (j * count + p) * part
            go_ref[:, column : column + part] = piece[
                :rows, j * part_wide : j * part_wide + part
            ]
    vo_ref[...], wo_ref[...] = adamw_step(
        go_ref[...], m_ref[...], v_ref[...], w_ref[...], rate_proj, decay_rate
    )


def update_columns(pieces, first, second, weight):
    count, _, width = pieces.shape
    spec = pl.BlockSpec(weight.shape, lambda i: (0, 0))
    return pl.pallas_call(
        functools.partial(
            update_kernel, count, weight.shape[1] // (2 * count), width // 2
        ),
        grid=(1,),
        in_specs=[pl.BlockSpec(pieces.shape, lambda i: (0, 0, 0))] + [spec] * 3,
        out_specs=[spec] * 3,
        out_shape=[jax.ShapeDtypeStruct(weight.shape, wide)] * 3,
        compiler_params=params(),
        cost_estimate=cost(1),
        name="update_columns",
    )(pieces, first, second, weight)


def flip(value, mask):
    count = lax.axis_size("dp")
    return lax.ppermute(value, "dp", [(i, i ^ mask) for i in range(count)])


def shift(value, step):
    count = lax.axis_size("group")
    return lax.ppermute(value, "group", [((i + step) % count, i) for i in range(count)])


def shift_within(value, step):
    count = lax.axis_size("group")
    pairs = [(i + step, i) for i in range(count) if 0 <= i + step < count]
    return lax.ppermute(value, "group", pairs)


def after(value, *others):
    return lax.optimization_barrier((value, *others))[0]


def group_pieces(block, steps=None):
    return [block] + [shift(block, s) for s in range(1, lax.axis_size("group"))]


def group_send(blocks):
    count = lax.axis_size("group")
    return [blocks[0]] + [shift(blocks[count - s].astype(low), s) for s in range(1, count)]


def add_up(terms):
    return functools.reduce(jnp.add, [term.astype(wide) for term in terms])


def gather_chips(column):
    evens = [column] + [flip(column, r) for r in range(2, lax.axis_size("dp"), 2)]
    return jnp.concatenate(evens, axis=0)


def scatter_pair(keep, send):
    return keep.astype(wide) + flip(send, 1).astype(wide)


def scatter_chips(pair):
    got = [flip(pair[r].astype(low), 2 * r) for r in range(1, pair.shape[0])]
    return add_up([pair[0]] + got)


def body(
    tokens,
    positions,
    cotangent,
    query_weight,
    query_first,
    query_second,
    keyval_weight,
    keyval_first,
    keyval_second,
    output_weight,
    output_first,
    output_second,
    gateup_weight,
    gateup_first,
    gateup_second,
    down_weight,
    down_first,
    down_second,
    small_weight,
    small_first,
    small_second,
):
    row_count = tokens.shape[0]
    half = row_count // 2
    n_dp = lax.axis_size("dp")
    group_size = lax.axis_size("group")
    device_count = n_dp * group_size
    my_dp = lax.axis_index("dp")
    my_index = lax.axis_index("group")
    flat_index = my_dp * group_size + my_index
    seq_len = row_count * group_size
    query_width = HQ * HD
    kv_width = HK * HD
    small_size = 2 * D + query_width + 2 * kv_width
    rest_length = small_size - kv_width
    rest_piece = rest_length // device_count
    value_piece = kv_width // device_count
    small_piece = small_size // device_count
    part = FF // n_dp
    part_wide = padded(part, LANES)
    in_rows = query_weight.shape[0]
    device = jnp.stack([my_dp & 1, my_dp >> 1, my_index, my_dp]).astype(jnp.int32)
    in_give = padded(in_rows + 2, ROWS)
    down_rows = down_weight.shape[0]

    every_block = pack_rows(
        keyval_weight, query_weight, output_weight, small_weight, small_second, in_give
    )
    place_row = positions[0]
    local_index = my_index * row_count + jnp.arange(row_count, dtype=jnp.int32)
    local_places = lax.dynamic_slice_in_dim(place_row, my_index * row_count, row_count, 0)
    starts = (local_index - local_places).reshape(2, half).astype(jnp.int32)
    starts = jnp.broadcast_to(starts[:, None, :], (2, 8, half))
    angles = rotary_angles(local_places)
    cosine, sine_table = jnp.cos(angles), jnp.sin(angles)
    cos_wide = jnp.concatenate([cosine] * 4, axis=1)
    sin_wide = jnp.concatenate([-sine_table, sine_table] * 2, axis=1)

    gateup_pieces = cut_columns(gateup_weight, n_dp, part_wide, in_give)
    every_pieces = group_pieces(every_block)
    every_pieces, cos_wide, sin_wide = after((every_pieces, cos_wide, sin_wide), gateup_pieces)
    every_column = jnp.concatenate(every_pieces, axis=0)
    keyval_column = every_column[:, : 2 * kv_width]
    both_column = every_column[:, 2 * kv_width :]
    keyval_own = gather_chips(keyval_column)
    down_part = lax.all_gather(down_weight.astype(low), "group", axis=0, tiled=True)

    keyval_full, small_row, second_row, inv_one, scaled_one, normed_one, keyval_low = assembled(
        functools.partial(keyval_kernel, small_piece), "project_keyval", device,
        keyval_own, flip(keyval_own, 1), in_rows, (tokens, cos_wide, sin_wide),
        [
            ((1, small_size), wide),
            ((1, small_size), wide),
            ((row_count, 1), wide),
            ((row_count, D), wide),
            ((row_count, D), low),
            ((row_count, 2 * kv_width), low),
        ],
    )
    gain_one, gain_two = small_row[:, :D], small_row[:, D : 2 * D]
    bias_query = small_row[:, 2 * D : 2 * D + query_width]
    keyval_parts = [keyval_low] + [shift_within(keyval_low, -s) for s in range(1, group_size)]
    both_own = gather_chips(after(both_column, keyval_low))
    gateup_column = lax.all_to_all(after(gateup_pieces, keyval_low), "dp", 0, 0, tiled=True)
    gateup_column = gateup_column.reshape(n_dp * in_give, 2 * part_wide)
    keyval_parts, down_part = after((keyval_parts, down_part))
    down_part = fill_rows(down_part, part_wide)
    both_own, gateup_column, down_part = after((both_own, gateup_column, down_part))
    cot_all = lax.all_gather(after(cotangent, both_own), "dp", axis=0, tiled=True)
    both_other = flip(both_own, 1)
    query_full, query_pre = assembled(
        project_kernel, "project_query", device, both_own, both_other, in_rows,
        (normed_one, bias_query), [((row_count, query_width), wide)], 0, 2,
    )
    gateup_pieces = group_pieces(gateup_column)
    attn_float, log_total, query_low = attention_forward(
        query_pre, cos_wide, sin_wide, starts, keyval_parts, device
    )
    output_full, attn_low, middle, inv_two, normed_two = assembled(
        attend_kernel, "attention_output", device, both_own, both_other, in_rows,
        (attn_float, tokens, gain_two),
        [
            ((row_count, query_width), low),
            ((row_count, D), wide),
            ((row_count, 1), wide),
            ((row_count, D), low),
        ],
        1, 2,
    )

    normed_two, gateup_pieces = after((normed_two, gateup_pieces))
    gateup_part = stack_rows(gateup_pieces, n_dp, in_rows, device, D)
    chips = n_dp // 2
    pieces, down_shape = (chips, 2, group_size), (1, 1, group_size)
    kept, sides, back = None, {0: normed_two}, {}
    for k in range(1, chips):
        if n_dp != 8 or k != 3:
            sides[k] = flip(normed_two, 2 * k)

    def visit(k, kept):
        back_a, back_b, *kept = feed_forward(
            sides[k], flip(sides[k], 1), cot_all, gateup_part, down_part, device, kept, k
        )
        back[k] = (back_a, flip(back_b, 1))
        return kept

    if n_dp == 8:
        kept = visit(0, kept)
        sides[1], sides[2] = after((sides[1], sides[2]), kept)
        across = [flip(sides[1][:half], 4), flip(sides[2][half:], 2)]
        kept = visit(1, kept)
        sides[3] = jnp.concatenate(after(across, kept), axis=0)
        kept = visit(3, kept)
        corner = add_up(back[3]).astype(low)
        across = [flip(corner[:half], 2), flip(corner[half:], 4)]
        kept = visit(2, kept)
        down_term = weight_gradient(kept[1], cot_all, down_shape, down_rows, device)
        across = after(across, down_term)
        x_sum, y_sum = return_sums(across, back[1], back[2])
        kept, y_sum = after((kept, y_sum))
        returned = [*back[0], flip(x_sum, 2), flip(y_sum, 4)]
    else:
        for k in range(chips):
            kept = visit(k, kept)
        down_term = weight_gradient(kept[1], cot_all, down_shape, down_rows, device)
        returned = list(back[0])
        returned += [flip(add_up(back[k]).astype(low), 2 * k) for k in range(1, chips)]
    out_all, _, gate_all, normed_all = kept
    down_got = group_send(down_term)
    gateup_term = weight_gradient(normed_all, gate_all, pieces, in_rows, device)
    gateup_got = group_send(gateup_term)
    returned, gateup_got[0], early = after((returned, gateup_got[0], down_got[1:-1]))
    down_got[1:-1] = early
    out_sum = lax.psum_scatter(after(out_all, returned), "dp", scatter_dimension=0, tiled=True)

    if len(returned) > 4:
        returned = returned[:3] + [add_up(returned[3:])]
    grad_middle, grad_attn_low, gain_two_term, *both_terms = feed_back(
        pieces,
        in_rows,
        device,
        (
            *returned,
            middle,
            inv_two,
            gain_two,
            cotangent,
            attn_low,
            output_full,
        ),
    )
    grad_query_pre, *keyval_terms = attention_backward(
        query_low,
        grad_attn_low,
        attn_float,
        log_total,
        starts,
        cosine.T,
        sine_table.T,
        keyval_parts,
        device,
    )
    both_terms = weight_gradient(
        normed_one, grad_query_pre, pieces, in_rows, device, split=True, columns=2, into=both_terms
    )
    keyval_terms, both_terms, gateup_got, down_got = after(
        (keyval_terms, both_terms, gateup_got, down_got)
    )
    keyval_got = [keyval_terms[0]]
    keyval_got += [shift_within(keyval_terms[s], s) for s in range(1, group_size)]
    both_pair = scatter_pair(both_terms[0], after(both_terms[1], out_sum))
    both_total = scatter_chips(both_pair)
    gateup_sum = sum_pieces(gateup_got).reshape(n_dp, -1, 2 * part_wide)
    gateup_sum = lax.all_to_all(gateup_sum, "dp", 0, 0, tiled=True)
    keyval_got, gateup_sum = after((keyval_got, gateup_sum), both_pair)
    bias_term = jnp.sum(grad_query_pre.astype(wide), axis=0)
    *last_terms, tokens_grad = finish_keyval(
        pieces,
        in_rows,
        in_give,
        ((0, small_piece), (0, rest_piece), (rest_length, value_piece)),
        device,
        keyval_got,
        (
            normed_one,
            scaled_one,
            inv_one,
            gain_one,
            grad_query_pre,
            query_full,
            grad_middle,
            keyval_full,
            cos_wide,
            sin_wide,
            jnp.concatenate([gain_two_term, bias_term[None]], axis=1),
        ),
    )
    small_width = small_piece + rest_piece + value_piece
    gateup_grad, gateup_second_out, gateup_weight_out = update_columns(
        after(gateup_sum, last_terms), gateup_first, gateup_second, gateup_weight
    )
    last_terms, gateup_second_out = after((last_terms, gateup_second_out), both_total)
    last_total = scatter_chips(scatter_pair(*last_terms))
    down_got = after(down_got, last_total)
    late_middle, out_sum = after((middle, out_sum), last_total)
    layer_out = (late_middle + out_sum.astype(wide)).astype(low)
    down_grad = add_up(down_got)[:down_rows]
    some = last_total.shape[1] - both_total.shape[1]
    both_total = jnp.pad(both_total, ((0, 0), (0, some), (0, 0)))
    down_second_out, down_weight_out = adamw_step(
        down_grad, down_first, down_second, down_weight, rate_proj, decay_rate
    )
    every_got = group_send(jnp.concatenate([both_total, last_total], axis=2))
    every_got, down_second_out, layer_out = after((every_got, down_second_out, layer_out))
    every_sum = add_up(every_got)
    query_grad = every_sum[:in_rows, :query_width]
    output_grad = every_sum[:in_rows, query_width : query_width + D]
    last_sum = every_sum[:, query_width + D :]
    keyval_grad = last_sum[:in_rows]
    small_sum = last_sum[in_rows, :small_width] + last_sum[in_rows + 1, :small_width]
    small_grad = small_sum[:small_piece]
    rest_grad = small_sum[small_piece : small_piece + rest_piece]
    value_grad = small_sum[small_piece + rest_piece :]

    query_second_out, query_weight_out = adamw_step(
        query_grad, query_first, query_second, query_weight, rate_proj, decay_rate
    )
    keyval_second_out, keyval_weight_out = adamw_step(
        keyval_grad, keyval_first, keyval_second, keyval_weight, rate_proj, decay_rate
    )
    output_second_out, output_weight_out = adamw_step(
        output_grad, output_first, output_second, output_weight, rate_out, decay_rate
    )
    _, small_weight_out = adamw_step(
        small_grad, small_first, small_second, small_weight, rate_small, 0.0
    )
    rest_second = lax.dynamic_slice_in_dim(
        second_row[0], flat_index * rest_piece, rest_piece, 0
    )
    value_second = lax.dynamic_slice_in_dim(
        second_row[0], rest_length + flat_index * value_piece, value_piece, 0
    )
    small_second_out = beta_two * rest_second + (1.0 - beta_two) * rest_grad * rest_grad
    value_bias_second_out = beta_two * value_second + (1.0 - beta_two) * value_grad * value_grad
    return (
        layer_out,
        tokens_grad,
        query_grad,
        query_second_out,
        query_weight_out,
        keyval_grad,
        keyval_second_out,
        keyval_weight_out,
        output_grad,
        output_second_out,
        output_weight_out,
        gateup_grad,
        gateup_second_out,
        gateup_weight_out,
        down_grad,
        down_second_out,
        down_weight_out,
        small_grad,
        small_second_out,
        value_bias_second_out,
        small_weight_out,
    )


def solution(mesh):
    rows = P(("dp", "group"), None)
    line = P(("dp", "group"))
    in_specs = (rows, P("dp", None)) + (rows,) * 16 + (line,) * 3
    out_specs = (rows,) * 17 + (line,) * 4
    return jax.shard_map(body, mesh=mesh, in_specs=in_specs, out_specs=out_specs, check_vma=False)
```

```python
import functools

import jax
import jax.numpy as jnp
from jax import lax
from jax.experimental import pallas as pl
from jax.experimental.pallas import tpu as pltpu
from jax.sharding import PartitionSpec as P

D = 896
HQ = 14
HK = 2
HD = 64
FF = 4864
STEP = 10


theta_base = 1000000.0
norm_eps = 1e-06
beta_one = 0.9
beta_two = 0.95
adam_eps = 1e-08
decay_rate = 0.1
rate_proj = 0.02
rate_out = 0.5
rate_small = 0.2
masked_score = -1e30

low = jnp.bfloat16
wide = jnp.float32


MIB = 1024 * 1024
LANES = 128
ROWS = 16
NT = (((1,), (1,)), ((), ()))
TN = (((0,), (0,)), ((), ()))


def padded(size, unit):
    return -(-size // unit) * unit


def rotary_angles(places):
    half_size = HD // 2
    inv_freq = theta_base ** (-(jnp.arange(half_size, dtype=wide) * 2.0) / HD)
    return places.astype(wide)[:, None] * inv_freq[None, :]


def adamw_step(gradient, first_old, second_old, weight, step_rate, decay_factor):
    first_new = beta_one * first_old + (1.0 - beta_one) * gradient
    second_new = beta_two * second_old + (1.0 - beta_two) * gradient * gradient
    first_hat = first_new / (1.0 - beta_one**STEP)
    second_hat = second_new / (1.0 - beta_two**STEP)
    updated = weight - step_rate * (
        first_hat / (jnp.sqrt(second_hat) + adam_eps) + decay_factor * weight
    )
    return (second_new, updated)


def params(limit=56):
    return pltpu.CompilerParams(
        vmem_limit_bytes=limit * MIB, dimension_semantics=("arbitrary",)
    )


def cost(micros):
    return pl.CostEstimate(flops=int(micros * 10**9), bytes_accessed=10**6, transcendentals=0)


def split_heads(pair, number):
    lane = lax.broadcasted_iota(jnp.int32, pair.shape, 1)
    zero = jnp.zeros_like(pair)
    turned = pltpu.roll(pair, HD, 1)
    low_a = 2 * number < HQ // HK
    low_b = 2 * number + 1 < HQ // HK
    first = jnp.where((lane < HD) == low_a, jnp.where(low_a, pair, turned), zero)
    second = jnp.where((lane < HD) == low_b, jnp.where(low_b, turned, pair), zero)
    return jnp.concatenate([first, second], axis=0)


def join_heads(both, number, half):
    low_a = 2 * number < HQ // HK
    low_b = 2 * number + 1 < HQ // HK
    first = jnp.where(low_a, both[:HD, :half], both[HD:, :half])
    second = jnp.where(low_b, both[:HD, half:], both[HD:, half:])
    return first, second


def key_mask(start, first_key, first_query, half, causal):
    key_row = lax.broadcasted_iota(jnp.int32, (half, half), 0)
    ok = key_row >= start - first_key
    if causal:
        ok &= key_row <= lax.broadcasted_iota(jnp.int32, (1, half), 1) + (first_query - first_key)
    return jnp.concatenate([ok, ok], axis=1)


def query_mask(start, first_key, first_query, half, causal):
    key = lax.broadcasted_iota(jnp.int32, (half, half), 1)
    ok = key >= jnp.concatenate([start - first_key] * (half // LANES), axis=1)
    if causal:
        ok &= key <= lax.broadcasted_iota(jnp.int32, (half, half), 0) + (first_query - first_key)
    return jnp.concatenate([ok, ok], axis=0)


def visit_blocks(meta, start_ref, half, pieces, visit):
    mine = meta[2]
    first_query = mine * 2 * half
    turned = start_ref.shape[2] == LANES
    mask_of = query_mask if turned else key_mask
    start_of = lambda sel: start_ref[sel] if turned else start_ref[sel, 0:1, :]
    for sel, block in ((0, 0), (1, 0), (1, 1)):
        mask = mask_of(
            start_of(sel), first_query + block * half, first_query + sel * half, half, sel == block
        )
        visit(sel, 0, block, 1, mask)
    for piece in range(1, pieces):
        first_key = (mine - piece) * 2 * half

        def region(cut):
            axis = 0 if turned else 1
            for sel in range(2):
                if cut:
                    mask = mask_of(start_of(sel), first_key, first_query, half, False)
                    visit(sel, piece, 0, 1, mask)
                    mask = start_of(sel) <= first_key + half
                    visit(sel, piece, 1, 1, jnp.concatenate([mask, mask], axis=axis))
                else:
                    mask = start_of(sel) <= first_key
                    visit(sel, piece, 0, 2, jnp.concatenate([mask, mask], axis=axis))

        pl.when(mine == piece)(functools.partial(region, True))
        pl.when(mine > piece)(functools.partial(region, False))


def forward_kernel(pieces, meta, pre_ref, cos_ref, sin_ref, start_ref, starts_ref, *refs):
    kv_refs = refs[:pieces]
    o_ref, lse_ref, q_ref, two_ref, top_ref, sum_ref, acc_ref = refs[pieces:]
    number = pl.program_id(0)
    rows = pre_ref.shape[0]
    half = rows // 2
    pre = pre_ref[...]
    lane = lax.broadcasted_iota(jnp.int32, pre.shape, 1)
    swapped = jnp.where(
        lane % HD < HD // 2, pltpu.roll(pre, LANES - HD // 2, 1), pltpu.roll(pre, HD // 2, 1)
    )
    turned = (pre * cos_ref[...] + swapped * sin_ref[...]).astype(low)
    turned = (turned.astype(wide) * (1.0 / HD**0.5)).astype(low)
    q_ref[...] = turned
    for which in range(2):
        two_ref[which] = split_heads(turned[which * half : (which + 1) * half, :], number)
    top_ref[...] = jnp.full_like(top_ref, masked_score)
    sum_ref[...] = jnp.zeros_like(sum_ref)
    acc_ref[...] = jnp.zeros_like(acc_ref)

    def scores_of(sel, piece, block, count):
        part = slice(block * half, (block + count) * half)
        return lax.dot_general(
            two_ref[sel], kv_refs[piece][part, :LANES], NT, preferred_element_type=wide
        )

    def find_top(sel, piece, block, count, mask):
        scores = scores_of(sel, piece, block, count)
        if mask.shape[1] > LANES:
            scores = jnp.where(mask, scores, masked_score)
        peak = functools.reduce(jnp.maximum, [scores[:, i : i + LANES] for i in range(0, count * half, LANES)])
        if mask.shape[1] <= LANES:
            peak = jnp.where(mask, peak, masked_score)
        top_ref[sel] = jnp.maximum(top_ref[sel], peak)

    def sum_up(sel, piece, block, count, mask):
        part = slice(block * half, (block + count) * half)
        scores = scores_of(sel, piece, block, count)
        level = top_ref[sel]
        if mask.shape[1] > LANES:
            scores = jnp.where(mask, scores, masked_score)
        else:
            level = jnp.where(mask, level, -masked_score)
        weights = [jnp.exp(scores[:, i : i + LANES] - level) for i in range(0, count * half, LANES)]
        sum_ref[sel] += functools.reduce(jnp.add, weights)
        acc_ref[sel] += jnp.dot(
            jnp.concatenate(weights, axis=1).astype(low),
            kv_refs[piece][part, LANES:],
            preferred_element_type=wide,
        )

    visit_blocks(meta, starts_ref, half, pieces, find_top)
    for which in range(2):
        top_ref[which] = jnp.broadcast_to(
            jnp.max(top_ref[which], axis=1, keepdims=True), top_ref.shape[1:]
        )
    visit_blocks(meta, starts_ref, half, pieces, sum_up)
    lane = lax.broadcasted_iota(jnp.int32, (half, LANES), 1)
    low_a = 2 * number < HQ // HK
    low_b = 2 * number + 1 < HQ // HK
    pick = jnp.where(lax.broadcasted_iota(jnp.int32, (8, LANES), 1) == 0, 1.0, 0.0).astype(wide)
    for which in range(2):
        total = jnp.sum(sum_ref[which], axis=1, keepdims=True)
        out = acc_ref[which] / total
        first, second = out[:half], out[half:]
        first = jnp.where(low_a, first, pltpu.roll(first, HD, 1))
        second = jnp.where(low_b, pltpu.roll(second, HD, 1), second)
        o_ref[which * half : (which + 1) * half, :] = jnp.where(lane < HD, first, second)
        lse = top_ref[which] + jnp.log(total)
        lse_ref[0, :, which * rows : (which + 1) * rows] = lax.dot_general(
            pick, lse, NT, precision=lax.Precision.HIGHEST, preferred_element_type=wide
        )


def attention_forward(pre, cos_wide, sin_wide, starts, kv_pieces, meta):
    rows, width = pre.shape
    pairs, pieces = width // LANES, len(kv_pieces)
    pair = pl.BlockSpec((rows, LANES), lambda p, m: (0, p))
    whole = lambda a: pl.BlockSpec(a.shape, lambda p, m: (0,) * a.ndim)
    starts_wide = jnp.broadcast_to(starts[:, 0, :, None], (2, rows // 2, LANES))
    operands = (cos_wide, sin_wide, starts, starts_wide, *kv_pieces)
    spec = pltpu.PrefetchScalarGridSpec(
        num_scalar_prefetch=1,
        grid=(pairs,),
        in_specs=[pair] + [whole(a) for a in operands],
        out_specs=[pair, pl.BlockSpec((1, 8, 2 * rows), lambda p, m: (p, 0, 0)), pair],
        scratch_shapes=[
            pltpu.VMEM((2, rows, LANES), low),
            pltpu.VMEM((2, rows, LANES), wide),
            pltpu.VMEM((2, rows, LANES), wide),
            pltpu.VMEM((2, rows, LANES), wide),
        ],
    )
    return pl.pallas_call(
        functools.partial(forward_kernel, pieces),
        grid_spec=spec,
        out_shape=[
            jax.ShapeDtypeStruct((rows, width), wide),
            jax.ShapeDtypeStruct((pairs, 8, 2 * rows), wide),
            jax.ShapeDtypeStruct((rows, width), low),
        ],
        compiler_params=params(48),
        cost_estimate=cost(40),
        name="attention_forward",
    )(meta, pre, *operands)


def backward_kernel(pieces, meta, q_ref, do_ref, o_ref, lse_ref, start_ref, cos_ref, sin_ref, *refs):
    kv_refs = refs[:pieces]
    dq_ref = refs[pieces]
    out_refs = refs[pieces + 1 : 2 * pieces + 1]
    kt_ref, two_ref, dot_ref, delta_ref, acc_ref, dkv_ref = refs[2 * pieces + 1 :]
    number = pl.program_id(0)
    rows = q_ref.shape[0]
    half = rows // 2

    @pl.when(number == 0)
    def _():
        dkv_ref[...] = jnp.zeros_like(dkv_ref)
        for piece in range(pieces):
            kt_ref[piece] = kv_refs[piece][:, :LANES].astype(wide).T.astype(low)

    acc_ref[...] = jnp.zeros_like(acc_ref)
    lane = lax.broadcasted_iota(jnp.int32, (8, LANES), 1)
    pick_a = jnp.where(lane < HD, 1.0, 0.0).astype(wide)
    pick_b = 1.0 - pick_a
    for which in range(2):
        part = slice(which * half, (which + 1) * half)
        two_ref[which] = split_heads(q_ref[part, :], number)
        dot_ref[which] = split_heads(do_ref[part, :], number)
        product = do_ref[part, :].astype(wide) * o_ref[part, :]
        delta_ref[which] = jnp.concatenate(
            [
                lax.dot_general(
                    pick, product, NT, precision=lax.Precision.HIGHEST, preferred_element_type=wide
                )
                for pick in (pick_a, pick_b)
            ],
            axis=1,
        )

    def visit(sel, piece, block, count, mask):
        part = slice(block * half, (block + count) * half)
        two, dot = two_ref[sel], dot_ref[sel]
        keys, values = kv_refs[piece][part, :LANES], kv_refs[piece][part, LANES:]
        scores = lax.dot_general(keys, two, NT, preferred_element_type=wide)
        grad_weights = lax.dot_general(values, dot, NT, preferred_element_type=wide)
        lse = lse_ref[0, 0:1, sel * rows : (sel + 1) * rows]
        if mask.shape[0] > 1:
            weights = jnp.where(mask, jnp.exp(scores - lse), 0.0)
        else:
            weights = jnp.exp(scores - jnp.where(mask, lse, -masked_score))
        grad_scores = (weights * (grad_weights - delta_ref[sel, 0:1, :])).astype(low)
        dkv_ref[piece, part, LANES:] += jnp.dot(
            weights.astype(low), dot, preferred_element_type=wide
        )
        dkv_ref[piece, part, :LANES] += jnp.dot(grad_scores, two, preferred_element_type=wide)
        acc_ref[sel] += jnp.dot(kt_ref[piece, :, part], grad_scores, preferred_element_type=wide)

    visit_blocks(meta, start_ref, half, pieces, visit)
    for which in range(2):
        part = slice(which * half, (which + 1) * half)
        cos, sin = cos_ref[:, part], sin_ref[:, part]
        turned = []
        for head in join_heads(acc_ref[which] * (1.0 / HD**0.5), number, half):
            upper, lower = head[: HD // 2], head[HD // 2 :]
            turned += [upper * cos + lower * sin, lower * cos - upper * sin]
        dq_ref[part, :] = jnp.concatenate(turned, axis=0).T.astype(low)

    @pl.when(number == pl.num_programs(0) - 1)
    def _():
        for piece in range(pieces):
            out_refs[piece][...] = dkv_ref[piece].astype(out_refs[piece].dtype)


def attention_backward(q, do, o, lse, starts, cos_turned, sin_turned, kv_pieces, meta):
    rows, width = q.shape
    pairs, pieces = width // LANES, len(kv_pieces)
    pair = pl.BlockSpec((rows, LANES), lambda p, m: (0, p))
    whole = lambda a: pl.BlockSpec(a.shape, lambda p, m: (0,) * a.ndim)
    fixed = (starts, cos_turned, sin_turned, *kv_pieces)
    spec = pltpu.PrefetchScalarGridSpec(
        num_scalar_prefetch=1,
        grid=(pairs,),
        in_specs=[pair, pair, pair, pl.BlockSpec((1, 8, 2 * rows), lambda p, m: (p, 0, 0))]
        + [whole(a) for a in fixed],
        out_specs=[pair] + [whole(a) for a in kv_pieces],
        scratch_shapes=[
            pltpu.VMEM((pieces, LANES, rows), low),
            pltpu.VMEM((2, rows, LANES), low),
            pltpu.VMEM((2, rows, LANES), low),
            pltpu.VMEM((2, 8, rows), wide),
            pltpu.VMEM((2, LANES, rows), wide),
            pltpu.VMEM((pieces, rows, 2 * LANES), wide),
        ],
    )
    return pl.pallas_call(
        functools.partial(backward_kernel, pieces),
        grid_spec=spec,
        out_shape=[jax.ShapeDtypeStruct((rows, width), low)]
        + [
            jax.ShapeDtypeStruct((rows, 2 * LANES), wide if piece == 0 else low)
            for piece in range(pieces)
        ],
        compiler_params=params(48),
        cost_estimate=cost(40),
        name="attention_backward",
    )(meta, q, do, o, lse, *fixed)


def feed_kernel(
    steps, fresh, device, n_a, n_b, cot_ref, gateup_ref, down_ref, *refs
):
    refs = refs[0 if fresh else 4 :]
    back_a, back_b, out_ref, hidden_ref, grad_ref, kept_ref = refs
    width = down_ref.shape[0]
    first = pl.program_id(0) < steps // 2
    normed = jnp.where(first, n_a[...], n_b[...])
    cot = cot_ref[...]
    gate = jnp.dot(normed, gateup_ref[:, :width], preferred_element_type=wide)
    up = jnp.dot(normed, gateup_ref[:, width:], preferred_element_type=wide)
    grad_hidden = lax.dot_general(cot, down_ref[...], NT, preferred_element_type=wide)
    sigmoid = jax.nn.sigmoid(gate)
    act = gate * sigmoid
    hidden = (act * up).astype(low)
    grad_gate = (grad_hidden * up * sigmoid * (1.0 + gate * (1.0 - sigmoid))).astype(low)
    grad_up = (grad_hidden * act).astype(low)
    kept_ref[...] = normed
    hidden_ref[...] = hidden
    grad_ref[:, :width] = grad_gate
    grad_ref[:, width:] = grad_up
    out_ref[...] = jnp.dot(hidden, down_ref[...], preferred_element_type=wide).astype(low)
    back = lax.dot_general(grad_gate, gateup_ref[:, :width], NT, preferred_element_type=wide)
    back = back + lax.dot_general(grad_up, gateup_ref[:, width:], NT, preferred_element_type=wide)

    @pl.when(first)
    def _():
        back_a[...] = back.astype(low)

    @pl.when(jnp.logical_not(first))
    def _():
        back_b[...] = back.astype(low)


def feed_forward(n_a, n_b, cot_all, gateup, down, device, kept, chip, block=256):
    rows, d = n_a.shape
    total, width = cot_all.shape[0], down.shape[0]
    block = min(block, rows)
    each = rows // block
    steps = 2 * each
    spot = lambda i, device: ((device[3] ^ (2 * chip + i // each)) * each + i % each, 0)
    whole = lambda a: pl.BlockSpec(a.shape, lambda i, device: (0, 0))
    halves = [
        pl.BlockSpec((block, d), lambda i, device: (jnp.minimum(i, each - 1), 0)),
        pl.BlockSpec((block, d), lambda i, device: (jnp.maximum(i - each, 0), 0)),
    ]
    in_specs = halves + [
        pl.BlockSpec((block, d), spot),
        whole(gateup),
        whole(down),
    ]
    fresh = kept is None
    if not fresh:
        in_specs += [pl.BlockSpec(memory_space=pl.ANY)] * 4
    spec = pltpu.PrefetchScalarGridSpec(
        num_scalar_prefetch=1,
        grid=(steps,),
        in_specs=in_specs,
        out_specs=halves
        + [pl.BlockSpec((block, n), spot) for n in (d, width, 2 * width, d)],
    )
    shapes = [(rows, d)] * 2 + [(total, n) for n in (d, width, 2 * width, d)]
    return pl.pallas_call(
        functools.partial(feed_kernel, steps, fresh),
        grid_spec=spec,
        out_shape=[jax.ShapeDtypeStruct(s, low) for s in shapes],
        input_output_aliases={} if fresh else {6 + i: 2 + i for i in range(4)},
        compiler_params=params(),
        cost_estimate=cost(15),
        name="feed_forward",
    )(device, n_a, n_b, cot_all, gateup, down, *(() if fresh else kept))


def weight_kernel(steps, shape, take, give, split, where, x_ref, y_ref, *refs):
    chips, cores, groups = shape
    outputs = 2 if split else groups
    acc_ref = refs[-1]
    out_refs = refs[-1 - outputs : -1]
    step = pl.program_id(0)
    size = x_ref.shape[1]
    product = lax.dot_general(x_ref[...], y_ref[...], TN, preferred_element_type=wide)

    @pl.when(step == 0)
    def _():
        acc_ref[:size] = product
        acc_ref[size:] = jnp.zeros_like(acc_ref[size:])

    @pl.when(step > 0)
    def _():
        acc_ref[:size] += product

    keep = lax.broadcasted_iota(jnp.int32, (give, 1), 0) < take

    def write(mine):
        for chip in range(chips):
            for core in range(cores):
                for group in range(groups):
                    low_edge = ((chip * cores + core) * groups + group) * take
                    value = jnp.where(keep, acc_ref[low_edge : low_edge + give], 0.0).astype(low)
                    if split:
                        at = lax.rem(group + groups - where[2], groups)
                        out_refs[core ^ mine][chip ^ where[1], at] = value
                    else:
                        row = (chip * cores + core) * give
                        out_refs[(group - mine) % groups][row : row + give] = value

    for mine in range(cores if split else groups):
        here = where[0 if split else 2] == mine
        pl.when((step == steps - 1) & here)(functools.partial(write, mine))


def weight_gradient(
    x, y, shape, take, where, split=False, block=1024, column=0, columns=1, into=()
):
    total, size = x.shape
    width = y.shape[1]
    give = padded(take, ROWS)
    block = min(block, total)
    steps = total // block
    chips, cores, groups = shape
    if split:
        out = pl.BlockSpec((chips, groups, give, width), lambda i, w: (0, 0, 0, column))
        shapes = [(chips, groups, give, columns * width)] * 2
    else:
        out = pl.BlockSpec((chips * cores * give, width), lambda i, w: (0, 0))
        shapes = [(chips * cores * give, width)] * groups
    return pl.pallas_call(
        functools.partial(weight_kernel, steps, shape, take, give, split),
        grid_spec=pltpu.PrefetchScalarGridSpec(
            num_scalar_prefetch=1,
            grid=(steps,),
            in_specs=[
                pl.BlockSpec((block, size), lambda i, w: (i, 0)),
                pl.BlockSpec((block, width), lambda i, w: (i, 0)),
            ]
            + [pl.BlockSpec(memory_space=pl.ANY)] * len(into),
            out_specs=[out] * len(shapes),
            scratch_shapes=[pltpu.VMEM((padded(size, 8) + give, width), wide)],
        ),
        out_shape=[jax.ShapeDtypeStruct(shape, low) for shape in shapes],
        input_output_aliases={3 + i: i for i in range(len(into))},
        compiler_params=params(),
        cost_estimate=cost(0.2),
        name="weight_gradient",
    )(where, x, y, *into)


def feed_back_kernel(
    shape, take, give, where, a_ref, b_ref, c_ref, d_ref, middle_ref, inv_ref, gain_ref, cot_ref,
    attn_ref, weight_ref, grad_ref, do_ref, gain_out, keep_ref, send_ref, acc_ref
):
    chips, cores, groups = shape
    size = attn_ref.shape[1]
    step = pl.program_id(0)

    @pl.when(step == 0)
    def _():
        gain_out[...] = jnp.zeros_like(gain_out)
        acc_ref[...] = jnp.zeros_like(acc_ref)

    grad = a_ref[...].astype(wide) + b_ref[...].astype(wide)
    grad = grad + (c_ref[...].astype(wide) + d_ref[...].astype(wide))
    inv = inv_ref[...]
    scaled = middle_ref[...] * inv
    gain_out[...] += jnp.sum(grad * scaled, axis=0, keepdims=True)
    grad = grad * gain_ref[...]
    mean = jnp.sum(grad * scaled, axis=1, keepdims=True) * (1.0 / size)
    grad = cot_ref[...].astype(wide) + inv * (grad - scaled * mean)
    grad_ref[...] = grad
    grad_low = grad.astype(low)
    do_ref[...] = lax.dot_general(
        grad_low, weight_ref[...], NT, preferred_element_type=wide
    ).astype(low)
    acc_ref[:size] += lax.dot_general(attn_ref[...], grad_low, TN, preferred_element_type=wide)
    keep = lax.broadcasted_iota(jnp.int32, (give, 1), 0) < take

    def write(mine):
        for chip in range(chips):
            for core in range(cores):
                for group in range(groups):
                    low_edge = ((chip * cores + core) * groups + group) * take
                    value = jnp.where(keep, acc_ref[low_edge : low_edge + give], 0.0)
                    at = lax.rem(group + groups - where[2], groups)
                    target = send_ref if core ^ mine else keep_ref
                    target[chip ^ where[1], at] = value.astype(low)

    for mine in range(cores):
        here = (step == pl.num_programs(0) - 1) & (where[0] == mine)
        pl.when(here)(functools.partial(write, mine))


def feed_back(shape, take, where, operands):
    chips, cores, groups = shape
    rows, size = operands[8].shape
    give = padded(take, ROWS)
    block = min(256, rows)
    part = lambda n: pl.BlockSpec((block, n), lambda i, w: (i, 0))
    spec = lambda a: part(a.shape[1]) if a.shape[0] == rows else whole(a.shape)
    whole = lambda shape: pl.BlockSpec(shape, lambda i, w: (0,) * len(shape))
    pieces = pl.BlockSpec((chips, groups, give, size), lambda i, w: (0, 0, 0, 1))
    return pl.pallas_call(
        functools.partial(feed_back_kernel, shape, take, give),
        grid_spec=pltpu.PrefetchScalarGridSpec(
            num_scalar_prefetch=1,
            grid=(rows // block,),
            in_specs=[spec(a) for a in operands],
            out_specs=[part(size), part(size), whole((1, size)), pieces, pieces],
            scratch_shapes=[pltpu.VMEM((padded(size, 8) + give, size), wide)],
        ),
        out_shape=[
            jax.ShapeDtypeStruct((rows, size), wide),
            jax.ShapeDtypeStruct((rows, size), low),
            jax.ShapeDtypeStruct((1, size), wide),
        ]
        + [jax.ShapeDtypeStruct((chips, groups, give, 2 * size), low)] * 2,
        compiler_params=params(),
        cost_estimate=cost(1),
        name="feed_back",
    )(where, *operands)


def finish_kernel(
    shape, take, give, cuts, pieces, where, normed_ref, scaled_ref, inv_ref, gain_ref, query_ref,
    query_weight_ref, middle_ref, weight_ref, cos_ref, sin_ref, small_ref, *refs
):
    got_refs = refs[:pieces]
    keep_ref, send_ref, out_ref, acc_ref, row_ref, cut_ref = refs[pieces:]
    chips, cores, groups = shape
    size = normed_ref.shape[1]
    total = got_refs[0][...]
    for ref in got_refs[1:]:
        total = total + ref[...].astype(wide)
    keys, values = total[:, :LANES], total[:, LANES:]
    lane = lax.broadcasted_iota(jnp.int32, keys.shape, 1)
    swapped = jnp.where(
        lane % HD < HD // 2, pltpu.roll(keys, LANES - HD // 2, 1), pltpu.roll(keys, HD // 2, 1)
    )
    keys = keys * cos_ref[...] - swapped * sin_ref[...]
    grads = jnp.concatenate([keys, values], axis=1).astype(low)
    acc_ref[:size] = lax.dot_general(
        normed_ref[...], grads, TN, preferred_element_type=wide
    )
    grad = lax.dot_general(
        query_ref[...], query_weight_ref[...], NT, preferred_element_type=wide
    ) + lax.dot_general(grads, weight_ref[...], NT, preferred_element_type=wide)
    scaled = scaled_ref[...]
    row_ref[:, :size] = jnp.sum(grad * scaled, axis=0, keepdims=True)
    row_ref[:, size : size + small_ref.shape[1]] = small_ref[...]
    row_ref[:, size + small_ref.shape[1] :] = jnp.sum(grads.astype(wide), axis=0, keepdims=True)
    grad = grad * gain_ref[...]
    mean = jnp.sum(grad * scaled, axis=1, keepdims=True) * (1.0 / size)
    out_ref[...] = (middle_ref[...] + inv_ref[...] * (grad - scaled * mean)).astype(low)
    cut_ref[...] = jnp.zeros_like(cut_ref)
    for i in range(chips * cores * groups):
        at = 0
        for first, width in cuts:
            begin = first + i * width
            cut_ref[i : i + 1, at : at + width] = row_ref[:, begin : begin + width]
            at += width
    high = cut_ref[...].astype(low).astype(wide)
    rest = cut_ref[...] - high
    row = lax.broadcasted_iota(jnp.int32, (give, 1), 0)

    def write(mine):
        for chip in range(chips):
            for core in range(cores):
                for group in range(groups):
                    i = (chip * cores + core) * groups + group
                    value = jnp.where(row < take, acc_ref[i * take : i * take + give], 0.0)
                    value = jnp.where(row == take, high[i : i + 1], value)
                    value = jnp.where(row == take + 1, rest[i : i + 1], value)
                    at = lax.rem(group + groups - where[2], groups)
                    target = send_ref if core ^ mine else keep_ref
                    target[chip ^ where[1], at] = value.astype(low)

    for mine in range(cores):
        pl.when(where[0] == mine)(functools.partial(write, mine))


def finish_keyval(shape, take, give, cuts, where, got, operands):
    chips, cores, groups = shape
    rows, size = operands[0].shape
    width = got[0].shape[1]
    total = size + operands[10].shape[1] + width
    whole = lambda a: pl.BlockSpec(a.shape, lambda i, w: (0,) * a.ndim)
    pieces = pl.BlockSpec((chips, groups, give, width), lambda i, w: (0, 0, 0, 0))
    return pl.pallas_call(
        functools.partial(finish_kernel, shape, take, give, cuts, len(got)),
        grid_spec=pltpu.PrefetchScalarGridSpec(
            num_scalar_prefetch=1,
            grid=(1,),
            in_specs=[whole(a) for a in (*operands, *got)],
            out_specs=[pieces, pieces, pl.BlockSpec((rows, size), lambda i, w: (0, 0))],
            scratch_shapes=[
                pltpu.VMEM((padded(size, 8) + give, width), wide),
                pltpu.VMEM((1, total), wide),
                pltpu.VMEM((padded(chips * cores * groups, 8), width), wide),
            ],
        ),
        out_shape=[jax.ShapeDtypeStruct((chips, groups, give, width), low)] * 2
        + [jax.ShapeDtypeStruct((rows, size), low)],
        compiler_params=params(),
        cost_estimate=cost(20),
        name="finish_keyval",
    )(where, *operands, *got)


def place_rows(n_dp, n_group, take, give, device, own_ref, other_ref, at_ref, acc_ref):
    me, mine = device[3], device[2]
    for r in range(n_dp):
        source = own_ref if r % 2 == 0 else other_ref
        for s in range(n_group):
            row = (r // 2 * n_group + s) * give
            z = lax.rem(mine + s, n_group)
            at_ref[(me ^ r) * n_group + z] = source[row : row + give].astype(wide)
    for i in range(n_dp * n_group):
        acc_ref[i * take : i * take + give] = at_ref[i]


def keyval_kernel(
    piece, sizes, device, own_ref, other_ref, tokens_ref, cos_ref, sin_ref, o_ref, small_ref,
    second_ref, inv_ref, scaled_ref, normed_ref, keyval_ref, at_ref, acc_ref
):
    place_rows(*sizes, device, own_ref, other_ref, at_ref, acc_ref)
    count, take = sizes[0] * sizes[1], sizes[2]
    o_ref[...] = acc_ref[: o_ref.shape[0]].astype(low)
    for i in range(count):
        first = at_ref[i, take : take + 1]
        rest = at_ref[i, take + 1 : take + 2]
        cut = slice(i * piece, (i + 1) * piece)
        small_ref[:, cut] = first[:, :piece]
        second_ref[:, cut] = (
            first[:, piece : 2 * piece] + rest[:, :piece] + rest[:, piece : 2 * piece]
        )
    tokens = tokens_ref[...].astype(wide)
    size, width = tokens.shape[1], o_ref.shape[1]
    mean = jnp.sum(tokens * tokens, axis=1, keepdims=True) * (1.0 / size)
    inv = lax.rsqrt(mean + norm_eps)
    inv_ref[...] = inv
    scaled = tokens * inv
    scaled_ref[...] = scaled
    normed = (scaled * small_ref[:, :size]).astype(low)
    normed_ref[...] = normed
    pre = jnp.dot(normed, o_ref[...], preferred_element_type=wide)
    pre = pre + small_ref[:, small_ref.shape[1] - width :]
    keys = pre[:, :LANES]
    lane = lax.broadcasted_iota(jnp.int32, keys.shape, 1)
    swapped = jnp.where(
        lane % HD < HD // 2, pltpu.roll(keys, LANES - HD // 2, 1), pltpu.roll(keys, HD // 2, 1)
    )
    keyval_ref[:, :LANES] = (keys * cos_ref[...] + swapped * sin_ref[...]).astype(low)
    keyval_ref[:, LANES:] = pre[:, LANES:].astype(low)


def project_kernel(
    sizes, device, own_ref, other_ref, normed_ref, bias_ref, o_ref, pre_ref, at_ref, acc_ref
):
    place_rows(*sizes, device, own_ref, other_ref, at_ref, acc_ref)
    o_ref[...] = acc_ref[: o_ref.shape[0]].astype(low)
    pre_ref[...] = (
        jnp.dot(normed_ref[...], o_ref[...], preferred_element_type=wide) + bias_ref[0:1]
    )


def attend_kernel(
    sizes, device, own_ref, other_ref, attn_ref, tokens_ref, gain_ref, o_ref, low_ref, middle_ref,
    inv_ref, normed_ref, at_ref, acc_ref
):
    place_rows(*sizes, device, own_ref, other_ref, at_ref, acc_ref)
    o_ref[...] = acc_ref[: o_ref.shape[0]].astype(low)
    attn = attn_ref[...].astype(low)
    low_ref[...] = attn
    middle = tokens_ref[...].astype(wide) + jnp.dot(
        attn, o_ref[...], preferred_element_type=wide
    )
    middle_ref[...] = middle
    mean = jnp.sum(middle * middle, axis=1, keepdims=True) * (1.0 / middle.shape[1])
    inv = lax.rsqrt(mean + norm_eps)
    inv_ref[...] = inv
    normed_ref[...] = (middle * inv * gain_ref[...]).astype(low)


def assembled(kernel, name, device, own, other, take, operands, outputs, column=0, columns=1):
    n_dp, n_group = lax.axis_size("dp"), lax.axis_size("group")
    give = own.shape[0] // (n_dp // 2 * n_group)
    width = own.shape[1] // columns
    size = n_dp * n_group * take
    whole = lambda shape: pl.BlockSpec(shape, lambda i, m: (0,) * len(shape))
    outputs = [((size, width), low)] + outputs
    return pl.pallas_call(
        functools.partial(kernel, (n_dp, n_group, take, give)),
        grid_spec=pltpu.PrefetchScalarGridSpec(
            num_scalar_prefetch=1,
            grid=(1,),
            in_specs=[pl.BlockSpec((own.shape[0], width), lambda i, m: (0, column))] * 2
            + [whole(a.shape) for a in operands],
            out_specs=[whole(shape) for shape, _ in outputs],
            scratch_shapes=[
                pltpu.VMEM((n_dp * n_group, give, width), wide),
                pltpu.VMEM((size + give, width), wide),
            ],
        ),
        out_shape=[jax.ShapeDtypeStruct(*output) for output in outputs],
        compiler_params=params(),
        cost_estimate=cost(0.1),
        name=name,
    )(device, own, other, *operands)


def sum_kernel(*refs):
    total = refs[0][...].astype(wide)
    for ref in refs[1:-1]:
        total = total + ref[...].astype(wide)
    refs[-1][...] = total.astype(low)


def sum_pieces(pieces):
    rows, width = pieces[0].shape
    block = rows // 2
    spec = pl.BlockSpec((block, width), lambda i: (i, 0))
    return pl.pallas_call(
        sum_kernel,
        grid=(2,),
        in_specs=[spec] * len(pieces),
        out_specs=spec,
        out_shape=jax.ShapeDtypeStruct((rows, width), low),
        compiler_params=params(),
        cost_estimate=cost(0.1),
        name="sum_pieces",
    )(*pieces)


def return_kernel(near_ref, far_ref, *refs):
    x_a, x_b, y_a, y_b, x_out, y_out = refs
    top = pl.program_id(0) == 0
    near, far = near_ref[...].astype(wide), far_ref[...].astype(wide)
    x_sum = x_a[...].astype(wide) + x_b[...].astype(wide)
    y_sum = y_a[...].astype(wide) + y_b[...].astype(wide)
    x_out[...] = jnp.where(top, x_sum, x_sum + far).astype(low)
    y_out[...] = jnp.where(top, y_sum + near, y_sum).astype(low)


def return_sums(across, x_parts, y_parts):
    half, width = across[0].shape
    spec = pl.BlockSpec((half, width), lambda i: (i, 0))
    one = pl.BlockSpec((half, width), lambda i: (0, 0))
    return pl.pallas_call(
        return_kernel,
        grid=(2,),
        in_specs=[one, one] + [spec] * 4,
        out_specs=[spec] * 2,
        out_shape=[jax.ShapeDtypeStruct((2 * half, width), low)] * 2,
        compiler_params=params(),
        cost_estimate=cost(0.1),
        name="return_sums",
    )(*across, *x_parts, *y_parts)


def pack_kernel(keyval_ref, query_ref, output_ref, small_ref, second_ref, o_ref, buffer_ref):
    rows = query_ref.shape[0]
    piece = small_ref.shape[1]
    buffer_ref[...] = jnp.zeros_like(buffer_ref)
    at = 0
    for ref in (keyval_ref, query_ref, output_ref):
        buffer_ref[:rows, at : at + ref.shape[1]] = ref[...]
        at += ref.shape[1]
    second = second_ref[...]
    first = second.astype(low).astype(wide)
    rest = second - first
    middle = rest.astype(low).astype(wide)
    buffer_ref[rows : rows + 1, :piece] = small_ref[...]
    buffer_ref[rows : rows + 1, piece : 2 * piece] = first
    buffer_ref[rows + 1 : rows + 2, :piece] = middle
    buffer_ref[rows + 1 : rows + 2, piece : 2 * piece] = rest - middle
    o_ref[...] = buffer_ref[...].astype(low)


def pack_rows(keyval, query, output, small, second, give):
    arrays = (keyval, query, output, small[None], second[None])
    width = sum(a.shape[1] for a in arrays[:3])
    return pl.pallas_call(
        pack_kernel,
        grid=(1,),
        in_specs=[pl.BlockSpec(a.shape, lambda i: (0, 0)) for a in arrays],
        out_specs=pl.BlockSpec((give, width), lambda i: (0, 0)),
        out_shape=jax.ShapeDtypeStruct((give, width), low),
        scratch_shapes=[pltpu.VMEM((give, width), wide)],
        compiler_params=params(),
        cost_estimate=cost(0.5),
        name="pack_rows",
    )(*arrays)


def fill_kernel(x_ref, o_ref):
    rows = x_ref.shape[0]
    o_ref[:rows] = x_ref[...]
    o_ref[rows:] = jnp.zeros_like(o_ref[rows:])


def fill_rows(block, rows):
    return pl.pallas_call(
        fill_kernel,
        grid=(1,),
        in_specs=[pl.BlockSpec(block.shape, lambda i: (0, 0))],
        out_specs=pl.BlockSpec((rows, block.shape[1]), lambda i: (0, 0)),
        out_shape=jax.ShapeDtypeStruct((rows, block.shape[1]), block.dtype),
        compiler_params=params(),
        cost_estimate=cost(0.1),
        name="fill_rows",
    )(block)


def widen_kernel(x_ref, o_ref):
    o_ref[...] = jnp.broadcast_to(x_ref[...], o_ref.shape)


def widen(row, rows):
    return pl.pallas_call(
        widen_kernel,
        out_shape=jax.ShapeDtypeStruct((rows, row.shape[1]), row.dtype),
        compiler_params=pltpu.CompilerParams(vmem_limit_bytes=MIB),
        cost_estimate=cost(20),
        name="widen",
    )(row)


def stack_kernel(outer, count, take, give, meta, *refs):
    o_ref, at_ref, acc_ref = refs[count:]
    for s in range(count):
        z = lax.rem(meta[2] + s, count)
        for i in range(outer):
            at_ref[i * count + z] = refs[s][i * give : (i + 1) * give].astype(wide)
    for i in range(outer * count):
        acc_ref[i * take : i * take + give] = at_ref[i]
    size = outer * count * take
    o_ref[:size] = acc_ref[:size].astype(low)
    if o_ref.shape[0] > size:
        o_ref[size:] = jnp.zeros_like(o_ref[size:])


def stack_rows(pieces, outer, take, me, rows):
    count, width = len(pieces), pieces[0].shape[1]
    give = pieces[0].shape[0] // outer
    whole = lambda r: pl.BlockSpec((r, width), lambda i, m: (0, 0))
    return pl.pallas_call(
        functools.partial(stack_kernel, outer, count, take, give),
        grid_spec=pltpu.PrefetchScalarGridSpec(
            num_scalar_prefetch=1,
            grid=(1,),
            in_specs=[whole(outer * give)] * count,
            out_specs=whole(rows),
            scratch_shapes=[
                pltpu.VMEM((outer * count, give, width), wide),
                pltpu.VMEM((padded(outer * count * take, 8) + give, width), wide),
            ],
        ),
        out_shape=jax.ShapeDtypeStruct((rows, width), low),
        compiler_params=params(),
        cost_estimate=cost(1),
        name="stack_rows",
    )(me, *pieces)


def cut_kernel(count, part, part_wide, w_ref, o_ref, buffer_ref):
    rows = w_ref.shape[0]
    buffer_ref[...] = jnp.zeros_like(buffer_ref)
    for p in range(count):
        for j in range(2):
            column = (j * count + p) * part
            buffer_ref[:rows, j * part_wide : j * part_wide + part] = w_ref[
                :, column : column + part
            ]
        o_ref[p] = buffer_ref[...].astype(low)


def cut_columns(weight, count, part_wide, give):
    rows, width = weight.shape
    part = width // (2 * count)
    shape = (count, give, 2 * part_wide)
    return pl.pallas_call(
        functools.partial(cut_kernel, count, part, part_wide),
        grid=(1,),
        in_specs=[pl.BlockSpec(weight.shape, lambda i: (0, 0))],
        out_specs=pl.BlockSpec(shape, lambda i: (0, 0, 0)),
        out_shape=jax.ShapeDtypeStruct(shape, low),
        scratch_shapes=[pltpu.VMEM((give, 2 * part_wide), wide)],
        compiler_params=params(),
        cost_estimate=cost(1),
        name="cut_columns",
    )(weight)


def update_kernel(count, part, part_wide, g_ref, m_ref, v_ref, w_ref, go_ref, vo_ref, wo_ref):
    rows = w_ref.shape[0]
    for p in range(count):
        piece = g_ref[p].astype(wide)
        for j in range(2):
            column = (j * count + p) * part
            go_ref[:, column : column + part] = piece[
                :rows, j * part_wide : j * part_wide + part
            ]
    vo_ref[...], wo_ref[...] = adamw_step(
        go_ref[...], m_ref[...], v_ref[...], w_ref[...], rate_proj, decay_rate
    )


def update_columns(pieces, first, second, weight):
    count, _, width = pieces.shape
    spec = pl.BlockSpec(weight.shape, lambda i: (0, 0))
    return pl.pallas_call(
        functools.partial(
            update_kernel, count, weight.shape[1] // (2 * count), width // 2
        ),
        grid=(1,),
        in_specs=[pl.BlockSpec(pieces.shape, lambda i: (0, 0, 0))] + [spec] * 3,
        out_specs=[spec] * 3,
        out_shape=[jax.ShapeDtypeStruct(weight.shape, wide)] * 3,
        compiler_params=params(),
        cost_estimate=cost(1),
        name="update_columns",
    )(pieces, first, second, weight)


def flip(value, mask):
    count = lax.axis_size("dp")
    return lax.ppermute(value, "dp", [(i, i ^ mask) for i in range(count)])


def shift(value, step):
    count = lax.axis_size("group")
    return lax.ppermute(value, "group", [((i + step) % count, i) for i in range(count)])


def shift_within(value, step):
    count = lax.axis_size("group")
    pairs = [(i + step, i) for i in range(count) if 0 <= i + step < count]
    return lax.ppermute(value, "group", pairs)


def after(value, *others):
    return lax.optimization_barrier((value, *others))[0]


def group_pieces(block, steps=None):
    return [block] + [shift(block, s) for s in range(1, lax.axis_size("group"))]


def group_send(blocks):
    count = lax.axis_size("group")
    return [blocks[0]] + [shift(blocks[count - s].astype(low), s) for s in range(1, count)]


def add_up(terms):
    return functools.reduce(jnp.add, [term.astype(wide) for term in terms])


def gather_chips(column, forward=None):
    n_dp = lax.axis_size("dp")
    if forward is not None and n_dp == 8:
        half = column.shape[0] // 2
        x_side, y_side = flip(column, 2), flip(column, 4)
        x_side, y_side = after((x_side, y_side), forward)
        across = [flip(x_side[:half], 4), flip(y_side[half:], 2)]
        return jnp.concatenate([column, x_side, y_side, *across], axis=0)
    evens = [column] + [flip(column, r) for r in range(2, n_dp, 2)]
    return jnp.concatenate(evens, axis=0)


def scatter_pair(keep, send):
    return keep.astype(wide) + flip(send, 1).astype(wide)


def scatter_chips(pair):
    got = [flip(pair[r].astype(low), 2 * r) for r in range(1, pair.shape[0])]
    return add_up([pair[0]] + got)


def body(
    tokens,
    positions,
    cotangent,
    query_weight,
    query_first,
    query_second,
    keyval_weight,
    keyval_first,
    keyval_second,
    output_weight,
    output_first,
    output_second,
    gateup_weight,
    gateup_first,
    gateup_second,
    down_weight,
    down_first,
    down_second,
    small_weight,
    small_first,
    small_second,
):
    row_count = tokens.shape[0]
    half = row_count // 2
    n_dp = lax.axis_size("dp")
    group_size = lax.axis_size("group")
    device_count = n_dp * group_size
    my_dp = lax.axis_index("dp")
    my_index = lax.axis_index("group")
    flat_index = my_dp * group_size + my_index
    seq_len = row_count * group_size
    query_width = HQ * HD
    kv_width = HK * HD
    small_size = 2 * D + query_width + 2 * kv_width
    rest_length = small_size - kv_width
    rest_piece = rest_length // device_count
    value_piece = kv_width // device_count
    small_piece = small_size // device_count
    part = FF // n_dp
    part_wide = padded(part, LANES)
    in_rows = query_weight.shape[0]
    device = jnp.stack([my_dp & 1, my_dp >> 1, my_index, my_dp]).astype(jnp.int32)
    in_give = padded(in_rows + 2, ROWS)
    down_rows = down_weight.shape[0]

    every_block = pack_rows(
        keyval_weight, query_weight, output_weight, small_weight, small_second, in_give
    )
    place_row = positions[0]
    local_index = my_index * row_count + jnp.arange(row_count, dtype=jnp.int32)
    local_places = lax.dynamic_slice_in_dim(place_row, my_index * row_count, row_count, 0)
    starts = (local_index - local_places).reshape(2, half).astype(jnp.int32)
    starts = jnp.broadcast_to(starts[:, None, :], (2, 8, half))
    angles = rotary_angles(local_places)
    cosine, sine_table = jnp.cos(angles), jnp.sin(angles)
    cos_wide = jnp.concatenate([cosine] * 4, axis=1)
    sin_wide = jnp.concatenate([-sine_table, sine_table] * 2, axis=1)

    gateup_pieces = cut_columns(gateup_weight, n_dp, part_wide, in_give)
    every_pieces = group_pieces(every_block)
    every_pieces, cos_wide, sin_wide = after((every_pieces, cos_wide, sin_wide), gateup_pieces)
    every_column = jnp.concatenate(every_pieces, axis=0)
    keyval_column = every_column[:, : 2 * kv_width]
    both_column = every_column[:, 2 * kv_width :]
    keyval_own = gather_chips(keyval_column)
    down_part = lax.all_gather(down_weight.astype(low), "group", axis=0, tiled=True)

    keyval_full, small_row, second_row, inv_one, scaled_one, normed_one, keyval_low = assembled(
        functools.partial(keyval_kernel, small_piece), "project_keyval", device,
        keyval_own, flip(keyval_own, 1), in_rows, (tokens, cos_wide, sin_wide),
        [
            ((1, small_size), wide),
            ((1, small_size), wide),
            ((row_count, 1), wide),
            ((row_count, D), wide),
            ((row_count, D), low),
            ((row_count, 2 * kv_width), low),
        ],
    )
    gain_one, gain_two = small_row[:, :D], small_row[:, D : 2 * D]
    bias_query = small_row[:, 2 * D : 2 * D + query_width]
    keyval_parts = [keyval_low] + [shift_within(keyval_low, -s) for s in range(1, group_size)]
    both_own = gather_chips(after(both_column, keyval_low), down_part)
    gateup_column = lax.all_to_all(after(gateup_pieces, keyval_low), "dp", 0, 0, tiled=True)
    gateup_column = gateup_column.reshape(n_dp * in_give, 2 * part_wide)
    down_part = fill_rows(down_part, part_wide)
    keyval_parts, down_part, bias_query = after((keyval_parts, down_part, bias_query))
    bias_query = widen(bias_query, 8)
    both_own, gateup_column, bias_query = after((both_own, gateup_column, bias_query))
    cot_all = lax.all_gather(after(cotangent, both_own), "dp", axis=0, tiled=True)
    both_other = flip(both_own, 1)
    query_full, query_pre = assembled(
        project_kernel, "project_query", device, both_own, both_other, in_rows,
        (normed_one, bias_query), [((row_count, query_width), wide)], 0, 2,
    )
    gateup_pieces = group_pieces(gateup_column)
    attn_float, log_total, query_low = attention_forward(
        query_pre, cos_wide, sin_wide, starts, keyval_parts, device
    )
    output_full, attn_low, middle, inv_two, normed_two = assembled(
        attend_kernel, "attention_output", device, both_own, both_other, in_rows,
        (attn_float, tokens, gain_two),
        [
            ((row_count, query_width), low),
            ((row_count, D), wide),
            ((row_count, 1), wide),
            ((row_count, D), low),
        ],
        1, 2,
    )

    normed_two, gateup_pieces = after((normed_two, gateup_pieces))
    gateup_part = stack_rows(gateup_pieces, n_dp, in_rows, device, D)
    chips = n_dp // 2
    pieces, down_shape = (chips, 2, group_size), (1, 1, group_size)
    kept, sides, back = None, {0: normed_two}, {}
    for k in range(1, chips):
        if n_dp != 8 or k != 3:
            sides[k] = flip(normed_two, 2 * k)

    def visit(k, kept):
        back_a, back_b, *kept = feed_forward(
            sides[k], flip(sides[k], 1), cot_all, gateup_part, down_part, device, kept, k
        )
        back[k] = (back_a, flip(back_b, 1))
        return kept

    if n_dp == 8:
        kept = visit(0, kept)
        sides[1], sides[2] = after((sides[1], sides[2]), kept)
        across = [flip(sides[1][:half], 4), flip(sides[2][half:], 2)]
        kept = visit(1, kept)
        sides[3] = jnp.concatenate(after(across, kept), axis=0)
        kept = visit(3, kept)
        corner = add_up(back[3]).astype(low)
        across = [flip(corner[:half], 2), flip(corner[half:], 4)]
        kept = visit(2, kept)
        down_term = weight_gradient(kept[1], cot_all, down_shape, down_rows, device)
        across = after(across, down_term)
        x_sum, y_sum = return_sums(across, back[1], back[2])
        kept, y_sum = after((kept, y_sum))
        returned = [*back[0], flip(x_sum, 2), flip(y_sum, 4)]
    else:
        for k in range(chips):
            kept = visit(k, kept)
        down_term = weight_gradient(kept[1], cot_all, down_shape, down_rows, device)
        returned = list(back[0])
        returned += [flip(add_up(back[k]).astype(low), 2 * k) for k in range(1, chips)]
    out_all, _, gate_all, normed_all = kept
    down_got = group_send(down_term)
    gateup_term = weight_gradient(normed_all, gate_all, pieces, in_rows, device)
    gateup_got = group_send(gateup_term)
    returned, gateup_got[0], early = after((returned, gateup_got[0], down_got[1:-1]))
    down_got[1:-1] = early
    out_sum = lax.psum_scatter(after(out_all, returned), "dp", scatter_dimension=0, tiled=True)

    if len(returned) > 4:
        returned = returned[:3] + [add_up(returned[3:])]
    grad_middle, grad_attn_low, gain_two_term, *both_terms = feed_back(
        pieces,
        in_rows,
        device,
        (
            *returned,
            middle,
            inv_two,
            gain_two,
            cotangent,
            attn_low,
            output_full,
        ),
    )
    grad_query_pre, *keyval_terms = attention_backward(
        query_low,
        grad_attn_low,
        attn_float,
        log_total,
        starts,
        cosine.T,
        sine_table.T,
        keyval_parts,
        device,
    )
    both_terms = weight_gradient(
        normed_one, grad_query_pre, pieces, in_rows, device, split=True, columns=2, into=both_terms
    )
    keyval_terms, both_terms, gateup_got, down_got = after(
        (keyval_terms, both_terms, gateup_got, down_got)
    )
    keyval_got = [keyval_terms[0]]
    keyval_got += [shift_within(keyval_terms[s], s) for s in range(1, group_size)]
    both_pair = scatter_pair(both_terms[0], after(both_terms[1], out_sum))
    both_total = scatter_chips(both_pair)
    gateup_sum = sum_pieces(gateup_got).reshape(n_dp, -1, 2 * part_wide)
    gateup_sum = lax.all_to_all(gateup_sum, "dp", 0, 0, tiled=True)
    keyval_got, gateup_sum = after((keyval_got, gateup_sum), both_pair)
    bias_term = jnp.sum(grad_query_pre.astype(wide), axis=0)
    *last_terms, tokens_grad = finish_keyval(
        pieces,
        in_rows,
        in_give,
        ((0, small_piece), (0, rest_piece), (rest_length, value_piece)),
        device,
        keyval_got,
        (
            normed_one,
            scaled_one,
            inv_one,
            gain_one,
            grad_query_pre,
            query_full,
            grad_middle,
            keyval_full,
            cos_wide,
            sin_wide,
            jnp.concatenate([gain_two_term, bias_term[None]], axis=1),
        ),
    )
    small_width = small_piece + rest_piece + value_piece
    gateup_grad, gateup_second_out, gateup_weight_out = update_columns(
        after(gateup_sum, last_terms), gateup_first, gateup_second, gateup_weight
    )
    last_terms, gateup_second_out = after((last_terms, gateup_second_out), both_total)
    last_total = scatter_chips(scatter_pair(*last_terms))
    down_got = after(down_got, last_total)
    late_middle, out_sum = after((middle, out_sum), last_total)
    layer_out = (late_middle + out_sum.astype(wide)).astype(low)
    down_grad = add_up(down_got)[:down_rows]
    some = last_total.shape[1] - both_total.shape[1]
    both_total = jnp.pad(both_total, ((0, 0), (0, some), (0, 0)))
    down_second_out, down_weight_out = adamw_step(
        down_grad, down_first, down_second, down_weight, rate_proj, decay_rate
    )
    every_got = group_send(jnp.concatenate([both_total, last_total], axis=2))
    every_got, down_second_out, layer_out = after((every_got, down_second_out, layer_out))
    every_sum = add_up(every_got)
    query_grad = every_sum[:in_rows, :query_width]
    output_grad = every_sum[:in_rows, query_width : query_width + D]
    last_sum = every_sum[:, query_width + D :]
    keyval_grad = last_sum[:in_rows]
    small_sum = last_sum[in_rows, :small_width] + last_sum[in_rows + 1, :small_width]
    small_grad = small_sum[:small_piece]
    rest_grad = small_sum[small_piece : small_piece + rest_piece]
    value_grad = small_sum[small_piece + rest_piece :]

    query_second_out, query_weight_out = adamw_step(
        query_grad, query_first, query_second, query_weight, rate_proj, decay_rate
    )
    keyval_second_out, keyval_weight_out = adamw_step(
        keyval_grad, keyval_first, keyval_second, keyval_weight, rate_proj, decay_rate
    )
    output_second_out, output_weight_out = adamw_step(
        output_grad, output_first, output_second, output_weight, rate_out, decay_rate
    )
    _, small_weight_out = adamw_step(
        small_grad, small_first, small_second, small_weight, rate_small, 0.0
    )
    rest_second = lax.dynamic_slice_in_dim(
        second_row[0], flat_index * rest_piece, rest_piece, 0
    )
    value_second = lax.dynamic_slice_in_dim(
        second_row[0], rest_length + flat_index * value_piece, value_piece, 0
    )
    small_second_out = beta_two * rest_second + (1.0 - beta_two) * rest_grad * rest_grad
    value_bias_second_out = beta_two * value_second + (1.0 - beta_two) * value_grad * value_grad
    return (
        layer_out,
        tokens_grad,
        query_grad,
        query_second_out,
        query_weight_out,
        keyval_grad,
        keyval_second_out,
        keyval_weight_out,
        output_grad,
        output_second_out,
        output_weight_out,
        gateup_grad,
        gateup_second_out,
        gateup_weight_out,
        down_grad,
        down_second_out,
        down_weight_out,
        small_grad,
        small_second_out,
        value_bias_second_out,
        small_weight_out,
    )


def solution(mesh):
    rows = P(("dp", "group"), None)
    line = P(("dp", "group"))
    in_specs = (rows, P("dp", None)) + (rows,) * 16 + (line,) * 3
    out_specs = (rows,) * 17 + (line,) * 4
    return jax.shard_map(body, mesh=mesh, in_specs=in_specs, out_specs=out_specs, check_vma=False)
```
